32 devices in a mesh: dp: 8 (over z, x), fsdp: 4 (over y, core).
Axes of the slice: x: 2, y: 2, z: 4, core: 2. Of those that a mesh axis runs over, the one named last changes fastest.
Arguments:
- frames: bfloat16 [8, 4, 48, 64, 128], P('dp', 'fsdp'), may hold values from -6 to 6
- occupied_slot_counts: int32 [4, 8], P('fsdp', 'dp'), may hold values from 1 to 48, 128 in all within a row
- block_frame_rows: int32 [8, 4, 48], P('dp', 'fsdp'), may hold values from 1 to 16
- order: int32 [4, 8], P('fsdp'), may hold values from 0 to 7, each once within a row
- cotangent: bfloat16 [8, 4, 16, 16, 1536], P('dp', 'fsdp'), may hold values from -6 to 6
- sub_weight: bfloat16 [512, 1536], P('fsdp'), may hold values from -0.25 to 0.25
- depth_kernel: float32 [31, 1536], replicated, may hold values from -1 to 1
- norm_gain: float32 [1536], replicated, may hold values from 0.5 to 1.5
- w_in: bfloat16 [1536, 3072], P('fsdp'), may hold values from -0.15625 to 0.15625
- w_out: bfloat16 [3072, 1536], P('fsdp'), may hold values from -0.109375 to 0.109375
Outputs:
- grad_in: bfloat16 [8, 1536, 3072], P('dp', 'fsdp')
- grad_out: bfloat16 [8, 3072, 1536], P('dp', 'fsdp')
- kernel_grad: float32 [31, 1536], replicated
The draws below stay inside these ranges and needn't reach their ends.
Inputs may be any that keep to these rules, and one draw needn't show every extreme that they name: `occupied_slot_counts`: for each fsdp index the 8 counts sum to 128, and the largest is 48.
All inputs are finite; a program needn't handle non-finite values. No bound on the sum of `occupied_slot_counts` on one device may be relied on, other than what follows from the above.
Results may differ from the reference program's by a relative error of at most 0.02.
Values may be sent and summed in bfloat16 or wider, within the bound.
No kernel may reach another device: no remote copies, remote signals or barrier semaphores. Data moves between devices by JAX's collectives and lax.ppermute only.
A program may use at most 128 MiB of HBM per device.

```python
import math
import jax
import jax.numpy as jnp
import numpy as np
from jax import lax

D = 1536
FF = 3072
MEL = 128
K = 31
BR = 16
BIN = 64
NB = 16
NH = 48
N_DP = 8
N_FSDP = 4


def with_ends(drawn, own_key, smallest, largest):
    longest = drawn.shape.index(max(drawn.shape))
    spots = []
    for shift in (0, 1):
        where = [jax.random.randint(jax.random.fold_in(own_key, axis), (), 0, length) for axis, length in enumerate(drawn.shape)]
        where[longest] = (where[longest] + shift) % drawn.shape[longest]
        spots.append(tuple(where))
    return drawn.at[spots[0]].set(smallest).at[spots[1]].set(largest)


def block_scale(stream_key, shape, cuts, smallest, largest):
    factor_of = 1.0
    for dim, blocks in cuts:
        heights = jax.random.uniform(jax.random.fold_in(jax.random.fold_in(stream_key, 6), dim), (blocks,), jnp.float32, smallest / len(cuts), largest / len(cuts))
        factor_of = factor_of * jnp.repeat(jnp.exp(heights), shape[dim] // blocks).reshape((-1,) + (1,) * (len(shape) - 1 - dim))
    return factor_of


def split_up(count, total, bound, lean):
    weights = [(1 << 20) // math.isqrt(rank ** lean) + 1 for rank in range(2, count + 1)]
    surplus, given = total - bound - (count - 1), [1] * (count - 1)
    while surplus > 0:
        free = [i for i in range(count - 1) if given[i] < bound]
        mass, remaining = sum([weights[i] for i in free]), surplus
        for i in free:
            addition = min(bound - given[i], max(1, remaining * weights[i] // mass), surplus)
            given[i] = given[i] + addition
            surplus = surplus - addition
    return np.array([bound] + given)


def ragged(rng, amount, total, limit, lean):
    if amount == 2:
        one = jax.random.randint(rng, (), max(1, total - limit), min(limit, total - 1) + 1)
        return jnp.stack([one, total - one])
    sizes = jnp.asarray(split_up(amount, total, limit, lean), jnp.int32)
    pairs = (amount - 1) // 2
    giver, taker = sizes[1:1 + 2 * pairs:2], sizes[2:2 + 2 * pairs:2]
    margin = jnp.minimum(giver - 1, limit - taker)
    shifted = jax.random.randint(jax.random.fold_in(rng, 1), (pairs,), 0, 1 << 20) % (margin + 1)
    sizes = sizes.at[1:1 + 2 * pairs:2].set(giver - shifted).at[2:2 + 2 * pairs:2].set(taker + shifted)
    return sizes[jax.random.permutation(jax.random.fold_in(rng, 2), amount)]


def scatter_about(rng, dims, scale, limit, pieces=(), held_as=jnp.bfloat16):
    factor_of = block_scale(rng, dims, pieces, -0.22, 0.18) if pieces else 1.0
    drawn = jax.random.normal(rng, dims, jnp.float32) * scale * factor_of
    return jnp.minimum(jnp.maximum(drawn, -limit), limit).astype(held_as)


def setup_inputs(seed: int = 0) -> dict:
    splits = jax.random.split(jax.random.key(seed), 11)
    return {
        "frames": scatter_about(splits[0], (N_DP, N_FSDP, NH, BIN, MEL), 1.0, 6.0, ((0, 8), (1, 4))),
        "occupied_slot_counts": jax.vmap(lambda own: ragged(own, N_DP, N_DP * NB, NH, 2))(jax.random.split(splits[1], N_FSDP)).reshape((N_FSDP, N_DP)).astype(jnp.int32),
        "block_frame_rows": with_ends(jax.random.randint(splits[2], (N_DP, N_FSDP, NH), 1, BR + 1), jax.random.fold_in(splits[2], 1), 1, BR).astype(jnp.int32),
        "order": jax.vmap(lambda own: jax.random.permutation(own, N_DP))(jax.random.split(splits[3], N_FSDP)).reshape((N_FSDP, N_DP)).astype(jnp.int32),
        "cotangent": scatter_about(splits[4], (N_DP, N_FSDP, NB, BR, D), 1.0, 6.0, ((0, 8), (1, 4))),
        "sub_weight": scatter_about(splits[5], (4 * MEL, D), (4 * MEL) ** -0.5, 0.25, ((0, 4),)),
        "depth_kernel": scatter_about(splits[6], (K, D), K ** -0.5, 1.0, (), jnp.float32),
        "norm_gain": jnp.clip(1.0 + 0.1 * jax.random.normal(splits[7], (D,), jnp.float32), 0.5, 1.5),
        "w_in": scatter_about(splits[8], (D, FF), D ** -0.5, 0.15625, ((0, 4),)),
        "w_out": scatter_about(splits[9], (FF, D), FF ** -0.5, 0.109375, ((0, 4),)),
    }


EPSILON = 1e-05

def swish_slope(values):
    sigma = jax.nn.sigmoid(values)
    return sigma * (1.0 + values * (1.0 - sigma))

def layer_norm(mixed, norm_gain):
    mean_value = lax.optimization_barrier(jnp.mean(mixed, axis=-1, keepdims=True))
    centred = mixed - mean_value
    variance = lax.optimization_barrier(jnp.mean(centred * centred, axis=-1, keepdims=True))
    return centred * lax.rsqrt(variance + EPSILON) * norm_gain

def padded_blocks(features, tap_count):
    half_span = (tap_count - 1) // 2
    return jnp.pad(features, ((0, 0), (half_span, half_span), (0, 0)))

def depthwise(features, depth_kernel):
    tap_count = depth_kernel.shape[0]
    steps_len = features.shape[1]
    padded = padded_blocks(features, tap_count)
    running = jnp.zeros(features.shape, features.dtype)
    for tap_index in range(tap_count):
        running = running + padded[:, tap_index:tap_index + steps_len, :] * depth_kernel[tap_index]
    return running

def kernel_terms(conv_grad, features, tap_count):
    steps_len = features.shape[1]
    padded = padded_blocks(features, tap_count)
    columns = [lax.optimization_barrier(jnp.sum(conv_grad * padded[:, tap_index:tap_index + steps_len, :], axis=(0, 1))) for tap_index in range(tap_count)]
    return jnp.stack(columns)

def contract(left, right, left_dim, right_dim):
    return lax.dot_general(left, right, (((left_dim,), (right_dim,)), ((), ())), preferred_element_type=jnp.float32)

def balanced_blocks(frames, occupied_slot_counts, block_frame_rows, order, data_parallel_index, sharded_parallel_index):
    counts = occupied_slot_counts[sharded_parallel_index]
    ends = jnp.cumsum(counts, dtype=jnp.int32)
    starts = ends - counts
    slot_index = jnp.arange(N_DP, dtype=jnp.int32)
    first = jnp.sum(jnp.where(order[sharded_parallel_index] == data_parallel_index, slot_index, 0), dtype=jnp.int32)
    global_index = first + jnp.arange(NB, dtype=jnp.int32) * N_DP
    source = lax.optimization_barrier(jnp.sum((ends[None, :] <= global_index[:, None]).astype(jnp.int32), axis=1, dtype=jnp.int32))
    within = global_index - starts[source]
    return (frames[source, sharded_parallel_index, within], block_frame_rows[source, sharded_parallel_index, within])

def device_step(frame_blocks, valid_row_counts, cot_blocks, sub_weight, depth_kernel, norm_gain, w_in, w_out):
    block_total = frame_blocks.shape[0]
    row_total = block_total * BR
    row_mask = (jnp.arange(BR, dtype=jnp.int32)[None, :] < valid_row_counts[:, None]).astype(jnp.float32).reshape(row_total, 1)
    patches = frame_blocks.reshape(row_total, 4 * MEL)
    features = (jnp.dot(patches, sub_weight, preferred_element_type=jnp.float32) * row_mask).astype(jnp.bfloat16)
    feature_blocks = lax.optimization_barrier(features).astype(jnp.float32).reshape(block_total, BR, D)
    block_mask = row_mask.reshape(block_total, BR, 1)
    conv_out = depthwise(feature_blocks, depth_kernel)
    mixed = feature_blocks + block_mask * conv_out * jax.nn.sigmoid(conv_out)
    mixed_rows = mixed.reshape(row_total, D)
    normed = layer_norm(mixed_rows, norm_gain).astype(jnp.bfloat16)
    pre_act = jnp.dot(normed, w_in, preferred_element_type=jnp.float32)
    hidden = (pre_act * jax.nn.sigmoid(pre_act)).astype(jnp.bfloat16)
    masked_cot = jnp.where(row_mask > 0, cot_blocks.reshape(row_total, D), jnp.zeros((), cot_blocks.dtype))
    hidden_grad = 0.5 * contract(masked_cot, w_out, 1, 1)
    pre_grad = (hidden_grad * swish_slope(pre_act)).astype(jnp.bfloat16)
    term_in = contract(normed, pre_grad, 0, 0)
    term_out = 0.5 * contract(hidden, masked_cot, 0, 0)
    normed_grad = contract(pre_grad, w_in, 1, 1)
    norm_pullback = jax.vjp(lambda values: layer_norm(values, norm_gain), mixed_rows)[1]
    mixed_grad = masked_cot.astype(jnp.float32) + norm_pullback(normed_grad)[0]
    conv_grad = block_mask * mixed_grad.reshape(block_total, BR, D) * swish_slope(conv_out)
    kernel_part = kernel_terms(conv_grad, feature_blocks, depth_kernel.shape[0])
    return (term_in, term_out, kernel_part)

def reference(frames, occupied_slot_counts, block_frame_rows, order, cotangent, sub_weight, depth_kernel, norm_gain, w_in, w_out):

    def one_group(data_parallel_index):
        grad_in_total = jnp.zeros((D, FF), jnp.float32)
        grad_out_total = jnp.zeros((FF, D), jnp.float32)
        kernel_total = jnp.zeros(depth_kernel.shape, jnp.float32)
        group_cot = lax.dynamic_index_in_dim(cotangent, data_parallel_index, 0, keepdims=False)
        for sharded_parallel_index in range(N_FSDP):
            frame_blocks, valid_row_counts = balanced_blocks(frames, occupied_slot_counts, block_frame_rows, order, data_parallel_index, sharded_parallel_index)
            term_in, term_out, kernel_part = device_step(frame_blocks, valid_row_counts, group_cot[sharded_parallel_index], sub_weight, depth_kernel, norm_gain, w_in, w_out)
            grad_in_total = grad_in_total + lax.optimization_barrier(term_in.astype(jnp.bfloat16)).astype(jnp.float32)
            grad_out_total = grad_out_total + lax.optimization_barrier(term_out.astype(jnp.bfloat16)).astype(jnp.float32)
            kernel_total = kernel_total + kernel_part
        return (grad_in_total.astype(jnp.bfloat16), grad_out_total.astype(jnp.bfloat16), kernel_total)
    grad_in, grad_out, kernel_parts = lax.map(one_group, jnp.arange(N_DP, dtype=jnp.int32))
    kernel_grad = lax.optimization_barrier(jnp.sum(kernel_parts, axis=0)) / (NB * BR)
    return (grad_in, grad_out, kernel_grad)
```

```python
import functools

import jax
import jax.numpy as jnp
from jax import lax
from jax.experimental import pallas as pl
from jax.experimental.pallas import tpu as pltpu
from jax.sharding import PartitionSpec as P

LANES = 128
HALF = 8
TILE = 16
EPSILON = 1e-05

VMEM = pl.BlockSpec(memory_space=pltpu.VMEM)
SMEM = pl.BlockSpec(memory_space=pltpu.SMEM)
ANY = pl.BlockSpec(memory_space=pl.ANY)
CHEAP = pl.CostEstimate(flops=0, transcendentals=0, bytes_accessed=0)


def params():
    return pltpu.CompilerParams(vmem_limit_bytes=56 * 1024 * 1024)


def sds(shape, dtype):
    return jax.ShapeDtypeStruct(shape, dtype)


def sigmoid(values):
    return 0.5 * jnp.tanh(0.5 * values) + 0.5


def dot(left, right, left_dim, right_dim):
    return lax.dot_general(
        left, right, (((left_dim,), (right_dim,)), ((), ())), preferred_element_type=jnp.float32
    )


def across(value, k):
    n = lax.axis_size("fsdp")
    return lax.ppermute(value, "fsdp", [(i, i ^ k) for i in range(n)])


def across_dp(value, k):
    n = lax.axis_size("dp")
    return lax.ppermute(value, "dp", [(i, i ^ k) for i in range(n)])


def columns_of(index, width):
    return pl.ds(pl.multiple_of(index * width, LANES), width)


def turn_kernel(blocks, steps, cot_ref, out_ref, scratch):
    rows = blocks * steps
    for c in range(cot_ref.shape[-1] // LANES):
        cols = slice(c * LANES, (c + 1) * LANES)
        scratch[c * rows : (c + 1) * rows, :] = (
            cot_ref[:, :, cols].reshape(rows, LANES).astype(jnp.float32)
        )
        for t in range(steps):
            out_ref[t * blocks : (t + 1) * blocks, cols] = scratch[
                pl.ds(c * rows + t, blocks, stride=steps), :
            ].astype(jnp.bfloat16)


def pack_kernel(n, split, order_ref, info_ref, frames_ref, out_ref, held, sems):
    me = lax.axis_index("dp")
    classes = held.shape[0]
    coming = []
    for c in range(classes):
        source = frames_ref.at[:, c] if split else frames_ref.at[pl.ds(c, 1)]
        coming.append(pltpu.make_async_copy(source, held.at[c], sems.at[c]))
        coming[c].start()
    start = jnp.int32(0)
    for i in range(n - 1):
        start = start + jnp.where(i < me, info_ref[i, 0], 0)
    leaving = []
    for c in range(classes):
        target = order_ref[0, lax.rem(start + c, n)]
        leaving.append(
            pltpu.make_async_copy(held.at[c], out_ref.at[target], sems.at[classes + c])
        )
        coming[c].wait()
        leaving[c].start()
    for copy in leaving:
        copy.wait()


def unpack_kernel(
    n, cap, blocks, steps, order_ref, info_ref, got_ref, out_ref, landed, scratch, sems
):
    me = lax.axis_index("dp")
    residue = jnp.int32(0)
    for r in range(n):
        residue = residue + jnp.where(order_ref[0, r] == me, r, 0)
    starts, so_far = [], jnp.int32(0)
    for i in range(n):
        starts.append(so_far)
        so_far = so_far + info_ref[i, 0]
    length = got_ref.shape[1]
    copies, rows = [], []
    for m in range(blocks):
        g = residue + m * n
        source, start = jnp.int32(0), jnp.int32(0)
        for i in range(1, n):
            later = starts[i] <= g
            source = jnp.where(later, i, source)
            start = jnp.where(later, starts[i], start)
        h = g - start
        copy = pltpu.make_async_copy(
            got_ref.at[source * cap + lax.div(h, n)], landed.at[m], sems.at[m]
        )
        copy.start()
        copies.append(copy)
        rows.append(info_ref[source, 1 + h])
    height = lax.broadcasted_iota(jnp.int32, (blocks, out_ref.shape[1]), 0)
    counts = jnp.zeros((blocks, out_ref.shape[1]), jnp.int32)
    for m in range(blocks):
        counts = jnp.where(height == m, rows[m], counts)
    out_ref[steps * blocks :, :] = counts.astype(jnp.float32).astype(jnp.bfloat16)
    for m in range(blocks):
        copies[m].wait()
        scratch[m * length : (m + 1) * length, :] = landed[m].astype(jnp.float32)
    group = length // steps
    for t in range(steps):
        for j in range(group):
            out_ref[t * blocks : (t + 1) * blocks, j * LANES : (j + 1) * LANES] = scratch[
                pl.ds(group * t + j, blocks, stride=length), :
            ].astype(jnp.bfloat16)


def cut_kernel(width, w_ref, p1, p2, p3, held, sems):
    me = lax.axis_index("fsdp")
    half = p2.shape[0]
    part = pl.ds(pl.multiple_of(lax.rem(lax.axis_index("dp"), 2) * half, TILE), half)
    stops = [
        (w_ref.at[part, columns_of(me ^ 2, width)], held.at[0, :half], p2),
        (w_ref.at[part, columns_of(me ^ 3, width)], held.at[1, :half], p3),
        (w_ref.at[:, columns_of(me ^ 1, width)], held.at[2], p1),
    ]
    coming = [
        pltpu.make_async_copy(source, place, sems.at[i])
        for i, (source, place, _) in enumerate(stops)
    ]
    leaving = [
        pltpu.make_async_copy(place, target, sems.at[3 + i])
        for i, (_, place, target) in enumerate(stops)
    ]
    for copy in coming:
        copy.start()
    for first, second in zip(coming, leaving):
        first.wait()
        second.start()
    for copy in leaving:
        copy.wait()


def tree(terms, low, high):
    if high - low == 1:
        left, right = terms[low]
        return left * right
    middle = (low + high) // 2
    return tree(terms, low, middle) + tree(terms, middle, high)


def project(patches_ref, subs, rows):
    me = lax.axis_index("fsdp")
    depth = subs[0].shape[0]
    left = jnp.concatenate(
        [patches_ref[:rows, columns_of(me ^ k, depth)] for k in range(4)], axis=1
    )
    right = jnp.concatenate([piece[...] for piece in subs], axis=0)
    return dot(left, right, 1, 0)


def forward(steps, blocks, patches, subs, depth_ref, gain_ref, work, mask, outs):
    rows = steps * blocks
    feat_ref, normed_ref, slope_ref, rstd_ref = outs
    width, taps = depth_ref.shape[1], depth_ref.shape[0]
    span = (taps - 1) // 2
    groups = range(len(patches))
    for g in groups:
        work[g * rows : (g + 1) * rows, :] = project(patches[g], subs, rows)
        counts = patches[g][rows:, :LANES].astype(jnp.float32)
        for t in range(steps):
            spot = g * rows + t * blocks
            mask[spot : spot + blocks, :] = jnp.where(counts > t, 1.0, 0.0)

    def column(c, _):
        cols = pl.ds(pl.multiple_of(c * LANES, LANES), LANES)
        weights = [
            jnp.broadcast_to(depth_ref[k : k + 1, cols], (blocks, LANES)).astype(jnp.bfloat16)
            for k in range(taps)
        ]
        for g in groups:
            spots = [
                slice(g * rows + t * blocks, g * rows + (t + 1) * blocks) for t in range(steps)
            ]
            values = []
            for t in range(steps):
                rounded = (work[spots[t], cols] * mask[spots[t], :]).astype(jnp.bfloat16)
                feat_ref[spots[t], cols] = rounded
                values.append(rounded)
            for t in range(steps):
                terms = [
                    (values[s], weights[s - t + span])
                    for s in range(steps)
                    if 0 <= s - t + span < taps
                ]
                conv = tree(terms, 0, len(terms)).astype(jnp.float32)
                keep = mask[spots[t], :]
                sigma = sigmoid(conv)
                swish = conv * sigma
                slope_ref[spots[t], cols] = (keep * (sigma + swish * (1.0 - sigma))).astype(
                    jnp.bfloat16
                )
                work[spots[t], cols] = values[t].astype(jnp.float32) + keep * swish
        return 0

    lax.fori_loop(0, width // LANES, column, 0)

    def norm(i, _):
        at = pl.ds(pl.multiple_of(i * 32, 32), 32)
        values = work[at, :]
        centred = values - jnp.mean(values, axis=-1, keepdims=True)
        rstd = lax.rsqrt(jnp.mean(centred * centred, axis=-1, keepdims=True) + EPSILON)
        normed_ref[at, :] = (centred * rstd * gain_ref[...]).astype(jnp.bfloat16)
        rstd_ref[at, :] = jnp.broadcast_to(rstd, (32, LANES))
        return 0

    lax.fori_loop(0, len(patches) * rows // 32, norm, 0)


def own_kernel(steps, blocks, patches, s0, s1, s2, s3, depth, gain, o0, o1, o2, o3, work, mask):
    forward(
        steps, blocks, [patches], [s0, s1, s2, s3], depth, gain, work, mask, (o0, o1, o2, o3)
    )


def middle_kernel(steps, blocks, *refs):
    patches, subs, depth, gain = refs[0:4], refs[4:8], refs[8], refs[9]
    rstd0, normed0, cots, w_own, w1, w2, w3, w2b, w3b, w_out_in = (
        refs[10], refs[11], refs[12:16], *refs[16:23]
    )
    grad_in, g1, g2, g3, pre_out, hidden_out, masked_out, w_slice_out = refs[23:31]
    feat_out, normed_out, slope_out, means_out = refs[31:35]
    work, mask, feat, normed, slope, rstd, means = refs[35:42]
    masked, w_in, w_out, pre_grad, scaled, hidden, grads, sems = refs[42:50]
    me = lax.axis_index("fsdp")
    parity = lax.rem(lax.axis_index("dp"), 2)
    rows = steps * blocks
    high, wide = w_own.shape[0], w1.shape[1]
    half = high // 2
    used = iter(range(sems.shape[0]))

    def move(source, place):
        copy = pltpu.make_async_copy(source, place, sems.at[next(used)])
        copy.start()
        return copy

    def rows_of(index, part=0, size=high):
        return pl.ds(pl.multiple_of(index * high + part * half, TILE), size)

    def group(k):
        return slice(k * rows, (k + 1) * rows)

    coming = [
        move(normed0, normed.at[group(0), :]),
        move(w_own.at[:, columns_of(me, wide)], w_in.at[rows_of(me), :]),
        move(w1, w_in.at[rows_of(me ^ 1), :]),
        move(w2, w_in.at[rows_of(me ^ 2, parity, half), :]),
        move(w3, w_in.at[rows_of(me ^ 3, parity, half), :]),
        move(w2b, w_in.at[rows_of(me ^ 2, 1 - parity, half), :]),
        move(w3b, w_in.at[rows_of(me ^ 3, 1 - parity, half), :]),
        move(w_out_in, w_out),
    ] + [move(cots[k], masked.at[group(k), :]) for k in range(4)]
    tail = slice(rows, 4 * rows)
    forward(
        steps, blocks, patches[1:], subs, depth, gain, work, mask,
        (feat, normed.at[tail, :], slope, rstd),
    )
    leaving = [
        move(feat, feat_out),
        move(normed.at[tail, :], normed_out),
        move(slope, slope_out),
    ]
    for copy in coming:
        copy.wait()
    leaving.append(move(w_in, w_slice_out))
    fine = jnp.broadcast_to(gain[...], (TILE, gain.shape[1]))
    coarse = fine.astype(jnp.bfloat16)
    small = (fine - coarse.astype(jnp.float32)).astype(jnp.bfloat16)
    pulled = (dot(coarse, w_in[...], 1, 0) + dot(small, w_in[...], 1, 0))[:1, :]
    share = 1.0 / gain.shape[1]
    for k in range(4):
        counts = patches[k][rows:, :LANES].astype(jnp.float32)[:, :1]
        keep = jnp.concatenate([counts > t for t in range(steps)], axis=0)
        at = group(k)
        kept = jnp.where(keep, masked[at, :], jnp.zeros((), jnp.bfloat16))
        masked[at, :] = kept
        pre = dot(normed[at, :], w_in[...], 1, 0)
        back = dot(kept, w_out[...], 1, 1)
        sigma = sigmoid(pre)
        swish = pre * sigma
        hidden[at, :] = swish.astype(jnp.bfloat16)
        grown = 0.5 * back * (sigma + swish * (1.0 - sigma))
        pre_grad[at, :] = grown.astype(jnp.bfloat16)
        grown = grown * (rstd0[:, :1] if k == 0 else rstd[(k - 1) * rows : k * rows, :1])
        scaled[at, :] = grown.astype(jnp.bfloat16)
        for i, other in enumerate((pulled, pre)):
            mean = jnp.sum(grown * other, axis=-1, keepdims=True) * share
            means[i, at, :] = jnp.broadcast_to(mean, (rows, LANES)).astype(jnp.bfloat16)
    leaving.append(move(scaled, pre_out))
    leaving.append(move(means, means_out))
    for slot, (k, place) in enumerate(((2, g2), (3, g3), (1, g1), (0, None))):
        part = dot(normed[:, columns_of(me ^ k, high)], pre_grad[...], 0, 0)
        grads[slot] = part.astype(jnp.bfloat16)
        leaving.append(
            move(grads.at[slot], grad_in.at[:, columns_of(me, wide)] if k == 0 else place)
        )
    leaving.append(move(hidden, hidden_out))
    leaving.append(move(masked, masked_out))
    for copy in leaving:
        copy.wait()


def backward_kernel(steps, blocks, *refs):
    gain, sources, taps_out = refs[0], refs[1:11], refs[11]
    scaled, w_in, masked, normed, slope, feat, means = refs[12:19]
    grad, sems = refs[19:21]
    rows = steps * blocks
    first, rest = slice(0, rows), slice(rows, 4 * rows)
    origins = list(sources)
    origins[2] = origins[2].at[first, :]
    places = [
        scaled, w_in, masked, normed.at[first, :], slope.at[first, :], feat.at[first, :], means,
        normed.at[rest, :], slope.at[rest, :], feat.at[rest, :],
    ]
    copies = [
        pltpu.make_async_copy(source, place, sems.at[i])
        for i, (source, place) in enumerate(zip(origins, places))
    ]
    for copy in copies:
        copy.start()
    for copy in copies[:3]:
        copy.wait()
    for k in range(4):
        at = slice(k * rows, (k + 1) * rows)
        pulled = dot(scaled[at, :], w_in[...], 1, 1) * gain[...]
        if k == 0:
            pulled = pulled + masked[...].astype(jnp.float32)
        grad[at, :] = pulled.astype(jnp.bfloat16)
    for copy in copies[3:]:
        copy.wait()
    taps = 2 * steps - 1

    def column(c, _):
        cols = pl.ds(pl.multiple_of(c * LANES, LANES), LANES)

        inverse = jnp.broadcast_to(1.0 / gain[:, cols], (blocks, LANES)).astype(jnp.bfloat16)

        def add(k, totals):
            spots = [
                pl.ds(pl.multiple_of(k * rows + t * blocks, TILE), blocks) for t in range(steps)
            ]
            left = [
                slope[spot, cols]
                * (
                    grad[spot, cols]
                    - means[0, spot, :]
                    - normed[spot, cols] * inverse * means[1, spot, :]
                )
                for spot in spots
            ]
            right = [feat[spot, cols] for spot in spots]
            new = []
            for tap in range(taps):
                shift = tap - (steps - 1)
                terms = [
                    (left[t], right[t + shift]) for t in range(steps) if 0 <= t + shift < steps
                ]
                part = tree(terms, 0, len(terms)).astype(jnp.float32)
                for half in range(0, blocks, HALF):
                    piece = part[half : half + HALF, :]
                    total = piece if half == 0 else total + piece
                new.append(totals[tap] + total)
            return tuple(new)

        zero = jnp.zeros((HALF, LANES), jnp.float32)
        totals = lax.fori_loop(0, 4, add, (zero,) * taps)
        for tap in range(taps):
            taps_out[tap, :, cols] = jnp.sum(totals[tap], axis=0, keepdims=True)
        taps_out[taps, :, cols] = jnp.zeros((1, LANES), jnp.float32)
        return 0

    lax.fori_loop(0, gain.shape[1] // LANES, column, 0)


def out_kernel(hidden, masked, out_ref, turned):
    turned[...] = hidden[...].T
    width = out_ref.shape[1]
    for c in range(0, width, 256):
        out_ref[:, c : c + 256] = (0.5 * dot(turned[...], masked[:, c : c + 256], 1, 0)).astype(
            jnp.bfloat16
        )


def join_kernel(width, start_ref, p1, p2, p3, out_ref, sems):
    me = lax.axis_index("fsdp")
    copies = [
        pltpu.make_async_copy(piece, out_ref.at[:, columns_of(me ^ k, width)], sems.at[k])
        for k, piece in enumerate((p1, p2, p3), 1)
    ]
    for copy in copies:
        copy.start()
    for copy in copies:
        copy.wait()


def on_device(
    frames,
    occupied_slot_counts,
    block_frame_rows,
    order,
    cotangent,
    sub_weight,
    depth_kernel,
    norm_gain,
    w_in,
    w_out,
):
    n = lax.axis_size("dp")
    home = frames.shape[2]
    cap = (home + n - 1) // n
    split = home % n == 0
    blocks, steps, width = cotangent.shape[2:]
    rows = blocks * steps
    deep, hidden_width = w_in.shape
    wide = hidden_width // 4
    bf16, f32 = jnp.bfloat16, jnp.float32
    dma = pltpu.SemaphoreType.DMA

    info = jnp.concatenate([occupied_slot_counts[0], block_frame_rows[0, 0]])
    infos = lax.all_to_all(
        jnp.broadcast_to(info[None], (n, home + 1)), "dp", split_axis=0, concat_axis=0, tiled=True
    )

    subs = [sub_weight, across(sub_weight, 1), across(sub_weight, 2)]
    w1, w2, w3 = pl.pallas_call(
        functools.partial(cut_kernel, wide),
        out_shape=(
            sds((deep, wide), bf16),
            sds((deep // 2, wide), bf16),
            sds((deep // 2, wide), bf16),
        ),
        in_specs=[ANY],
        out_specs=(ANY,) * 3,
        scratch_shapes=[pltpu.VMEM((3, deep, wide), bf16), dma((6,))],
        compiler_params=params(),
        cost_estimate=CHEAP,
    )(w_in)
    w1, w2, w3 = across(w1, 1), across(w2, 2), across(w3, 3)

    cot0 = pl.pallas_call(
        functools.partial(turn_kernel, blocks, steps),
        out_shape=sds((rows, width), bf16),
        in_specs=[VMEM],
        out_specs=VMEM,
        scratch_shapes=[pltpu.VMEM((rows * width // LANES, LANES), f32)],
        compiler_params=params(),
        cost_estimate=CHEAP,
    )(cotangent[0, 0])
    cots = [cot0, across(cot0, 1), across(cot0, 2)]

    block_shape = frames.shape[3:]
    held = frames[0, 0].reshape((cap, n) + block_shape) if split else frames[0, 0]
    packed = pl.pallas_call(
        functools.partial(pack_kernel, n, split),
        out_shape=sds((n, cap) + block_shape, bf16),
        in_specs=[SMEM, SMEM, ANY],
        out_specs=ANY,
        scratch_shapes=[
            pltpu.VMEM((n if split else home, cap) + block_shape, bf16),
            dma((2 * (n if split else home),)),
        ],
        compiler_params=params(),
        cost_estimate=CHEAP,
    )(order, infos, held)
    gain = norm_gain.reshape(1, width)
    packed, w2, w3, gain = lax.optimization_barrier((packed, w2, w3, gain))
    w2b, w3b = across_dp(w2, 1), across_dp(w3, 1)
    got = lax.all_to_all(packed, "dp", split_axis=0, concat_axis=0, tiled=True)
    subs.append(across(subs[2], 1))
    got, subs[1], subs[2], subs[3] = lax.optimization_barrier((got, subs[1], subs[2], subs[3]))
    patches0 = pl.pallas_call(
        functools.partial(unpack_kernel, n, cap, blocks, steps),
        out_shape=sds((rows + blocks, block_shape[0] // steps * LANES), bf16),
        in_specs=[SMEM, SMEM, ANY],
        out_specs=VMEM,
        scratch_shapes=[
            pltpu.VMEM((blocks,) + block_shape, bf16),
            pltpu.VMEM((blocks * block_shape[0], LANES), f32),
            dma((blocks,)),
        ],
        compiler_params=params(),
        cost_estimate=CHEAP,
    )(order, infos, got.reshape((n * cap,) + block_shape))
    patches = [patches0, across(patches0, 1), across(patches0, 2)]
    patches.append(across(patches[2], 1))
    cots.append(across(cots[2], 1))

    def kept(count):
        return (
            sds((count * rows, width), bf16),
            sds((count * rows, width), bf16),
            sds((count * rows, width), bf16),
            sds((count * rows, LANES), f32),
        )

    feat0, normed0, slope0, rstd0 = pl.pallas_call(
        functools.partial(own_kernel, steps, blocks),
        out_shape=kept(1),
        in_specs=[VMEM] * 7,
        out_specs=(VMEM,) * 4,
        scratch_shapes=[pltpu.VMEM((rows, width), f32), pltpu.VMEM((rows, LANES), f32)],
        compiler_params=params(),
        cost_estimate=CHEAP,
    )(patches0, *subs, depth_kernel, gain)
    (
        grad_in, g1, g2, g3, scaled, hidden, masked, w_slice, feat, normed, slope, means
    ) = pl.pallas_call(
        functools.partial(middle_kernel, steps, blocks),
        out_shape=(
            sds((deep, hidden_width), bf16),
            *[sds((deep, wide), bf16)] * 3,
            sds((4 * rows, wide), bf16),
            sds((4 * rows, wide), bf16),
            sds((4 * rows, width), bf16),
            sds((width, wide), bf16),
            *kept(3)[:3],
            sds((2, 4 * rows, LANES), bf16),
        ),
        in_specs=[VMEM] * 11 + [ANY] * 12,
        out_specs=(ANY,) * 12,
        scratch_shapes=[
            pltpu.VMEM((3 * rows, width), f32),
            pltpu.VMEM((3 * rows, LANES), f32),
            pltpu.VMEM((3 * rows, width), bf16),
            pltpu.VMEM((4 * rows, width), bf16),
            pltpu.VMEM((3 * rows, width), bf16),
            pltpu.VMEM((3 * rows, LANES), f32),
            pltpu.VMEM((2, 4 * rows, LANES), bf16),
            pltpu.VMEM((4 * rows, width), bf16),
            pltpu.VMEM((width, wide), bf16),
            pltpu.VMEM((wide, width), bf16),
            pltpu.VMEM((4 * rows, wide), bf16),
            pltpu.VMEM((4 * rows, wide), bf16),
            pltpu.VMEM((4 * rows, wide), bf16),
            pltpu.VMEM((4, deep, wide), bf16),
            dma((32,)),
        ],
        compiler_params=params(),
        cost_estimate=CHEAP,
    )(
        *patches, *subs, depth_kernel, gain, rstd0, normed0, *cots, w_in, w1, w2, w3, w2b, w3b, w_out
    )
    g1, g2, g3 = across(g1, 1), across(g2, 2), across(g3, 3)

    taps = pl.pallas_call(
        functools.partial(backward_kernel, steps, blocks),
        out_shape=sds((2 * steps, 1, width), f32),
        in_specs=[VMEM] + [ANY] * 10,
        out_specs=VMEM,
        scratch_shapes=[
            pltpu.VMEM((4 * rows, wide), bf16),
            pltpu.VMEM((width, wide), bf16),
            pltpu.VMEM((rows, width), bf16),
            pltpu.VMEM((4 * rows, width), bf16),
            pltpu.VMEM((4 * rows, width), bf16),
            pltpu.VMEM((4 * rows, width), bf16),
            pltpu.VMEM((2, 4 * rows, LANES), bf16),
            pltpu.VMEM((4 * rows, width), bf16),
            dma((10,)),
        ],
        compiler_params=params(),
        cost_estimate=CHEAP,
    )(gain, scaled, w_slice, masked, normed0, slope0, feat0, means, normed, slope, feat)

    every = ("dp", "fsdp")
    devices = n * lax.axis_size("fsdp")
    shares = lax.all_to_all(
        taps.reshape(devices, 1, -1), every, split_axis=0, concat_axis=0, tiled=True
    )
    share = jnp.sum(shares, axis=0, keepdims=True) / rows
    whole = lax.all_to_all(
        jnp.broadcast_to(share, shares.shape), every, split_axis=0, concat_axis=0, tiled=True
    )
    kernel_grad = whole.reshape(2 * steps, width)[: depth_kernel.shape[0]]

    grad_out = pl.pallas_call(
        out_kernel,
        out_shape=sds((wide, width), bf16),
        in_specs=[VMEM] * 2,
        out_specs=VMEM,
        scratch_shapes=[pltpu.VMEM((wide, 4 * rows), bf16)],
        compiler_params=params(),
        cost_estimate=CHEAP,
    )(hidden, masked)
    grad_in = pl.pallas_call(
        functools.partial(join_kernel, wide),
        out_shape=sds((deep, hidden_width), bf16),
        in_specs=[ANY] + [VMEM] * 3,
        out_specs=ANY,
        scratch_shapes=[dma((4,))],
        input_output_aliases={0: 0},
        compiler_params=params(),
        cost_estimate=CHEAP,
    )(grad_in, g1, g2, g3)
    return (grad_in[None], grad_out[None], kernel_grad)


def solution(mesh):
    placed = (
        P("dp", "fsdp", None, None, None),
        P("fsdp", "dp"),
        P("dp", "fsdp", None),
        P("fsdp", None),
        P("dp", "fsdp", None, None, None),
        P("fsdp", None),
        P(),
        P(),
        P("fsdp", None),
        P("fsdp", None),
    )
    return jax.shard_map(
        on_device,
        mesh=mesh,
        in_specs=placed,
        out_specs=(P("dp", "fsdp", None), P("dp", "fsdp", None), P()),
        check_vma=False,
    )
```

```python
import functools

import jax
import jax.numpy as jnp
from jax import lax
from jax.experimental import pallas as pl
from jax.experimental.pallas import tpu as pltpu
from jax.sharding import PartitionSpec as P

LANES = 128
HALF = 8
TILE = 16
EPSILON = 1e-05

VMEM = pl.BlockSpec(memory_space=pltpu.VMEM)
SMEM = pl.BlockSpec(memory_space=pltpu.SMEM)
ANY = pl.BlockSpec(memory_space=pl.ANY)
CHEAP = pl.CostEstimate(flops=0, transcendentals=0, bytes_accessed=0)


def params(mebibytes=16):
    return pltpu.CompilerParams(vmem_limit_bytes=mebibytes * 1024 * 1024)


def near(*arrays):
    return [pltpu.with_memory_space_constraint(array, pltpu.VMEM) for array in arrays]


def sds(shape, dtype):
    return jax.ShapeDtypeStruct(shape, dtype)


def sigmoid(values):
    return 0.5 * jnp.tanh(0.5 * values) + 0.5


def dot(left, right, left_dim, right_dim):
    return lax.dot_general(
        left, right, (((left_dim,), (right_dim,)), ((), ())), preferred_element_type=jnp.float32
    )


def across(value, k):
    n = lax.axis_size("fsdp")
    return lax.ppermute(value, "fsdp", [(i, i ^ k) for i in range(n)])


def across_dp(value, k):
    n = lax.axis_size("dp")
    return lax.ppermute(value, "dp", [(i, i ^ k) for i in range(n)])


def columns_of(index, width):
    return pl.ds(pl.multiple_of(index * width, LANES), width)


def turn_kernel(blocks, steps, cot_ref, out_ref, scratch):
    rows = blocks * steps
    for c in range(cot_ref.shape[-1] // LANES):
        cols = slice(c * LANES, (c + 1) * LANES)
        scratch[c * rows : (c + 1) * rows, :] = (
            cot_ref[:, :, cols].reshape(rows, LANES).astype(jnp.float32)
        )
        for t in range(steps):
            out_ref[t * blocks : (t + 1) * blocks, cols] = scratch[
                pl.ds(c * rows + t, blocks, stride=steps), :
            ].astype(jnp.bfloat16)


def pack_kernel(n, split, order_ref, info_ref, frames_ref, out_ref, held, sems):
    me = lax.axis_index("dp")
    classes = held.shape[0]
    coming = []
    for c in range(classes):
        source = frames_ref.at[:, c] if split else frames_ref.at[pl.ds(c, 1)]
        coming.append(pltpu.make_async_copy(source, held.at[c], sems.at[c]))
        coming[c].start()
    start = jnp.int32(0)
    for i in range(n - 1):
        start = start + jnp.where(i < me, info_ref[i, 0], 0)
    leaving = []
    for c in range(classes):
        target = order_ref[0, lax.rem(start + c, n)]
        leaving.append(
            pltpu.make_async_copy(held.at[c], out_ref.at[target], sems.at[classes + c])
        )
        coming[c].wait()
        leaving[c].start()
    for copy in leaving:
        copy.wait()


def unpack_kernel(
    n, cap, blocks, steps, order_ref, info_ref, got_ref, out_ref, landed, scratch, sems
):
    me = lax.axis_index("dp")
    residue = jnp.int32(0)
    for r in range(n):
        residue = residue + jnp.where(order_ref[0, r] == me, r, 0)
    starts, so_far = [], jnp.int32(0)
    for i in range(n):
        starts.append(so_far)
        so_far = so_far + info_ref[i, 0]
    length = got_ref.shape[1]
    copies, rows = [], []
    for m in range(blocks):
        g = residue + m * n
        source, start = jnp.int32(0), jnp.int32(0)
        for i in range(1, n):
            later = starts[i] <= g
            source = jnp.where(later, i, source)
            start = jnp.where(later, starts[i], start)
        h = g - start
        copy = pltpu.make_async_copy(
            got_ref.at[source * cap + lax.div(h, n)], landed.at[m], sems.at[m]
        )
        copy.start()
        copies.append(copy)
        rows.append(info_ref[source, 1 + h])
    height = lax.broadcasted_iota(jnp.int32, (blocks, out_ref.shape[1]), 0)
    counts = jnp.zeros((blocks, out_ref.shape[1]), jnp.int32)
    for m in range(blocks):
        counts = jnp.where(height == m, rows[m], counts)
    out_ref[steps * blocks :, :] = counts.astype(jnp.float32).astype(jnp.bfloat16)
    for m in range(blocks):
        copies[m].wait()
        scratch[m * length : (m + 1) * length, :] = landed[m].astype(jnp.float32)
    group = length // steps
    for t in range(steps):
        for j in range(group):
            out_ref[t * blocks : (t + 1) * blocks, j * LANES : (j + 1) * LANES] = scratch[
                pl.ds(group * t + j, blocks, stride=length), :
            ].astype(jnp.bfloat16)


def cut_kernel(width, w_ref, p0, p1, p2, p3, sems):
    me = lax.axis_index("fsdp")
    half = p2.shape[0]
    part = pl.ds(pl.multiple_of(lax.rem(lax.axis_index("dp"), 2) * half, TILE), half)
    copies = [
        pltpu.make_async_copy(w_ref.at[part, columns_of(me ^ 2, width)], p2, sems.at[2]),
        pltpu.make_async_copy(w_ref.at[part, columns_of(me ^ 3, width)], p3, sems.at[3]),
        pltpu.make_async_copy(w_ref.at[:, columns_of(me ^ 1, width)], p1, sems.at[1]),
        pltpu.make_async_copy(w_ref.at[:, columns_of(me, width)], p0, sems.at[0]),
    ]
    for copy in copies:
        copy.start()
    for copy in copies:
        copy.wait()


def tree(terms, low, high):
    if high - low == 1:
        left, right = terms[low]
        return left * right
    middle = (low + high) // 2
    return tree(terms, low, middle) + tree(terms, middle, high)


def project(patches_ref, subs, rows):
    me = lax.axis_index("fsdp")
    depth = subs[0].shape[0]
    left = jnp.concatenate(
        [patches_ref[:rows, columns_of(me ^ k, depth)] for k in range(4)], axis=1
    )
    right = jnp.concatenate([piece[...] for piece in subs], axis=0)
    return dot(left, right, 1, 0)


def forward(steps, blocks, patches, subs, depth_ref, gain_ref, work, mask, outs):
    rows = steps * blocks
    feat_ref, normed_ref, slope_ref, rstd_ref = outs
    width, taps = depth_ref.shape[1], depth_ref.shape[0]
    span = (taps - 1) // 2
    groups = range(len(patches))
    for g in groups:
        work[g * rows : (g + 1) * rows, :] = project(patches[g], subs, rows)
        counts = patches[g][rows:, :LANES].astype(jnp.float32)
        for t in range(steps):
            spot = g * rows + t * blocks
            mask[spot : spot + blocks, :] = jnp.where(counts > t, 1.0, 0.0)

    def column(c, _):
        cols = pl.ds(pl.multiple_of(c * LANES, LANES), LANES)
        weights = [
            jnp.broadcast_to(depth_ref[k : k + 1, cols], (blocks, LANES)).astype(jnp.bfloat16)
            for k in range(taps)
        ]
        for g in groups:
            spots = [
                slice(g * rows + t * blocks, g * rows + (t + 1) * blocks) for t in range(steps)
            ]
            values = []
            for t in range(steps):
                rounded = (work[spots[t], cols] * mask[spots[t], :]).astype(jnp.bfloat16)
                feat_ref[spots[t], cols] = rounded
                values.append(rounded)
            for t in range(steps):
                terms = [
                    (values[s], weights[s - t + span])
                    for s in range(steps)
                    if 0 <= s - t + span < taps
                ]
                conv = tree(terms, 0, len(terms)).astype(jnp.float32)
                keep = mask[spots[t], :]
                sigma = sigmoid(conv)
                swish = conv * sigma
                slope_ref[spots[t], cols] = (keep * (sigma + swish * (1.0 - sigma))).astype(
                    jnp.bfloat16
                )
                work[spots[t], cols] = values[t].astype(jnp.float32) + keep * swish
        return 0

    lax.fori_loop(0, width // LANES, column, 0)

    def norm(i, _):
        at = pl.ds(pl.multiple_of(i * 32, 32), 32)
        values = work[at, :]
        centred = values - jnp.mean(values, axis=-1, keepdims=True)
        rstd = lax.rsqrt(jnp.mean(centred * centred, axis=-1, keepdims=True) + EPSILON)
        normed_ref[at, :] = (centred * rstd * gain_ref[...]).astype(jnp.bfloat16)
        rstd_ref[at, :] = jnp.broadcast_to(rstd, (32, LANES))
        return 0

    lax.fori_loop(0, len(patches) * rows // 32, norm, 0)


def own_kernel(steps, blocks, patches, s0, s1, s2, s3, depth, gain, o0, o1, o2, o3, work, mask):
    forward(
        steps, blocks, [patches], [s0, s1, s2, s3], depth, gain, work, mask, (o0, o1, o2, o3)
    )


def middle_kernel(steps, blocks, *refs):
    patches, subs, depth, gain, rstd0, normed0 = refs[0:4], refs[4:8], *refs[8:12]
    cots, w_own, w1, w2, w3, w2b, w3b, w_out = refs[12:16], *refs[16:23]
    grads, scaled, hidden, masked, w_in = refs[23:27], *refs[27:31]
    feat, normed, slope, means = refs[31:35]
    work, mask, rstd, pre_grad = refs[35:39]
    me = lax.axis_index("fsdp")
    parity = lax.rem(lax.axis_index("dp"), 2)
    rows = steps * blocks
    high, wide = w1.shape
    half = high // 2

    def rows_of(index, part=0, size=high):
        return pl.ds(pl.multiple_of(index * high + part * half, TILE), size)

    w_in[rows_of(me), :] = w_own[...]
    w_in[rows_of(me ^ 1), :] = w1[...]
    w_in[rows_of(me ^ 2, parity, half), :] = w2[...]
    w_in[rows_of(me ^ 3, parity, half), :] = w3[...]
    w_in[rows_of(me ^ 2, 1 - parity, half), :] = w2b[...]
    w_in[rows_of(me ^ 3, 1 - parity, half), :] = w3b[...]
    forward(
        steps, blocks, patches[1:], subs, depth, gain, work, mask, (feat, normed, slope, rstd)
    )
    fine = jnp.broadcast_to(gain[...], (TILE, gain.shape[1]))
    coarse = fine.astype(jnp.bfloat16)
    small = (fine - coarse.astype(jnp.float32)).astype(jnp.bfloat16)
    pulled = (dot(coarse, w_in[...], 1, 0) + dot(small, w_in[...], 1, 0))[:1, :]
    share = 1.0 / gain.shape[1]
    for k in range(4):
        at = slice(k * rows, (k + 1) * rows)
        tail = slice((k - 1) * rows, k * rows)
        counts = patches[k][rows:, :LANES].astype(jnp.float32)[:, :1]
        keep = jnp.concatenate([counts > t for t in range(steps)], axis=0)
        kept = jnp.where(keep, cots[k][...], jnp.zeros((), jnp.bfloat16))
        masked[at, :] = kept
        pre = dot(normed0[...] if k == 0 else normed[tail, :], w_in[...], 1, 0)
        back = dot(kept, w_out[...], 1, 1)
        sigma = sigmoid(pre)
        swish = pre * sigma
        hidden[at, :] = swish.astype(jnp.bfloat16)
        grown = 0.5 * back * (sigma + swish * (1.0 - sigma))
        pre_grad[at, :] = grown.astype(jnp.bfloat16)
        grown = grown * (rstd0[:, :1] if k == 0 else rstd[tail, :1])
        scaled[at, :] = grown.astype(jnp.bfloat16)
        for i, other in enumerate((pulled, pre)):
            mean = jnp.sum(grown * other, axis=-1, keepdims=True) * share
            means[i, at, :] = jnp.broadcast_to(mean, (rows, LANES)).astype(jnp.bfloat16)
    for k in (2, 3, 1, 0):
        cols = columns_of(me ^ k, high)
        left = jnp.concatenate([normed0[:, cols], normed[:, cols]], axis=0)
        grads[k][...] = dot(left, pre_grad[...], 0, 0).astype(jnp.bfloat16)


def backward_kernel(steps, blocks, *refs):
    gain, scaled, w_in, masked, means, normed0, slope0, feat0, normed, slope, feat = refs[0:11]
    taps_out, grad = refs[11:13]
    rows = steps * blocks
    for k in range(4):
        at = slice(k * rows, (k + 1) * rows)
        pulled = dot(scaled[at, :], w_in[...], 1, 1) * gain[...]
        if k == 0:
            pulled = pulled + masked[at, :].astype(jnp.float32)
        grad[at, :] = pulled.astype(jnp.bfloat16)
    taps = 2 * steps - 1

    def column(c, _):
        cols = pl.ds(pl.multiple_of(c * LANES, LANES), LANES)

        inverse = jnp.broadcast_to(1.0 / gain[:, cols], (blocks, LANES)).astype(jnp.bfloat16)

        def add(k, totals, held, near_normed, near_slope, near_feat):
            def spots(group):
                return [
                    pl.ds(pl.multiple_of(group * rows + t * blocks, TILE), blocks)
                    for t in range(steps)
                ]

            left = [
                near_slope[here, cols]
                * (
                    grad[spot, cols]
                    - means[0, spot, :]
                    - near_normed[here, cols] * inverse * means[1, spot, :]
                )
                for spot, here in zip(spots(k), spots(held))
            ]
            right = [near_feat[here, cols] for here in spots(held)]
            new = []
            for tap in range(taps):
                shift = tap - (steps - 1)
                terms = [
                    (left[t], right[t + shift]) for t in range(steps) if 0 <= t + shift < steps
                ]
                part = tree(terms, 0, len(terms)).astype(jnp.float32)
                for half in range(0, blocks, HALF):
                    piece = part[half : half + HALF, :]
                    total = piece if half == 0 else total + piece
                new.append(totals[tap] + total)
            return tuple(new)

        zero = jnp.zeros((HALF, LANES), jnp.float32)
        totals = add(0, (zero,) * taps, 0, normed0, slope0, feat0)
        totals = lax.fori_loop(
            1, 4, lambda k, totals: add(k, totals, k - 1, normed, slope, feat), totals
        )
        for tap in range(taps):
            taps_out[tap, :, cols] = jnp.sum(totals[tap], axis=0, keepdims=True)
        taps_out[taps, :, cols] = jnp.zeros((1, LANES), jnp.float32)
        return 0

    lax.fori_loop(0, gain.shape[1] // LANES, column, 0)


def out_kernel(hidden, masked, out_ref, turned):
    turned[...] = hidden[...].T
    width = out_ref.shape[1]
    for c in range(0, width, 256):
        out_ref[:, c : c + 256] = (0.5 * dot(turned[...], masked[:, c : c + 256], 1, 0)).astype(
            jnp.bfloat16
        )


def join_kernel(width, p0, p1, p2, p3, out_ref, sems):
    me = lax.axis_index("fsdp")
    copies = [
        pltpu.make_async_copy(piece, out_ref.at[:, columns_of(me ^ k, width)], sems.at[k])
        for k, piece in enumerate((p0, p1, p2, p3))
    ]
    for copy in copies:
        copy.start()
    for copy in copies:
        copy.wait()


def on_device(
    frames,
    occupied_slot_counts,
    block_frame_rows,
    order,
    cotangent,
    sub_weight,
    depth_kernel,
    norm_gain,
    w_in,
    w_out,
):
    n = lax.axis_size("dp")
    home = frames.shape[2]
    cap = (home + n - 1) // n
    split = home % n == 0
    blocks, steps, width = cotangent.shape[2:]
    rows = blocks * steps
    deep, hidden_width = w_in.shape
    wide = hidden_width // 4
    bf16, f32 = jnp.bfloat16, jnp.float32
    dma = pltpu.SemaphoreType.DMA

    info = jnp.concatenate([occupied_slot_counts[0], block_frame_rows[0, 0]])
    infos = lax.all_to_all(
        jnp.broadcast_to(info[None], (n, home + 1)), "dp", split_axis=0, concat_axis=0, tiled=True
    )

    subs = [sub_weight, across(sub_weight, 1), across(sub_weight, 2)]
    w0, w1, w2, w3 = pl.pallas_call(
        functools.partial(cut_kernel, wide),
        out_shape=(
            pltpu.VMEM((deep, wide), bf16),
            pltpu.VMEM((deep, wide), bf16),
            pltpu.VMEM((deep // 2, wide), bf16),
            pltpu.VMEM((deep // 2, wide), bf16),
        ),
        in_specs=[ANY],
        out_specs=(VMEM,) * 4,
        scratch_shapes=[dma((4,))],
        compiler_params=params(),
        cost_estimate=CHEAP,
    )(w_in)
    w1, w2, w3 = across(w1, 1), across(w2, 2), across(w3, 3)

    cot0 = pl.pallas_call(
        functools.partial(turn_kernel, blocks, steps),
        out_shape=sds((rows, width), bf16),
        in_specs=[VMEM],
        out_specs=VMEM,
        scratch_shapes=[pltpu.VMEM((rows * width // LANES, LANES), f32)],
        compiler_params=params(),
        cost_estimate=CHEAP,
    )(cotangent[0, 0])
    cots = [cot0, across(cot0, 1), across(cot0, 2)]

    block_shape = frames.shape[3:]
    held = frames[0, 0].reshape((cap, n) + block_shape) if split else frames[0, 0]
    packed = pl.pallas_call(
        functools.partial(pack_kernel, n, split),
        out_shape=sds((n, cap) + block_shape, bf16),
        in_specs=[SMEM, SMEM, ANY],
        out_specs=ANY,
        scratch_shapes=[
            pltpu.VMEM((n if split else home, cap) + block_shape, bf16),
            dma((2 * (n if split else home),)),
        ],
        compiler_params=params(),
        cost_estimate=CHEAP,
    )(order, infos, held)
    gain = norm_gain.reshape(1, width)
    packed, w2, w3, subs[2], gain = lax.optimization_barrier((packed, w2, w3, subs[2], gain))
    w2b, w3b = across_dp(w2, 1), across_dp(w3, 1)
    got = lax.all_to_all(packed, "dp", split_axis=0, concat_axis=0, tiled=True)
    subs.append(across(subs[2], 1))
    got, subs[1], subs[3] = lax.optimization_barrier((got, subs[1], subs[3]))
    patches0 = pl.pallas_call(
        functools.partial(unpack_kernel, n, cap, blocks, steps),
        out_shape=sds((rows + blocks, block_shape[0] // steps * LANES), bf16),
        in_specs=[SMEM, SMEM, ANY],
        out_specs=VMEM,
        scratch_shapes=[
            pltpu.VMEM((blocks,) + block_shape, bf16),
            pltpu.VMEM((blocks * block_shape[0], LANES), f32),
            dma((blocks,)),
        ],
        compiler_params=params(),
        cost_estimate=CHEAP,
    )(order, infos, got.reshape((n * cap,) + block_shape))
    patches = [patches0, across(patches0, 1), across(patches0, 2)]
    patches.append(across(patches[2], 1))
    cots.append(across(cots[2], 1))

    def kept(count):
        return (
            pltpu.VMEM((count * rows, width), bf16),
            pltpu.VMEM((count * rows, width), bf16),
            pltpu.VMEM((count * rows, width), bf16),
            pltpu.VMEM((count * rows, LANES), f32),
        )

    feat0, normed0, slope0, rstd0 = pl.pallas_call(
        functools.partial(own_kernel, steps, blocks),
        out_shape=kept(1),
        in_specs=[VMEM] * 7,
        out_specs=(VMEM,) * 4,
        scratch_shapes=[pltpu.VMEM((rows, width), f32), pltpu.VMEM((rows, LANES), f32)],
        compiler_params=params(),
        cost_estimate=CHEAP,
    )(*near(patches0, *subs, depth_kernel, gain))
    (
        g0, g1, g2, g3, scaled, hidden, masked, w_slice, feat, normed, slope, means
    ) = pl.pallas_call(
        functools.partial(middle_kernel, steps, blocks),
        out_shape=(
            *[pltpu.VMEM((deep, wide), bf16)] * 4,
            pltpu.VMEM((4 * rows, wide), bf16),
            pltpu.VMEM((4 * rows, wide), bf16),
            pltpu.VMEM((4 * rows, width), bf16),
            pltpu.VMEM((width, wide), bf16),
            *kept(3)[:3],
            pltpu.VMEM((2, 4 * rows, LANES), bf16),
        ),
        in_specs=[VMEM] * 23,
        out_specs=(VMEM,) * 12,
        scratch_shapes=[
            pltpu.VMEM((3 * rows, width), f32),
            pltpu.VMEM((3 * rows, LANES), f32),
            pltpu.VMEM((3 * rows, LANES), f32),
            pltpu.VMEM((4 * rows, wide), bf16),
        ],
        compiler_params=params(24),
        cost_estimate=CHEAP,
    )(
        *near(
            *patches, *subs, depth_kernel, gain, rstd0, normed0, *cots,
            w0, w1, w2, w3, w2b, w3b, w_out,
        )
    )
    g1, g2, g3 = across(g1, 1), across(g2, 2), across(g3, 3)

    taps = pl.pallas_call(
        functools.partial(backward_kernel, steps, blocks),
        out_shape=sds((2 * steps, 1, width), f32),
        in_specs=[VMEM] * 11,
        out_specs=VMEM,
        scratch_shapes=[pltpu.VMEM((4 * rows, width), bf16)],
        compiler_params=params(),
        cost_estimate=CHEAP,
    )(
        *near(
            gain, scaled, w_slice, masked, means, normed0, slope0, feat0, normed, slope, feat
        )
    )
    taps, g2, hidden = lax.optimization_barrier((taps, g2, hidden))

    every = ("dp", "fsdp")
    devices = n * lax.axis_size("fsdp")
    shares = lax.all_to_all(
        taps.reshape(devices, 1, -1), every, split_axis=0, concat_axis=0, tiled=True
    )
    share = jnp.sum(shares, axis=0, keepdims=True) / rows
    whole = lax.all_to_all(
        jnp.broadcast_to(share, shares.shape), every, split_axis=0, concat_axis=0, tiled=True
    )
    kernel_grad = whole.reshape(2 * steps, width)[: depth_kernel.shape[0]]

    grad_out = pl.pallas_call(
        out_kernel,
        out_shape=sds((wide, width), bf16),
        in_specs=[VMEM] * 2,
        out_specs=VMEM,
        scratch_shapes=[pltpu.VMEM((wide, 4 * rows), bf16)],
        compiler_params=params(),
        cost_estimate=CHEAP,
    )(*near(hidden, masked))
    grad_in = pl.pallas_call(
        functools.partial(join_kernel, wide),
        out_shape=sds((deep, hidden_width), bf16),
        in_specs=[VMEM] * 4,
        out_specs=ANY,
        scratch_shapes=[dma((4,))],
        compiler_params=params(),
        cost_estimate=CHEAP,
    )(*near(g0, g1, g2, g3))
    return (grad_in[None], grad_out[None], kernel_grad)


def solution(mesh):
    placed = (
        P("dp", "fsdp", None, None, None),
        P("fsdp", "dp"),
        P("dp", "fsdp", None),
        P("fsdp", None),
        P("dp", "fsdp", None, None, None),
        P("fsdp", None),
        P(),
        P(),
        P("fsdp", None),
        P("fsdp", None),
    )
    return jax.shard_map(
        on_device,
        mesh=mesh,
        in_specs=placed,
        out_specs=(P("dp", "fsdp", None), P("dp", "fsdp", None), P()),
        check_vma=False,
    )
```

```python
import functools

import jax
import jax.numpy as jnp
from jax import lax
from jax.experimental import pallas as pl
from jax.experimental.pallas import tpu as pltpu
from jax.sharding import PartitionSpec as P

LANES = 128
HALF = 8
TILE = 16
EPSILON = 1e-05

VMEM = pl.BlockSpec(memory_space=pltpu.VMEM)
SMEM = pl.BlockSpec(memory_space=pltpu.SMEM)
ANY = pl.BlockSpec(memory_space=pl.ANY)


def params(mebibytes=16):
    return pltpu.CompilerParams(vmem_limit_bytes=mebibytes * 1024 * 1024)


def cost(microseconds):
    return pl.CostEstimate(
        flops=0, transcendentals=0, bytes_accessed=int(microseconds * 3.6e6)
    )


def near(*arrays):
    return [pltpu.with_memory_space_constraint(array, pltpu.VMEM) for array in arrays]


def sds(shape, dtype):
    return jax.ShapeDtypeStruct(shape, dtype)


def sigmoid(values):
    return 0.5 * jnp.tanh(0.5 * values) + 0.5


def dot(left, right, left_dim, right_dim):
    return lax.dot_general(
        left, right, (((left_dim,), (right_dim,)), ((), ())), preferred_element_type=jnp.float32
    )


def across(value, k):
    n = lax.axis_size("fsdp")
    return lax.ppermute(value, "fsdp", [(i, i ^ k) for i in range(n)])


def across_dp(value, k):
    n = lax.axis_size("dp")
    return lax.ppermute(value, "dp", [(i, i ^ k) for i in range(n)])


def columns_of(index, width):
    return pl.ds(pl.multiple_of(index * width, LANES), width)


def prepare_kernel(blocks, steps, width, cot_ref, w_ref, out_ref, pair_ref, scratch, sems):
    rows = blocks * steps
    half = pair_ref.shape[0] - rows
    cols = columns_of(lax.axis_index("fsdp") ^ 1, width)
    copies = [
        pltpu.make_async_copy(
            w_ref.at[i * half : (i + 1) * half, cols],
            pair_ref.at[rows:, i * width : (i + 1) * width],
            sems.at[i],
        )
        for i in range(2)
    ]
    for copy in copies:
        copy.start()
    for c in range(cot_ref.shape[-1] // LANES):
        cols = slice(c * LANES, (c + 1) * LANES)
        scratch[c * rows : (c + 1) * rows, :] = (
            cot_ref[:, :, cols].reshape(rows, LANES).astype(jnp.float32)
        )
        for t in range(steps):
            at = slice(t * blocks, (t + 1) * blocks)
            turned = scratch[pl.ds(c * rows + t, blocks, stride=steps), :].astype(jnp.bfloat16)
            out_ref[at, cols] = turned
            pair_ref[at, cols] = turned
    for copy in copies:
        copy.wait()


def pack_kernel(n, split, order_ref, info_ref, frames_ref, out_ref, held, sems):
    me = lax.axis_index("dp")
    classes = held.shape[0]
    coming = []
    for c in range(classes):
        source = frames_ref.at[:, c] if split else frames_ref.at[pl.ds(c, 1)]
        coming.append(pltpu.make_async_copy(source, held.at[c], sems.at[c]))
        coming[c].start()
    start = jnp.int32(0)
    for i in range(n - 1):
        start = start + jnp.where(i < me, info_ref[i, 0], 0)
    leaving = []
    for c in range(classes):
        target = order_ref[0, lax.rem(start + c, n)]
        leaving.append(
            pltpu.make_async_copy(held.at[c], out_ref.at[target], sems.at[classes + c])
        )
        coming[c].wait()
        leaving[c].start()
    for copy in leaving:
        copy.wait()


def unpack_kernel(
    n, cap, blocks, steps, order_ref, info_ref, got_ref, out_ref, landed, scratch, sems
):
    me = lax.axis_index("dp")
    residue = jnp.int32(0)
    for r in range(n):
        residue = residue + jnp.where(order_ref[0, r] == me, r, 0)
    starts, so_far = [], jnp.int32(0)
    for i in range(n):
        starts.append(so_far)
        so_far = so_far + info_ref[i, 0]
    length = got_ref.shape[1]
    copies, rows = [], []
    for m in range(blocks):
        g = residue + m * n
        source, start = jnp.int32(0), jnp.int32(0)
        for i in range(1, n):
            later = starts[i] <= g
            source = jnp.where(later, i, source)
            start = jnp.where(later, starts[i], start)
        h = g - start
        copy = pltpu.make_async_copy(
            got_ref.at[source * cap + lax.div(h, n)], landed.at[m], sems.at[m]
        )
        copy.start()
        copies.append(copy)
        rows.append(info_ref[source, 1 + h])
    height = lax.broadcasted_iota(jnp.int32, (blocks, out_ref.shape[1]), 0)
    counts = jnp.zeros((blocks, out_ref.shape[1]), jnp.int32)
    for m in range(blocks):
        counts = jnp.where(height == m, rows[m], counts)
    out_ref[steps * blocks :, :] = counts.astype(jnp.float32).astype(jnp.bfloat16)
    for m in range(blocks):
        copies[m].wait()
        scratch[m * length : (m + 1) * length, :] = landed[m].astype(jnp.float32)
    group = length // steps
    for t in range(steps):
        for j in range(group):
            out_ref[t * blocks : (t + 1) * blocks, j * LANES : (j + 1) * LANES] = scratch[
                pl.ds(group * t + j, blocks, stride=length), :
            ].astype(jnp.bfloat16)


def cut_kernel(width, w_ref, p2, p3, held, sems):
    me = lax.axis_index("fsdp")
    half = p2.shape[0]
    part = pl.ds(pl.multiple_of(lax.rem(lax.axis_index("dp"), 2) * half, TILE), half)
    coming = [
        pltpu.make_async_copy(w_ref.at[part, columns_of(me ^ k, width)], held.at[i], sems.at[0, i])
        for i, k in enumerate((2, 3))
    ]
    leaving = [
        pltpu.make_async_copy(held.at[i], target, sems.at[1, i])
        for i, target in enumerate((p2, p3))
    ]
    for copy in coming:
        copy.start()
    for first, second in zip(coming, leaving):
        first.wait()
        second.start()
    for copy in leaving:
        copy.wait()


def tree(terms, low, high):
    if high - low == 1:
        left, right = terms[low]
        return left * right
    middle = (low + high) // 2
    return tree(terms, low, middle) + tree(terms, middle, high)


def forward(steps, blocks, patches, sub_ref, depth_ref, gain_ref, work, mask, outs):
    rows = steps * blocks
    feat_ref, normed_ref, slope_ref, rstd_ref = outs
    width, taps = depth_ref.shape[1], depth_ref.shape[0]
    span = (taps - 1) // 2
    groups = range(len(patches))
    for g in groups:
        work[g * rows : (g + 1) * rows, :] = dot(patches[g][:rows, :], sub_ref[...], 1, 0)
        counts = patches[g][rows:, :LANES].astype(jnp.float32)
        for t in range(steps):
            spot = g * rows + t * blocks
            mask[spot : spot + blocks, :] = jnp.where(counts > t, 1.0, 0.0)

    def column(c, _):
        cols = pl.ds(pl.multiple_of(c * LANES, LANES), LANES)
        weights = [
            jnp.broadcast_to(depth_ref[k : k + 1, cols], (blocks, LANES)).astype(jnp.bfloat16)
            for k in range(taps)
        ]
        for g in groups:
            spots = [
                slice(g * rows + t * blocks, g * rows + (t + 1) * blocks) for t in range(steps)
            ]
            values = []
            for t in range(steps):
                rounded = (work[spots[t], cols] * mask[spots[t], :]).astype(jnp.bfloat16)
                feat_ref[spots[t], cols] = rounded
                values.append(rounded)
            for t in range(steps):
                terms = [
                    (values[s], weights[s - t + span])
                    for s in range(steps)
                    if 0 <= s - t + span < taps
                ]
                conv = tree(terms, 0, len(terms)).astype(jnp.float32)
                keep = mask[spots[t], :]
                sigma = sigmoid(conv)
                swish = conv * sigma
                slope_ref[spots[t], cols] = (keep * (sigma + swish * (1.0 - sigma))).astype(
                    jnp.bfloat16
                )
                work[spots[t], cols] = values[t].astype(jnp.float32) + keep * swish
        return 0

    lax.fori_loop(0, width // LANES, column, 0)

    def norm(i, _):
        at = pl.ds(pl.multiple_of(i * 32, 32), 32)
        values = work[at, :]
        centred = values - jnp.mean(values, axis=-1, keepdims=True)
        rstd = lax.rsqrt(jnp.mean(centred * centred, axis=-1, keepdims=True) + EPSILON)
        normed_ref[at, :] = (centred * rstd * gain_ref[...]).astype(jnp.bfloat16)
        rstd_ref[at, :] = jnp.broadcast_to(rstd, (32, LANES))
        return 0

    lax.fori_loop(0, len(patches) * rows // 32, norm, 0)


def own_kernel(steps, blocks, patches, weight, depth, gain, o0, o1, o2, o3, work, mask):
    forward(steps, blocks, [patches], weight, depth, gain, work, mask, (o0, o1, o2, o3))


def middle_kernel(steps, blocks, *refs):
    patches, weight, depth, gain, rstd0, normed0 = refs[0:4], *refs[4:9]
    cot0, pair, cot2, cot3, w_own, w2, w3, w2b, w3b, w_out_in = refs[9:19]
    grads, scaled, hidden, masked, w_in = refs[19:23], *refs[23:27]
    feat, normed, slope, means = refs[27:31]
    work, mask, rstd, pre_grad, w_out, held, sems = refs[31:38]
    me = lax.axis_index("fsdp")
    parity = lax.rem(lax.axis_index("dp"), 2)
    rows = steps * blocks
    half, wide = w2.shape
    high = 2 * half
    used = iter(range(sems.shape[0]))

    def move(source, place):
        copy = pltpu.make_async_copy(source, place, sems.at[next(used)])
        copy.start()
        return copy

    def rows_of(index, part=0, size=high):
        return pl.ds(pl.multiple_of(index * high + part * half, TILE), size)

    coming = [
        move(w_own.at[:, columns_of(me, wide)], w_in.at[rows_of(me), :]),
        move(pair.at[rows:, :wide], w_in.at[rows_of(me ^ 1, 0, half), :]),
        move(pair.at[rows:, wide:], w_in.at[rows_of(me ^ 1, 1, half), :]),
        move(w2, w_in.at[rows_of(me ^ 2, parity, half), :]),
        move(w3, w_in.at[rows_of(me ^ 3, parity, half), :]),
        move(w2b, w_in.at[rows_of(me ^ 2, 1 - parity, half), :]),
        move(w3b, w_in.at[rows_of(me ^ 3, 1 - parity, half), :]),
        move(w_out_in, w_out),
        move(cot0, masked.at[:rows, :]),
        move(pair.at[:rows, :], masked.at[rows : 2 * rows, :]),
        move(cot2, masked.at[2 * rows : 3 * rows, :]),
        move(cot3, masked.at[3 * rows :, :]),
    ]
    forward(
        steps, blocks, patches[1:], weight, depth, gain, work, mask, (feat, normed, slope, rstd)
    )
    for copy in coming:
        copy.wait()
    fine = jnp.broadcast_to(gain[...], (TILE, gain.shape[1]))
    coarse = fine.astype(jnp.bfloat16)
    small = (fine - coarse.astype(jnp.float32)).astype(jnp.bfloat16)
    pulled = (dot(coarse, w_in[...], 1, 0) + dot(small, w_in[...], 1, 0))[:1, :]
    share = 1.0 / gain.shape[1]
    for k in range(4):
        at = slice(k * rows, (k + 1) * rows)
        tail = slice((k - 1) * rows, k * rows)
        counts = patches[k][rows:, :LANES].astype(jnp.float32)[:, :1]
        keep = jnp.concatenate([counts > t for t in range(steps)], axis=0)
        kept = jnp.where(keep, masked[at, :], jnp.zeros((), jnp.bfloat16))
        masked[at, :] = kept
        pre = dot(normed0[...] if k == 0 else normed[tail, :], w_in[...], 1, 0)
        back = dot(kept, w_out[...], 1, 1)
        sigma = sigmoid(pre)
        swish = pre * sigma
        hidden[at, :] = swish.astype(jnp.bfloat16)
        grown = 0.5 * back * (sigma + swish * (1.0 - sigma))
        pre_grad[at, :] = grown.astype(jnp.bfloat16)
        grown = grown * (rstd0[:, :1] if k == 0 else rstd[tail, :1])
        scaled[at, :] = grown.astype(jnp.bfloat16)
        for i, other in enumerate((pulled, pre)):
            mean = jnp.sum(grown * other, axis=-1, keepdims=True) * share
            means[i, at, :] = jnp.broadcast_to(mean, (rows, LANES)).astype(jnp.bfloat16)
    leaving = []
    for k in (2, 3, 1, 0):
        cols = columns_of(me ^ k, high)
        left = jnp.concatenate([normed0[:, cols], normed[:, cols]], axis=0)
        held[k] = dot(left, pre_grad[...], 0, 0).astype(jnp.bfloat16)
        leaving.append(move(held.at[k], grads[k]))
    for copy in leaving:
        copy.wait()


def backward_kernel(steps, blocks, *refs):
    gain, scaled, w_in, masked, means, normed0, slope0, feat0, normed, slope, feat = refs[0:11]
    taps_out, grad = refs[11:13]
    rows = steps * blocks
    for k in range(4):
        at = slice(k * rows, (k + 1) * rows)
        pulled = dot(scaled[at, :], w_in[...], 1, 1) * gain[...]
        if k == 0:
            pulled = pulled + masked[at, :].astype(jnp.float32)
        grad[at, :] = pulled.astype(jnp.bfloat16)
    taps = 2 * steps - 1

    def column(c, _):
        cols = pl.ds(pl.multiple_of(c * LANES, LANES), LANES)

        inverse = jnp.broadcast_to(1.0 / gain[:, cols], (blocks, LANES)).astype(jnp.bfloat16)

        def add(k, totals, held, near_normed, near_slope, near_feat):
            def spots(group):
                return [
                    pl.ds(pl.multiple_of(group * rows + t * blocks, TILE), blocks)
                    for t in range(steps)
                ]

            left = [
                near_slope[here, cols]
                * (
                    grad[spot, cols]
                    - means[0, spot, :]
                    - near_normed[here, cols] * inverse * means[1, spot, :]
                )
                for spot, here in zip(spots(k), spots(held))
            ]
            right = [near_feat[here, cols] for here in spots(held)]
            new = []
            for tap in range(taps):
                shift = tap - (steps - 1)
                terms = [
                    (left[t], right[t + shift]) for t in range(steps) if 0 <= t + shift < steps
                ]
                part = tree(terms, 0, len(terms)).astype(jnp.float32)
                for half in range(0, blocks, HALF):
                    piece = part[half : half + HALF, :]
                    total = piece if half == 0 else total + piece
                new.append(totals[tap] + total)
            return tuple(new)

        zero = jnp.zeros((HALF, LANES), jnp.float32)
        totals = add(0, (zero,) * taps, 0, normed0, slope0, feat0)
        totals = lax.fori_loop(
            1, 4, lambda k, totals: add(k, totals, k - 1, normed, slope, feat), totals
        )
        for tap in range(taps):
            taps_out[tap, :, cols] = jnp.sum(totals[tap], axis=0, keepdims=True)
        taps_out[taps, :, cols] = jnp.zeros((1, LANES), jnp.float32)
        return 0

    lax.fori_loop(0, gain.shape[1] // LANES, column, 0)


def out_kernel(hidden, masked, out_ref, turned):
    turned[...] = hidden[...].T
    width = out_ref.shape[1]
    for c in range(0, width, 256):
        out_ref[:, c : c + 256] = (0.5 * dot(turned[...], masked[:, c : c + 256], 1, 0)).astype(
            jnp.bfloat16
        )


def join_kernel(width, *refs):
    pieces, out_ref, held, sems = refs[0:4], refs[4], refs[5], refs[6]
    me = lax.axis_index("fsdp")
    coming = [
        pltpu.make_async_copy(piece, held.at[k], sems.at[0, k]) for k, piece in enumerate(pieces)
    ]
    leaving = [
        pltpu.make_async_copy(held.at[k], out_ref.at[:, columns_of(me ^ k, width)], sems.at[1, k])
        for k in range(4)
    ]
    for copy in coming:
        copy.start()
    for first, second in zip(coming, leaving):
        first.wait()
        second.start()
    for copy in leaving:
        copy.wait()


def on_device(
    frames,
    occupied_slot_counts,
    block_frame_rows,
    order,
    cotangent,
    sub_weight,
    depth_kernel,
    norm_gain,
    w_in,
    w_out,
):
    n = lax.axis_size("dp")
    home = frames.shape[2]
    cap = (home + n - 1) // n
    split = home % n == 0
    blocks, steps, width = cotangent.shape[2:]
    rows = blocks * steps
    deep, hidden_width = w_in.shape
    wide = hidden_width // 4
    bf16, f32 = jnp.bfloat16, jnp.float32
    dma = pltpu.SemaphoreType.DMA

    info = jnp.concatenate([occupied_slot_counts[0], block_frame_rows[0, 0]])
    infos = lax.all_to_all(
        jnp.broadcast_to(info[None], (n, home + 1)), "dp", split_axis=0, concat_axis=0, tiled=True
    )

    weight = lax.all_gather(sub_weight, "fsdp", axis=0, tiled=True)
    w_far = pltpu.with_memory_space_constraint(w_in, pltpu.HBM)
    w2, w3 = pl.pallas_call(
        functools.partial(cut_kernel, wide),
        out_shape=(sds((deep // 2, wide), bf16),) * 2,
        in_specs=[ANY],
        out_specs=(ANY,) * 2,
        scratch_shapes=[pltpu.VMEM((2, deep // 2, wide), bf16), dma((2, 2))],
        compiler_params=params(),
        cost_estimate=cost(1),
    )(w_far)
    w2, w3 = across(w2, 2), across(w3, 3)

    block_shape = frames.shape[3:]
    held = frames[0, 0].reshape((cap, n) + block_shape) if split else frames[0, 0]
    packed = pl.pallas_call(
        functools.partial(pack_kernel, n, split),
        out_shape=sds((n, cap) + block_shape, bf16),
        in_specs=[SMEM, SMEM, ANY],
        out_specs=ANY,
        scratch_shapes=[
            pltpu.VMEM((n if split else home, cap) + block_shape, bf16),
            dma((2 * (n if split else home),)),
        ],
        compiler_params=params(),
        cost_estimate=cost(2),
    )(order, infos, held)
    gain = norm_gain.reshape(1, width)
    packed, w2, w3, gain, cot = lax.optimization_barrier(
        (packed, w2, w3, gain, cotangent[0, 0])
    )
    got = lax.all_to_all(packed, "dp", split_axis=0, concat_axis=0, tiled=True)
    cot0, pair = pl.pallas_call(
        functools.partial(prepare_kernel, blocks, steps, wide),
        out_shape=(sds((rows, width), bf16), sds((rows + deep // 2, width), bf16)),
        in_specs=[VMEM, ANY],
        out_specs=(VMEM,) * 2,
        scratch_shapes=[pltpu.VMEM((rows * width // LANES, LANES), f32), dma((2,))],
        compiler_params=params(),
        cost_estimate=cost(2),
    )(cot, w_far)
    cot2, pair = across(cot0, 2), across(pair, 1)
    w2b, w3b = across_dp(w2, 1), across_dp(w3, 1)
    got, w2b = lax.optimization_barrier((got, w2b))
    patches0 = pl.pallas_call(
        functools.partial(unpack_kernel, n, cap, blocks, steps),
        out_shape=sds((rows + blocks, block_shape[0] // steps * LANES), bf16),
        in_specs=[SMEM, SMEM, ANY],
        out_specs=VMEM,
        scratch_shapes=[
            pltpu.VMEM((blocks,) + block_shape, bf16),
            pltpu.VMEM((blocks * block_shape[0], LANES), f32),
            dma((blocks,)),
        ],
        compiler_params=params(),
        cost_estimate=cost(2),
    )(order, infos, got.reshape((n * cap,) + block_shape))
    patches = [patches0, across(patches0, 1), across(patches0, 2)]

    def kept(count):
        return (
            pltpu.VMEM((count * rows, width), bf16),
            pltpu.VMEM((count * rows, width), bf16),
            pltpu.VMEM((count * rows, width), bf16),
            pltpu.VMEM((count * rows, LANES), f32),
        )

    feat0, normed0, slope0, rstd0 = pl.pallas_call(
        functools.partial(own_kernel, steps, blocks),
        out_shape=kept(1),
        in_specs=[VMEM] * 4,
        out_specs=(VMEM,) * 4,
        scratch_shapes=[pltpu.VMEM((rows, width), f32), pltpu.VMEM((rows, LANES), f32)],
        compiler_params=params(),
        cost_estimate=cost(4),
    )(*near(patches0), weight, depth_kernel, gain)
    feat0, cot_relay, patch_relay, w3b = lax.optimization_barrier(
        (feat0, cot2, patches[2], w3b)
    )
    cot3 = across(cot_relay, 1)
    patches.append(across(patch_relay, 1))
    (
        g0, g1, g2, g3, scaled, hidden, masked, w_slice, feat, normed, slope, means
    ) = pl.pallas_call(
        functools.partial(middle_kernel, steps, blocks),
        out_shape=(
            *[sds((deep, wide), bf16)] * 4,
            pltpu.VMEM((4 * rows, wide), bf16),
            pltpu.VMEM((4 * rows, wide), bf16),
            pltpu.VMEM((4 * rows, width), bf16),
            pltpu.VMEM((width, wide), bf16),
            *kept(3)[:3],
            pltpu.VMEM((2, 4 * rows, LANES), bf16),
        ),
        in_specs=[VMEM] * 9 + [ANY] * 10,
        out_specs=(ANY,) * 4 + (VMEM,) * 8,
        scratch_shapes=[
            pltpu.VMEM((3 * rows, width), f32),
            pltpu.VMEM((3 * rows, LANES), f32),
            pltpu.VMEM((3 * rows, LANES), f32),
            pltpu.VMEM((4 * rows, wide), bf16),
            pltpu.VMEM((wide, width), bf16),
            pltpu.VMEM((4, deep, wide), bf16),
            dma((16,)),
        ],
        compiler_params=params(28),
        cost_estimate=cost(20),
    )(
        *near(*patches), weight, depth_kernel, gain, *near(rstd0, normed0),
        cot0, pair, cot2, cot3, w_far, w2, w3, w2b, w3b, w_out,
    )
    g1, g2, g3 = across(g1, 1), across(g2, 2), across(g3, 3)

    taps = pl.pallas_call(
        functools.partial(backward_kernel, steps, blocks),
        out_shape=sds((2 * steps, 1, width), f32),
        in_specs=[VMEM] * 11,
        out_specs=VMEM,
        scratch_shapes=[pltpu.VMEM((4 * rows, width), bf16)],
        compiler_params=params(),
        cost_estimate=cost(13),
    )(
        *near(
            gain, scaled, w_slice, masked, means, normed0, slope0, feat0, normed, slope, feat
        )
    )
    taps, g2, hidden = lax.optimization_barrier((taps, g2, hidden))

    every = ("dp", "fsdp")
    devices = n * lax.axis_size("fsdp")
    shares = lax.all_to_all(
        taps.reshape(devices, 1, -1), every, split_axis=0, concat_axis=0, tiled=True
    )
    share = jnp.sum(shares, axis=0, keepdims=True) / rows
    grad_out = pl.pallas_call(
        out_kernel,
        out_shape=sds((wide, width), bf16),
        in_specs=[VMEM] * 2,
        out_specs=VMEM,
        scratch_shapes=[pltpu.VMEM((wide, 4 * rows), bf16)],
        compiler_params=params(),
        cost_estimate=cost(4),
    )(*near(hidden, masked))
    share, grad_out = lax.optimization_barrier((share, grad_out))
    whole = lax.all_to_all(
        jnp.broadcast_to(share, shares.shape), every, split_axis=0, concat_axis=0, tiled=True
    )
    kernel_grad = whole.reshape(2 * steps, width)[: depth_kernel.shape[0]]

    grad_in = pl.pallas_call(
        functools.partial(join_kernel, wide),
        out_shape=sds((deep, hidden_width), bf16),
        in_specs=[ANY] * 4,
        out_specs=ANY,
        scratch_shapes=[pltpu.VMEM((4, deep, wide), bf16), dma((2, 4))],
        compiler_params=params(),
        cost_estimate=cost(2),
    )(g0, g1, g2, g3)
    return (grad_in[None], grad_out[None], kernel_grad)


def solution(mesh):
    placed = (
        P("dp", "fsdp", None, None, None),
        P("fsdp", "dp"),
        P("dp", "fsdp", None),
        P("fsdp", None),
        P("dp", "fsdp", None, None, None),
        P("fsdp", None),
        P(),
        P(),
        P("fsdp", None),
        P("fsdp", None),
    )
    return jax.shard_map(
        on_device,
        mesh=mesh,
        in_specs=placed,
        out_specs=(P("dp", "fsdp", None), P("dp", "fsdp", None), P()),
        check_vma=False,
    )
```

```python
import functools

import jax
import jax.numpy as jnp
from jax import lax
from jax.experimental import pallas as pl
from jax.experimental.pallas import tpu as pltpu
from jax.sharding import PartitionSpec as P

LANES = 128
HALF = 8
TILE = 16
EPSILON = 1e-05

VMEM = pl.BlockSpec(memory_space=pltpu.VMEM)
SMEM = pl.BlockSpec(memory_space=pltpu.SMEM)
ANY = pl.BlockSpec(memory_space=pl.ANY)


def params(mebibytes=16):
    return pltpu.CompilerParams(vmem_limit_bytes=mebibytes * 1024 * 1024)


def cost(microseconds):
    return pl.CostEstimate(
        flops=0, transcendentals=0, bytes_accessed=int(microseconds * 3.6e6)
    )


def near(*arrays):
    return [pltpu.with_memory_space_constraint(array, pltpu.VMEM) for array in arrays]


def far(*arrays):
    return [pltpu.with_memory_space_constraint(array, pltpu.HBM) for array in arrays]


def sds(shape, dtype):
    return jax.ShapeDtypeStruct(shape, dtype)


def sigmoid(values):
    return 0.5 * jnp.tanh(0.5 * values) + 0.5


def dot(left, right, left_dim, right_dim):
    return lax.dot_general(
        left, right, (((left_dim,), (right_dim,)), ((), ())), preferred_element_type=jnp.float32
    )


def across(value, k):
    n = lax.axis_size("fsdp")
    return lax.ppermute(value, "fsdp", [(i, i ^ k) for i in range(n)])


def across_dp(value, k):
    n = lax.axis_size("dp")
    return lax.ppermute(value, "dp", [(i, i ^ k) for i in range(n)])


def columns_of(index, width):
    return pl.ds(pl.multiple_of(index * width, LANES), width)


def prepare_kernel(
    blocks, steps, width, cot_ref, w_ref, cot_out, pair_out, cot, pair, scratch, sems
):
    rows = blocks * steps
    half = w_ref.shape[0] // 2
    cols = columns_of(lax.axis_index("fsdp") ^ 1, width)
    copies = [
        pltpu.make_async_copy(
            w_ref.at[i * half : (i + 1) * half, cols],
            pair.at[rows:, i * width : (i + 1) * width],
            sems.at[i],
        )
        for i in range(2)
    ]
    for copy in copies:
        copy.start()
    for c in range(cot_ref.shape[-1] // LANES):
        cols = slice(c * LANES, (c + 1) * LANES)
        scratch[c * rows : (c + 1) * rows, :] = (
            cot_ref[:, :, cols].reshape(rows, LANES).astype(jnp.float32)
        )
        for t in range(steps):
            at = slice(t * blocks, (t + 1) * blocks)
            turned = scratch[pl.ds(c * rows + t, blocks, stride=steps), :].astype(jnp.bfloat16)
            cot[at, cols] = turned
            pair[at, cols] = turned
    for copy in copies:
        copy.wait()
    leaving = [
        pltpu.make_async_copy(cot, cot_out, sems.at[3]),
        pltpu.make_async_copy(pair, pair_out, sems.at[4]),
    ]
    for copy in leaving:
        copy.start()
    for copy in leaving:
        copy.wait()


def pack_kernel(n, split, order_ref, info_ref, frames_ref, out_ref, held, sems):
    me = lax.axis_index("dp")
    classes = held.shape[0]
    coming = []
    for c in range(classes):
        source = frames_ref.at[:, c] if split else frames_ref.at[pl.ds(c, 1)]
        coming.append(pltpu.make_async_copy(source, held.at[c], sems.at[c]))
        coming[c].start()
    start = jnp.int32(0)
    for i in range(n - 1):
        start = start + jnp.where(i < me, info_ref[i, 0], 0)
    leaving = []
    for c in range(classes):
        target = order_ref[0, lax.rem(start + c, n)]
        leaving.append(
            pltpu.make_async_copy(held.at[c], out_ref.at[target], sems.at[classes + c])
        )
        coming[c].wait()
        leaving[c].start()
    for copy in leaving:
        copy.wait()


def unpack_kernel(
    n, cap, blocks, steps, order_ref, info_ref, got_ref, out_ref, landed, scratch, sems
):
    me = lax.axis_index("dp")
    residue = jnp.int32(0)
    for r in range(n):
        residue = residue + jnp.where(order_ref[0, r] == me, r, 0)
    starts, so_far = [], jnp.int32(0)
    for i in range(n):
        starts.append(so_far)
        so_far = so_far + info_ref[i, 0]
    length = got_ref.shape[1]
    copies, rows = [], []
    for m in range(blocks):
        g = residue + m * n
        source, start = jnp.int32(0), jnp.int32(0)
        for i in range(1, n):
            later = starts[i] <= g
            source = jnp.where(later, i, source)
            start = jnp.where(later, starts[i], start)
        h = g - start
        copy = pltpu.make_async_copy(
            got_ref.at[source * cap + lax.div(h, n)], landed.at[m], sems.at[m]
        )
        copy.start()
        copies.append(copy)
        rows.append(info_ref[source, 1 + h])
    height = lax.broadcasted_iota(jnp.int32, (blocks, out_ref.shape[1]), 0)
    counts = jnp.zeros((blocks, out_ref.shape[1]), jnp.int32)
    for m in range(blocks):
        counts = jnp.where(height == m, rows[m], counts)
    out_ref[steps * blocks :, :] = counts.astype(jnp.float32).astype(jnp.bfloat16)
    for m in range(blocks):
        copies[m].wait()
        scratch[m * length : (m + 1) * length, :] = landed[m].astype(jnp.float32)
    group = length // steps
    for t in range(steps):
        for j in range(group):
            out_ref[t * blocks : (t + 1) * blocks, j * LANES : (j + 1) * LANES] = scratch[
                pl.ds(group * t + j, blocks, stride=length), :
            ].astype(jnp.bfloat16)


def cut_kernel(width, w_ref, p2, p3, held, sems):
    me = lax.axis_index("fsdp")
    half = p2.shape[0]
    part = pl.ds(pl.multiple_of(lax.rem(lax.axis_index("dp"), 2) * half, TILE), half)
    coming = [
        pltpu.make_async_copy(w_ref.at[part, columns_of(me ^ k, width)], held.at[i], sems.at[0, i])
        for i, k in enumerate((2, 3))
    ]
    leaving = [
        pltpu.make_async_copy(held.at[i], target, sems.at[1, i])
        for i, target in enumerate((p2, p3))
    ]
    for copy in coming:
        copy.start()
    for first, second in zip(coming, leaving):
        first.wait()
        second.start()
    for copy in leaving:
        copy.wait()


def tree(terms, low, high):
    if high - low == 1:
        left, right = terms[low]
        return left * right
    middle = (low + high) // 2
    return tree(terms, low, middle) + tree(terms, middle, high)


def forward(steps, blocks, patches, sub_ref, scales, work, mask, outs):
    rows = steps * blocks
    feat_ref, normed_ref, slope_ref, rstd_ref = outs
    width, taps = scales.shape[1], scales.shape[0] - 1
    span = (taps - 1) // 2
    groups = range(len(patches))
    for g in groups:
        work[g * rows : (g + 1) * rows, :] = dot(patches[g][:rows, :], sub_ref[...], 1, 0)
        counts = patches[g][rows:, :LANES].astype(jnp.float32)
        for t in range(steps):
            spot = g * rows + t * blocks
            mask[spot : spot + blocks, :] = jnp.where(counts > t, 1.0, 0.0)

    def column(c, _):
        cols = pl.ds(pl.multiple_of(c * LANES, LANES), LANES)
        weights = [
            jnp.broadcast_to(scales[k : k + 1, cols], (blocks, LANES)).astype(jnp.bfloat16)
            for k in range(taps)
        ]
        for g in groups:
            spots = [
                slice(g * rows + t * blocks, g * rows + (t + 1) * blocks) for t in range(steps)
            ]
            values = []
            for t in range(steps):
                rounded = (work[spots[t], cols] * mask[spots[t], :]).astype(jnp.bfloat16)
                feat_ref[spots[t], cols] = rounded
                values.append(rounded)
            for t in range(steps):
                terms = [
                    (values[s], weights[s - t + span])
                    for s in range(steps)
                    if 0 <= s - t + span < taps
                ]
                conv = tree(terms, 0, len(terms)).astype(jnp.float32)
                keep = mask[spots[t], :]
                sigma = sigmoid(conv)
                swish = conv * sigma
                slope_ref[spots[t], cols] = (keep * (sigma + swish * (1.0 - sigma))).astype(
                    jnp.bfloat16
                )
                work[spots[t], cols] = values[t].astype(jnp.float32) + keep * swish
        return 0

    lax.fori_loop(0, width // LANES, column, 0)

    def norm(i, _):
        at = pl.ds(pl.multiple_of(i * 32, 32), 32)
        values = work[at, :]
        centred = values - jnp.mean(values, axis=-1, keepdims=True)
        rstd = lax.rsqrt(jnp.mean(centred * centred, axis=-1, keepdims=True) + EPSILON)
        normed_ref[at, :] = (centred * rstd * scales[taps:, :]).astype(jnp.bfloat16)
        rstd_ref[at, :] = jnp.broadcast_to(rstd, (32, LANES))
        return 0

    lax.fori_loop(0, len(patches) * rows // 32, norm, 0)


def next_kernel(steps, blocks, patches, weight, scales, o0, o1, o2, o3, work, mask):
    forward(steps, blocks, [patches], weight, scales, work, mask, (o0, o1, o2, o3))


def first_kernel(
    steps, blocks, patches, sub0, sub1, sub2, sub3, depth, gain,
    o0, o1, o2, o3, weight, scales, work, mask, sems,
):
    me = lax.axis_index("fsdp")
    deep = sub0.shape[0]
    copies = [
        pltpu.make_async_copy(
            piece, weight.at[pl.ds(pl.multiple_of((me ^ k) * deep, TILE), deep), :], sems.at[k]
        )
        for k, piece in enumerate((sub0, sub1, sub2, sub3))
    ]
    for copy in copies:
        copy.start()
    scales[: depth.shape[0], :] = depth[...]
    scales[depth.shape[0] :, :] = gain[...]
    for copy in copies:
        copy.wait()
    forward(steps, blocks, [patches], weight, scales, work, mask, (o0, o1, o2, o3))


def middle_kernel(steps, blocks, *refs):
    patches, normed, rstds, gain = refs[0:4], refs[4:8], refs[8:12], refs[12]
    cot0, pair, cot2, cot3, w_own, w2, w3, w2b, w3b, w_out_in = refs[13:23]
    grads, scaled, hidden, masked, w_in, means = refs[23:27], *refs[27:32]
    pre_grad, w_out, held, sems = refs[32:36]
    me = lax.axis_index("fsdp")
    parity = lax.rem(lax.axis_index("dp"), 2)
    rows = steps * blocks
    half, wide = w2.shape
    high = 2 * half
    used = iter(range(sems.shape[0]))

    def move(source, place):
        copy = pltpu.make_async_copy(source, place, sems.at[next(used)])
        copy.start()
        return copy

    def rows_of(index, part=0, size=high):
        return pl.ds(pl.multiple_of(index * high + part * half, TILE), size)

    coming = [
        move(w_own.at[:, columns_of(me, wide)], w_in.at[rows_of(me), :]),
        move(pair.at[rows:, :wide], w_in.at[rows_of(me ^ 1, 0, half), :]),
        move(pair.at[rows:, wide:], w_in.at[rows_of(me ^ 1, 1, half), :]),
        move(w2, w_in.at[rows_of(me ^ 2, parity, half), :]),
        move(w3, w_in.at[rows_of(me ^ 3, parity, half), :]),
        move(w2b, w_in.at[rows_of(me ^ 2, 1 - parity, half), :]),
        move(w3b, w_in.at[rows_of(me ^ 3, 1 - parity, half), :]),
    ]
    later = [
        move(w_out_in, w_out),
        move(cot0, masked.at[:rows, :]),
        move(pair.at[:rows, :], masked.at[rows : 2 * rows, :]),
        move(cot2, masked.at[2 * rows : 3 * rows, :]),
        move(cot3, masked.at[3 * rows :, :]),
    ]
    for copy in coming:
        copy.wait()
    fine = jnp.broadcast_to(gain[...], (TILE, gain.shape[1]))
    coarse = fine.astype(jnp.bfloat16)
    small = (fine - coarse.astype(jnp.float32)).astype(jnp.bfloat16)
    pulled = (dot(coarse, w_in[...], 1, 0) + dot(small, w_in[...], 1, 0))[:1, :]
    share = 1.0 / gain.shape[1]
    for k in range(4):
        at = slice(k * rows, (k + 1) * rows)
        counts = patches[k][rows:, :LANES].astype(jnp.float32)[:, :1]
        keep = jnp.concatenate([counts > t for t in range(steps)], axis=0)
        pre = dot(normed[k][...], w_in[...], 1, 0)
        for copy in later[:2] if k == 0 else later[k + 1 : k + 2]:
            copy.wait()
        kept = jnp.where(keep, masked[at, :], jnp.zeros((), jnp.bfloat16))
        masked[at, :] = kept
        back = dot(kept, w_out[...], 1, 1)
        sigma = sigmoid(pre)
        swish = pre * sigma
        hidden[at, :] = swish.astype(jnp.bfloat16)
        grown = 0.5 * back * (sigma + swish * (1.0 - sigma))
        pre_grad[at, :] = grown.astype(jnp.bfloat16)
        grown = grown * rstds[k][:, :1]
        scaled[at, :] = grown.astype(jnp.bfloat16)
        for i, other in enumerate((pulled, pre)):
            mean = jnp.sum(grown * other, axis=-1, keepdims=True) * share
            means[i, at, :] = jnp.broadcast_to(mean, (rows, LANES)).astype(jnp.bfloat16)
    leaving = []
    for k in (2, 3, 1, 0):
        cols = columns_of(me ^ k, high)
        left = jnp.concatenate([normed[j][:, cols] for j in range(4)], axis=0)
        held[k] = dot(left, pre_grad[...], 0, 0).astype(jnp.bfloat16)
        leaving.append(move(held.at[k], grads[k]))
    for copy in leaving:
        copy.wait()


def backward_kernel(steps, blocks, *refs):
    gain, scaled, w_in, masked, means = refs[0:5]
    normed, slope, feat = refs[5:9], refs[9:13], refs[13:17]
    taps_out, grad, totals = refs[17:20]
    rows = steps * blocks
    for k in range(4):
        at = slice(k * rows, (k + 1) * rows)
        pulled = dot(scaled[at, :], w_in[...], 1, 1) * gain[...]
        if k == 0:
            pulled = pulled + masked[at, :].astype(jnp.float32)
        grad[at, :] = pulled.astype(jnp.bfloat16)
    taps = 2 * steps - 1

    def column(k, c):
        cols = pl.ds(pl.multiple_of(c * LANES, LANES), LANES)
        inverse = jnp.broadcast_to(1.0 / gain[:, cols], (blocks, LANES)).astype(jnp.bfloat16)
        here = [slice(t * blocks, (t + 1) * blocks) for t in range(steps)]
        spots = [slice(k * rows + t * blocks, k * rows + (t + 1) * blocks) for t in range(steps)]
        left = [
            slope[k][at, cols]
            * (
                grad[spot, cols]
                - means[0, spot, :]
                - normed[k][at, cols] * inverse * means[1, spot, :]
            )
            for spot, at in zip(spots, here)
        ]
        right = [feat[k][at, cols] for at in here]
        for tap in range(taps):
            shift = tap - (steps - 1)
            terms = [(left[t], right[t + shift]) for t in range(steps) if 0 <= t + shift < steps]
            part = tree(terms, 0, len(terms))
            if k > 0:
                part = part + totals[tap, :, cols]
            if k < 3:
                totals[tap, :, cols] = part
            else:
                taps_out[tap, :, cols] = jnp.sum(part.astype(jnp.float32), axis=0, keepdims=True)
        if k == 3:
            taps_out[taps, :, cols] = jnp.zeros((1, LANES), jnp.float32)

    def step(c, _, k):
        column(k, c)
        return 0

    for k in range(4):
        lax.fori_loop(0, gain.shape[1] // LANES, functools.partial(step, k=k), 0)


def out_kernel(hidden, masked, out_ref, turned):
    turned[...] = hidden[...].T
    width = out_ref.shape[1]
    for c in range(0, width, 256):
        out_ref[:, c : c + 256] = (0.5 * dot(turned[...], masked[:, c : c + 256], 1, 0)).astype(
            jnp.bfloat16
        )


def join_kernel(width, *refs):
    pieces, out_ref, held, sems = refs[0:4], refs[4], refs[5], refs[6]
    me = lax.axis_index("fsdp")
    coming = [
        pltpu.make_async_copy(piece, held.at[k], sems.at[0, k]) for k, piece in enumerate(pieces)
    ]
    leaving = [
        pltpu.make_async_copy(held.at[k], out_ref.at[:, columns_of(me ^ k, width)], sems.at[1, k])
        for k in range(4)
    ]
    for copy in coming:
        copy.start()
    for first, second in zip(coming, leaving):
        first.wait()
        second.start()
    for copy in leaving:
        copy.wait()


def on_device(
    frames,
    occupied_slot_counts,
    block_frame_rows,
    order,
    cotangent,
    sub_weight,
    depth_kernel,
    norm_gain,
    w_in,
    w_out,
):
    n = lax.axis_size("dp")
    home = frames.shape[2]
    cap = (home + n - 1) // n
    split = home % n == 0
    blocks, steps, width = cotangent.shape[2:]
    rows = blocks * steps
    deep, hidden_width = w_in.shape
    wide = hidden_width // 4
    bf16, f32 = jnp.bfloat16, jnp.float32
    dma = pltpu.SemaphoreType.DMA

    info = jnp.concatenate([occupied_slot_counts[0], block_frame_rows[0, 0]])
    infos = lax.all_to_all(
        jnp.broadcast_to(info[None], (n, home + 1)), "dp", split_axis=0, concat_axis=0, tiled=True
    )

    w_far, w_out, sub_weight, depth_kernel = far(w_in, w_out, sub_weight, depth_kernel)
    sub1, sub2 = across(sub_weight, 1), across(sub_weight, 2)

    block_shape = frames.shape[3:]
    held = frames[0, 0].reshape((cap, n) + block_shape) if split else frames[0, 0]
    packed = pl.pallas_call(
        functools.partial(pack_kernel, n, split),
        out_shape=sds((n, cap) + block_shape, bf16),
        in_specs=[SMEM, SMEM, ANY],
        out_specs=ANY,
        scratch_shapes=[
            pltpu.VMEM((n if split else home, cap) + block_shape, bf16),
            dma((2 * (n if split else home),)),
        ],
        compiler_params=params(),
        cost_estimate=cost(2),
    )(order, infos, held)
    gain = norm_gain.reshape(1, width)
    packed, sub1, sub2, gain, cot, w_late = lax.optimization_barrier(
        (packed, sub1, sub2, gain, cotangent[0, 0], w_far)
    )
    got = lax.all_to_all(packed, "dp", split_axis=0, concat_axis=0, tiled=True)
    w_late = far(w_late)[0]
    w2, w3 = pl.pallas_call(
        functools.partial(cut_kernel, wide),
        out_shape=(pltpu.HBM((deep // 2, wide), bf16),) * 2,
        in_specs=[ANY],
        out_specs=(ANY,) * 2,
        scratch_shapes=[pltpu.VMEM((2, deep // 2, wide), bf16), dma((2, 2))],
        compiler_params=params(),
        cost_estimate=cost(1),
    )(w_late)
    w2, w3 = across(w2, 2), across(w3, 3)
    sub_rows = sub_weight.shape[0]
    cot0, pair = pl.pallas_call(
        functools.partial(prepare_kernel, blocks, steps, wide),
        out_shape=(
            pltpu.HBM((rows, width), bf16),
            pltpu.HBM((rows + deep // 2, width), bf16),
        ),
        in_specs=[VMEM, ANY],
        out_specs=(ANY,) * 2,
        scratch_shapes=[
            pltpu.VMEM((rows, width), bf16),
            pltpu.VMEM((rows + deep // 2, width), bf16),
            pltpu.VMEM((rows * width // LANES, LANES), f32),
            dma((5,)),
        ],
        compiler_params=params(),
        cost_estimate=cost(2),
    )(cot, w_late)
    sub3 = across(sub2, 1)
    cot2, pair = across(cot0, 2), across(pair, 1)
    got, sub3, w2, w3 = lax.optimization_barrier((got, sub3, w2, w3))
    w2b, w3b = across_dp(w2, 1), across_dp(w3, 1)
    patches0 = pl.pallas_call(
        functools.partial(unpack_kernel, n, cap, blocks, steps),
        out_shape=sds((rows + blocks, block_shape[0] // steps * LANES), bf16),
        in_specs=[SMEM, SMEM, ANY],
        out_specs=VMEM,
        scratch_shapes=[
            pltpu.VMEM((blocks,) + block_shape, bf16),
            pltpu.VMEM((blocks * block_shape[0], LANES), f32),
            dma((blocks,)),
        ],
        compiler_params=params(),
        cost_estimate=cost(2),
    )(order, infos, got.reshape((n * cap,) + block_shape))
    patches = [patches0, across(patches0, 1), across(patches0, 2)]

    kept = (
        pltpu.VMEM((rows, width), bf16),
        pltpu.VMEM((rows, width), bf16),
        pltpu.VMEM((rows, width), bf16),
        pltpu.VMEM((rows, LANES), f32),
    )
    work = [pltpu.VMEM((rows, width), f32), pltpu.VMEM((rows, LANES), f32)]
    *first, weight, scales = pl.pallas_call(
        functools.partial(first_kernel, steps, blocks),
        out_shape=(
            *kept,
            pltpu.VMEM((4 * sub_rows, width), bf16),
            pltpu.VMEM((2 * steps, width), f32),
        ),
        in_specs=[VMEM] + [ANY] * 4 + [VMEM] * 2,
        out_specs=(VMEM,) * 6,
        scratch_shapes=[*work, dma((4,))],
        compiler_params=params(),
        cost_estimate=cost(4),
    )(*near(patches0), sub_weight, *far(sub1, sub2, sub3), depth_kernel, gain)
    first[0], cot_relay, patch_relay = lax.optimization_barrier((first[0], cot2, patches[2]))
    cot3 = across(cot_relay, 1)
    patches.append(across(patch_relay, 1))
    following = pl.pallas_call(
        functools.partial(next_kernel, steps, blocks),
        out_shape=kept,
        in_specs=[VMEM] * 3,
        out_specs=(VMEM,) * 4,
        scratch_shapes=work,
        compiler_params=params(),
        cost_estimate=cost(4),
    )
    groups = [first]
    for k in (1, 2, 3):
        groups.append(following(*near(patches[k], weight, scales)))
    feats, normeds, slopes, rstds = [near(*arrays) for arrays in zip(*groups)]
    g0, g1, g2, g3, scaled, hidden, masked, w_slice, means = pl.pallas_call(
        functools.partial(middle_kernel, steps, blocks),
        out_shape=(
            *[pltpu.HBM((deep, wide), bf16)] * 4,
            pltpu.VMEM((4 * rows, wide), bf16),
            pltpu.VMEM((4 * rows, wide), bf16),
            pltpu.VMEM((4 * rows, width), bf16),
            pltpu.VMEM((width, wide), bf16),
            pltpu.VMEM((2, 4 * rows, LANES), bf16),
        ),
        in_specs=[VMEM] * 13 + [ANY] * 10,
        out_specs=(ANY,) * 4 + (VMEM,) * 5,
        scratch_shapes=[
            pltpu.VMEM((4 * rows, wide), bf16),
            pltpu.VMEM((wide, width), bf16),
            pltpu.VMEM((4, deep, wide), bf16),
            dma((16,)),
        ],
        compiler_params=params(24),
        cost_estimate=cost(12),
    )(
        *patches, *normeds, *rstds, gain,
        *far(cot0, pair, cot2, cot3), w_far, *far(w2, w3, w2b, w3b), w_out,
    )
    g3, g2, g1 = across(g3, 3), across(g2, 2), across(g1, 1)

    taps = pl.pallas_call(
        functools.partial(backward_kernel, steps, blocks),
        out_shape=sds((2 * steps, 1, width), f32),
        in_specs=[VMEM] * 17,
        out_specs=VMEM,
        scratch_shapes=[
            pltpu.VMEM((4 * rows, width), bf16),
            pltpu.VMEM((2 * steps - 1, blocks, width), bf16),
        ],
        compiler_params=params(),
        cost_estimate=cost(13),
    )(gain, *near(scaled, w_slice, masked, means), *normeds, *slopes, *feats)
    taps, g2, hidden = lax.optimization_barrier((taps, g2, hidden))

    every = ("dp", "fsdp")
    devices = n * lax.axis_size("fsdp")
    shares = lax.all_to_all(
        taps.reshape(devices, 1, -1), every, split_axis=0, concat_axis=0, tiled=True
    )
    share = jnp.sum(shares, axis=0, keepdims=True) / rows
    grad_out = pl.pallas_call(
        out_kernel,
        out_shape=sds((wide, width), bf16),
        in_specs=[VMEM] * 2,
        out_specs=VMEM,
        scratch_shapes=[pltpu.VMEM((wide, 4 * rows), bf16)],
        compiler_params=params(),
        cost_estimate=cost(4),
    )(*near(hidden, masked))
    share, grad_out = lax.optimization_barrier((share, grad_out))
    whole = lax.all_to_all(
        jnp.broadcast_to(share, shares.shape), every, split_axis=0, concat_axis=0, tiled=True
    )
    kernel_grad = whole.reshape(2 * steps, width)[: depth_kernel.shape[0]]

    grad_in = pl.pallas_call(
        functools.partial(join_kernel, wide),
        out_shape=sds((deep, hidden_width), bf16),
        in_specs=[ANY] * 4,
        out_specs=ANY,
        scratch_shapes=[pltpu.VMEM((4, deep, wide), bf16), dma((2, 4))],
        compiler_params=params(),
        cost_estimate=cost(2),
    )(*far(g0, g1, g2, g3))
    return (grad_in[None], grad_out[None], kernel_grad)


def solution(mesh):
    placed = (
        P("dp", "fsdp", None, None, None),
        P("fsdp", "dp"),
        P("dp", "fsdp", None),
        P("fsdp", None),
        P("dp", "fsdp", None, None, None),
        P("fsdp", None),
        P(),
        P(),
        P("fsdp", None),
        P("fsdp", None),
    )
    return jax.shard_map(
        on_device,
        mesh=mesh,
        in_specs=placed,
        out_specs=(P("dp", "fsdp", None), P("dp", "fsdp", None), P()),
        check_vma=False,
    )
```

```python
import functools

import jax
import jax.numpy as jnp
from jax import lax
from jax.experimental import pallas as pl
from jax.experimental.pallas import tpu as pltpu
from jax.sharding import PartitionSpec as P

LANES = 128
HALF = 8
TILE = 16
EPSILON = 1e-05

VMEM = pl.BlockSpec(memory_space=pltpu.VMEM)
SMEM = pl.BlockSpec(memory_space=pltpu.SMEM)
ANY = pl.BlockSpec(memory_space=pl.ANY)


def params(mebibytes=16):
    return pltpu.CompilerParams(vmem_limit_bytes=mebibytes * 1024 * 1024)


def cost(microseconds):
    return pl.CostEstimate(
        flops=0, transcendentals=0, bytes_accessed=int(microseconds * 3.6e6)
    )


def near(*arrays):
    return [pltpu.with_memory_space_constraint(array, pltpu.VMEM) for array in arrays]


def far(*arrays):
    return [pltpu.with_memory_space_constraint(array, pltpu.HBM) for array in arrays]


def sds(shape, dtype):
    return jax.ShapeDtypeStruct(shape, dtype)


def sigmoid(values):
    return 0.5 * jnp.tanh(0.5 * values) + 0.5


def dot(left, right, left_dim, right_dim):
    return lax.dot_general(
        left, right, (((left_dim,), (right_dim,)), ((), ())), preferred_element_type=jnp.float32
    )


def across(value, k):
    n = lax.axis_size("fsdp")
    return lax.ppermute(value, "fsdp", [(i, i ^ k) for i in range(n)])


def across_dp(value, k):
    n = lax.axis_size("dp")
    return lax.ppermute(value, "dp", [(i, i ^ k) for i in range(n)])


def columns_of(index, width):
    return pl.ds(pl.multiple_of(index * width, LANES), width)


def prepare_kernel(
    blocks, steps, width, cot_ref, w_ref, cot_out, pair_out, cot, pair, scratch, sems
):
    rows = blocks * steps
    half = w_ref.shape[0] // 2
    cols = columns_of(lax.axis_index("fsdp") ^ 1, width)
    copies = [
        pltpu.make_async_copy(
            w_ref.at[i * half : (i + 1) * half, cols],
            pair.at[rows:, i * width : (i + 1) * width],
            sems.at[i],
        )
        for i in range(2)
    ]
    for copy in copies:
        copy.start()
    for c in range(cot_ref.shape[-1] // LANES):
        cols = slice(c * LANES, (c + 1) * LANES)
        scratch[c * rows : (c + 1) * rows, :] = (
            cot_ref[:, :, cols].reshape(rows, LANES).astype(jnp.float32)
        )
        for t in range(steps):
            at = slice(t * blocks, (t + 1) * blocks)
            turned = scratch[pl.ds(c * rows + t, blocks, stride=steps), :].astype(jnp.bfloat16)
            cot[at, cols] = turned
            pair[at, cols] = turned
    for copy in copies:
        copy.wait()
    leaving = [
        pltpu.make_async_copy(cot, cot_out, sems.at[3]),
        pltpu.make_async_copy(pair, pair_out, sems.at[4]),
    ]
    for copy in leaving:
        copy.start()
    for copy in leaving:
        copy.wait()


def pack_kernel(n, split, order_ref, info_ref, frames_ref, out_ref, held, sems):
    me = lax.axis_index("dp")
    classes = held.shape[0]
    coming = []
    for c in range(classes):
        source = frames_ref.at[:, c] if split else frames_ref.at[pl.ds(c, 1)]
        coming.append(pltpu.make_async_copy(source, held.at[c], sems.at[c]))
        coming[c].start()
    start = jnp.int32(0)
    for i in range(n - 1):
        start = start + jnp.where(i < me, info_ref[i, 0], 0)
    leaving = []
    for c in range(classes):
        target = order_ref[0, lax.rem(start + c, n)]
        leaving.append(
            pltpu.make_async_copy(held.at[c], out_ref.at[target], sems.at[classes + c])
        )
        coming[c].wait()
        leaving[c].start()
    for copy in leaving:
        copy.wait()


def unpack_kernel(
    n, cap, blocks, steps, order_ref, info_ref, got_ref, out_ref, landed, scratch, sems
):
    me = lax.axis_index("dp")
    residue = jnp.int32(0)
    for r in range(n):
        residue = residue + jnp.where(order_ref[0, r] == me, r, 0)
    starts, so_far = [], jnp.int32(0)
    for i in range(n):
        starts.append(so_far)
        so_far = so_far + info_ref[i, 0]
    length = got_ref.shape[1]
    copies, rows = [], []
    for m in range(blocks):
        g = residue + m * n
        source, start = jnp.int32(0), jnp.int32(0)
        for i in range(1, n):
            later = starts[i] <= g
            source = jnp.where(later, i, source)
            start = jnp.where(later, starts[i], start)
        h = g - start
        copy = pltpu.make_async_copy(
            got_ref.at[source * cap + lax.div(h, n)], landed.at[m], sems.at[m]
        )
        copy.start()
        copies.append(copy)
        rows.append(info_ref[source, 1 + h])
    height = lax.broadcasted_iota(jnp.int32, (blocks, out_ref.shape[1]), 0)
    counts = jnp.zeros((blocks, out_ref.shape[1]), jnp.int32)
    for m in range(blocks):
        counts = jnp.where(height == m, rows[m], counts)
    out_ref[steps * blocks :, :] = counts.astype(jnp.float32).astype(jnp.bfloat16)
    for m in range(blocks):
        copies[m].wait()
        scratch[m * length : (m + 1) * length, :] = landed[m].astype(jnp.float32)
    group = length // steps
    for t in range(steps):
        for j in range(group):
            out_ref[t * blocks : (t + 1) * blocks, j * LANES : (j + 1) * LANES] = scratch[
                pl.ds(group * t + j, blocks, stride=length), :
            ].astype(jnp.bfloat16)


def cut_kernel(width, w_ref, p2, p3, held, sems):
    me = lax.axis_index("fsdp")
    half = p2.shape[0]
    part = pl.ds(pl.multiple_of(lax.rem(lax.axis_index("dp"), 2) * half, TILE), half)
    coming = [
        pltpu.make_async_copy(w_ref.at[part, columns_of(me ^ k, width)], held.at[i], sems.at[0, i])
        for i, k in enumerate((2, 3))
    ]
    leaving = [
        pltpu.make_async_copy(held.at[i], target, sems.at[1, i])
        for i, target in enumerate((p2, p3))
    ]
    for copy in coming:
        copy.start()
    for first, second in zip(coming, leaving):
        first.wait()
        second.start()
    for copy in leaving:
        copy.wait()


def tree(terms, low, high):
    if high - low == 1:
        left, right = terms[low]
        return left * right
    middle = (low + high) // 2
    return tree(terms, low, middle) + tree(terms, middle, high)


def order_kernel(sub0, sub1, sub2, sub3, depth, gain, weight, scales, sems):
    me = lax.axis_index("fsdp")
    deep = sub0.shape[0]
    copies = [
        pltpu.make_async_copy(
            piece, weight.at[pl.ds(pl.multiple_of((me ^ k) * deep, TILE), deep), :], sems.at[k]
        )
        for k, piece in enumerate((sub0, sub1, sub2, sub3))
    ]
    for copy in copies:
        copy.start()
    scales[: depth.shape[0], :] = depth[...]
    scales[depth.shape[0] :, :] = gain[...]
    for copy in copies:
        copy.wait()


def forward_kernel(
    steps, blocks, patches, weight, scales, feat_ref, normed_ref, slope_ref, rstd_ref, mixed, mask
):
    rows = steps * blocks
    width, taps = scales.shape[1], scales.shape[0] - 1
    span = (taps - 1) // 2
    feat_ref[...] = dot(patches[:rows, :], weight[...], 1, 0).astype(jnp.bfloat16)
    counts = patches[rows:, :LANES].astype(jnp.float32)
    spots = [slice(t * blocks, (t + 1) * blocks) for t in range(steps)]
    for t in range(steps):
        mask[spots[t], :] = jnp.where(counts > t, 1.0, 0.0).astype(jnp.bfloat16)

    def column(c, _):
        cols = pl.ds(pl.multiple_of(c * LANES, LANES), LANES)
        weights = [
            jnp.broadcast_to(scales[k : k + 1, cols], (blocks, LANES)).astype(jnp.bfloat16)
            for k in range(taps)
        ]
        values = []
        for t in range(steps):
            values.append(feat_ref[spots[t], cols] * mask[spots[t], :])
            feat_ref[spots[t], cols] = values[t]
        for t in range(steps):
            terms = [
                (values[s], weights[s - t + span])
                for s in range(steps)
                if 0 <= s - t + span < taps
            ]
            conv = tree(terms, 0, len(terms))
            keep = mask[spots[t], :]
            sigma = sigmoid(conv)
            swish = conv * sigma
            slope_ref[spots[t], cols] = keep * (sigma + swish * (1.0 - sigma))
            mixed[spots[t], cols] = values[t] + keep * swish
        return 0

    lax.fori_loop(0, width // LANES, column, 0)

    def norm(i, _):
        at = pl.ds(pl.multiple_of(i * 32, 32), 32)
        values = mixed[at, :].astype(jnp.float32)
        centred = values - jnp.mean(values, axis=-1, keepdims=True)
        rstd = lax.rsqrt(jnp.mean(centred * centred, axis=-1, keepdims=True) + EPSILON)
        normed_ref[at, :] = (centred * rstd * scales[taps:, :]).astype(jnp.bfloat16)
        rstd_ref[at, :] = jnp.broadcast_to(rstd, (32, LANES))
        return 0

    lax.fori_loop(0, rows // 32, norm, 0)


def middle_kernel(steps, blocks, *refs):
    patches, normed, rstds, gain = refs[0:4], refs[4:8], refs[8:12], refs[12]
    cot0, pair, cot2, cot3, w_own, w2, w3, w2b, w3b, w_out_in = refs[13:23]
    grads, scaled, hidden, masked, w_in, means = refs[23:27], *refs[27:32]
    pre_grad, w_out, held, sems = refs[32:36]
    me = lax.axis_index("fsdp")
    parity = lax.rem(lax.axis_index("dp"), 2)
    rows = steps * blocks
    half, wide = w2.shape
    high = 2 * half
    used = iter(range(sems.shape[0]))

    def move(source, place):
        copy = pltpu.make_async_copy(source, place, sems.at[next(used)])
        copy.start()
        return copy

    def rows_of(index, part=0, size=high):
        return pl.ds(pl.multiple_of(index * high + part * half, TILE), size)

    coming = [
        move(w_own.at[:, columns_of(me, wide)], w_in.at[rows_of(me), :]),
        move(pair.at[rows:, :wide], w_in.at[rows_of(me ^ 1, 0, half), :]),
        move(pair.at[rows:, wide:], w_in.at[rows_of(me ^ 1, 1, half), :]),
        move(w2, w_in.at[rows_of(me ^ 2, parity, half), :]),
        move(w3, w_in.at[rows_of(me ^ 3, parity, half), :]),
        move(w2b, w_in.at[rows_of(me ^ 2, 1 - parity, half), :]),
        move(w3b, w_in.at[rows_of(me ^ 3, 1 - parity, half), :]),
    ]
    later = [
        move(w_out_in, w_out),
        move(cot0, masked.at[:rows, :]),
        move(pair.at[:rows, :], masked.at[rows : 2 * rows, :]),
        move(cot2, masked.at[2 * rows : 3 * rows, :]),
        move(cot3, masked.at[3 * rows :, :]),
    ]
    for copy in coming:
        copy.wait()
    fine = jnp.broadcast_to(gain[...], (TILE, gain.shape[1]))
    coarse = fine.astype(jnp.bfloat16)
    small = (fine - coarse.astype(jnp.float32)).astype(jnp.bfloat16)
    pulled = (dot(coarse, w_in[...], 1, 0) + dot(small, w_in[...], 1, 0))[:1, :]
    share = 1.0 / gain.shape[1]
    for k in range(4):
        at = slice(k * rows, (k + 1) * rows)
        counts = patches[k][rows:, :LANES].astype(jnp.float32)[:, :1]
        keep = jnp.concatenate([counts > t for t in range(steps)], axis=0)
        pre = dot(normed[k][...], w_in[...], 1, 0)
        for copy in later[:2] if k == 0 else later[k + 1 : k + 2]:
            copy.wait()
        kept = jnp.where(keep, masked[at, :], jnp.zeros((), jnp.bfloat16))
        masked[at, :] = kept
        back = dot(kept, w_out[...], 1, 1)
        sigma = sigmoid(pre)
        swish = pre * sigma
        hidden[at, :] = swish.astype(jnp.bfloat16)
        grown = 0.5 * back * (sigma + swish * (1.0 - sigma))
        pre_grad[at, :] = grown.astype(jnp.bfloat16)
        grown = grown * rstds[k][:, :1]
        scaled[at, :] = grown.astype(jnp.bfloat16)
        for i, other in enumerate((pulled, pre)):
            mean = jnp.sum(grown * other, axis=-1, keepdims=True) * share
            means[i, at, :] = jnp.broadcast_to(mean, (rows, LANES)).astype(jnp.bfloat16)
    leaving = []
    for k in (2, 3, 1, 0):
        cols = columns_of(me ^ k, high)
        left = jnp.concatenate([normed[j][:, cols] for j in range(4)], axis=0)
        held[k] = dot(left, pre_grad[...], 0, 0).astype(jnp.bfloat16)
        leaving.append(move(held.at[k], grads[k]))
    for copy in leaving:
        copy.wait()


def backward_kernel(steps, blocks, *refs):
    gain, scaled, w_in, masked, means = refs[0:5]
    normed, slope, feat = refs[5:9], refs[9:13], refs[13:17]
    taps_out, grad, totals = refs[17:20]
    rows = steps * blocks
    for k in range(4):
        at = slice(k * rows, (k + 1) * rows)
        pulled = dot(scaled[at, :], w_in[...], 1, 1) * gain[...]
        if k == 0:
            pulled = pulled + masked[at, :].astype(jnp.float32)
        grad[at, :] = pulled.astype(jnp.bfloat16)
    taps = 2 * steps - 1

    def column(k, c):
        cols = pl.ds(pl.multiple_of(c * LANES, LANES), LANES)
        inverse = jnp.broadcast_to(1.0 / gain[:, cols], (blocks, LANES)).astype(jnp.bfloat16)
        here = [slice(t * blocks, (t + 1) * blocks) for t in range(steps)]
        spots = [slice(k * rows + t * blocks, k * rows + (t + 1) * blocks) for t in range(steps)]
        left = [
            slope[k][at, cols]
            * (
                grad[spot, cols]
                - means[0, spot, :]
                - normed[k][at, cols] * inverse * means[1, spot, :]
            )
            for spot, at in zip(spots, here)
        ]
        right = [feat[k][at, cols] for at in here]
        for tap in range(taps):
            shift = tap - (steps - 1)
            terms = [(left[t], right[t + shift]) for t in range(steps) if 0 <= t + shift < steps]
            part = tree(terms, 0, len(terms))
            if k > 0:
                part = part + totals[tap, :, cols]
            if k < 3:
                totals[tap, :, cols] = part
            else:
                taps_out[tap, :, cols] = jnp.sum(part.astype(jnp.float32), axis=0, keepdims=True)
        if k == 3:
            taps_out[taps, :, cols] = jnp.zeros((1, LANES), jnp.float32)

    def step(c, _, k):
        column(k, c)
        return 0

    for k in range(4):
        lax.fori_loop(0, gain.shape[1] // LANES, functools.partial(step, k=k), 0)


def out_kernel(hidden, masked, out_ref, turned):
    turned[...] = hidden[...].T
    width = out_ref.shape[1]
    for c in range(0, width, 256):
        out_ref[:, c : c + 256] = (0.5 * dot(turned[...], masked[:, c : c + 256], 1, 0)).astype(
            jnp.bfloat16
        )


def join_kernel(width, *refs):
    pieces, out_ref, held, sems = refs[0:4], refs[4], refs[5], refs[6]
    me = lax.axis_index("fsdp")
    coming = [
        pltpu.make_async_copy(piece, held.at[k], sems.at[0, k]) for k, piece in enumerate(pieces)
    ]
    leaving = [
        pltpu.make_async_copy(held.at[k], out_ref.at[:, columns_of(me ^ k, width)], sems.at[1, k])
        for k in range(4)
    ]
    for copy in coming:
        copy.start()
    for first, second in zip(coming, leaving):
        first.wait()
        second.start()
    for copy in leaving:
        copy.wait()


def on_device(
    frames,
    occupied_slot_counts,
    block_frame_rows,
    order,
    cotangent,
    sub_weight,
    depth_kernel,
    norm_gain,
    w_in,
    w_out,
):
    n = lax.axis_size("dp")
    home = frames.shape[2]
    cap = (home + n - 1) // n
    split = home % n == 0
    blocks, steps, width = cotangent.shape[2:]
    rows = blocks * steps
    deep, hidden_width = w_in.shape
    wide = hidden_width // 4
    bf16, f32 = jnp.bfloat16, jnp.float32
    dma = pltpu.SemaphoreType.DMA

    info = jnp.concatenate([occupied_slot_counts[0], block_frame_rows[0, 0]])
    infos = lax.all_to_all(
        jnp.broadcast_to(info[None], (n, home + 1)), "dp", split_axis=0, concat_axis=0, tiled=True
    )

    w_far, w_out, sub_weight, depth_kernel = far(w_in, w_out, sub_weight, depth_kernel)
    sub1, sub2 = across(sub_weight, 1), across(sub_weight, 2)
    w2, w3 = pl.pallas_call(
        functools.partial(cut_kernel, wide),
        out_shape=(pltpu.HBM((deep // 2, wide), bf16),) * 2,
        in_specs=[ANY],
        out_specs=(ANY,) * 2,
        scratch_shapes=[pltpu.VMEM((2, deep // 2, wide), bf16), dma((2, 2))],
        compiler_params=params(),
        cost_estimate=cost(1),
    )(w_far)
    w2 = across(w2, 2)

    block_shape = frames.shape[3:]
    held = frames[0, 0].reshape((cap, n) + block_shape) if split else frames[0, 0]
    packed = pl.pallas_call(
        functools.partial(pack_kernel, n, split),
        out_shape=sds((n, cap) + block_shape, bf16),
        in_specs=[SMEM, SMEM, ANY],
        out_specs=ANY,
        scratch_shapes=[
            pltpu.VMEM((n if split else home, cap) + block_shape, bf16),
            dma((2 * (n if split else home),)),
        ],
        compiler_params=params(),
        cost_estimate=cost(2),
    )(order, infos, held)
    gain = norm_gain.reshape(1, width)
    packed, sub1, sub2, gain, cot, w2 = lax.optimization_barrier(
        (packed, sub1, sub2, gain, cotangent[0, 0], w2)
    )
    w3 = across(w3, 3)
    got = lax.all_to_all(packed, "dp", split_axis=0, concat_axis=0, tiled=True)
    sub_rows = sub_weight.shape[0]
    cot0, pair = pl.pallas_call(
        functools.partial(prepare_kernel, blocks, steps, wide),
        out_shape=(
            pltpu.HBM((rows, width), bf16),
            pltpu.HBM((rows + deep // 2, width), bf16),
        ),
        in_specs=[VMEM, ANY],
        out_specs=(ANY,) * 2,
        scratch_shapes=[
            pltpu.VMEM((rows, width), bf16),
            pltpu.VMEM((rows + deep // 2, width), bf16),
            pltpu.VMEM((rows * width // LANES, LANES), f32),
            dma((5,)),
        ],
        compiler_params=params(),
        cost_estimate=cost(2),
    )(cot, w_far)
    sub3 = across(sub2, 1)
    cot2, pair = across(cot0, 2), across(pair, 1)
    weight, scales = pl.pallas_call(
        order_kernel,
        out_shape=(
            pltpu.VMEM((4 * sub_rows, width), bf16),
            pltpu.VMEM((2 * steps, width), f32),
        ),
        in_specs=[ANY] * 4 + [VMEM] * 2,
        out_specs=(VMEM,) * 2,
        scratch_shapes=[dma((4,))],
        compiler_params=params(),
        cost_estimate=cost(1),
    )(sub_weight, *far(sub1, sub2, sub3), depth_kernel, gain)
    got, weight = lax.optimization_barrier((got, weight))
    w2b = across_dp(w2, 1)
    patches0 = pl.pallas_call(
        functools.partial(unpack_kernel, n, cap, blocks, steps),
        out_shape=sds((rows + blocks, block_shape[0] // steps * LANES), bf16),
        in_specs=[SMEM, SMEM, ANY],
        out_specs=VMEM,
        scratch_shapes=[
            pltpu.VMEM((blocks,) + block_shape, bf16),
            pltpu.VMEM((blocks * block_shape[0], LANES), f32),
            dma((blocks,)),
        ],
        compiler_params=params(),
        cost_estimate=cost(2),
    )(order, infos, got.reshape((n * cap,) + block_shape))
    patches = [patches0, across(patches0, 1), across(patches0, 2)]

    kept = (
        pltpu.VMEM((rows, width), bf16),
        pltpu.VMEM((rows, width), bf16),
        pltpu.VMEM((rows, width), bf16),
        pltpu.VMEM((rows, LANES), f32),
    )
    forward = pl.pallas_call(
        functools.partial(forward_kernel, steps, blocks),
        out_shape=kept,
        in_specs=[VMEM] * 3,
        out_specs=(VMEM,) * 4,
        scratch_shapes=[pltpu.VMEM((rows, width), bf16), pltpu.VMEM((rows, LANES), bf16)],
        compiler_params=params(),
        cost_estimate=cost(4),
    )
    groups = [list(forward(*near(patches0, weight, scales)))]
    groups[0][0], cot_relay, patch_relay, w3, w2b = lax.optimization_barrier(
        (groups[0][0], cot2, patches[2], w3, w2b)
    )
    w3b = across_dp(w3, 1)
    cot3 = across(cot_relay, 1)
    patches.append(across(patch_relay, 1))
    for k in (1, 2, 3):
        groups.append(forward(*near(patches[k], weight, scales)))
    feats, normeds, slopes, rstds = [near(*arrays) for arrays in zip(*groups)]
    g0, g1, g2, g3, scaled, hidden, masked, w_slice, means = pl.pallas_call(
        functools.partial(middle_kernel, steps, blocks),
        out_shape=(
            *[pltpu.HBM((deep, wide), bf16)] * 4,
            pltpu.VMEM((4 * rows, wide), bf16),
            pltpu.VMEM((4 * rows, wide), bf16),
            pltpu.VMEM((4 * rows, width), bf16),
            pltpu.VMEM((width, wide), bf16),
            pltpu.VMEM((2, 4 * rows, LANES), bf16),
        ),
        in_specs=[VMEM] * 13 + [ANY] * 10,
        out_specs=(ANY,) * 4 + (VMEM,) * 5,
        scratch_shapes=[
            pltpu.VMEM((4 * rows, wide), bf16),
            pltpu.VMEM((wide, width), bf16),
            pltpu.VMEM((4, deep, wide), bf16),
            dma((16,)),
        ],
        compiler_params=params(24),
        cost_estimate=cost(12),
    )(
        *patches, *normeds, *rstds, gain,
        *far(cot0, pair, cot2, cot3), w_far, *far(w2, w3, w2b, w3b), w_out,
    )
    g3, g2, g1 = across(g3, 3), across(g2, 2), across(g1, 1)

    taps = pl.pallas_call(
        functools.partial(backward_kernel, steps, blocks),
        out_shape=sds((2 * steps, 1, width), f32),
        in_specs=[VMEM] * 17,
        out_specs=VMEM,
        scratch_shapes=[
            pltpu.VMEM((4 * rows, width), bf16),
            pltpu.VMEM((2 * steps - 1, blocks, width), bf16),
        ],
        compiler_params=params(),
        cost_estimate=cost(13),
    )(gain, *near(scaled, w_slice, masked, means), *normeds, *slopes, *feats)
    taps, g2, hidden = lax.optimization_barrier((taps, g2, hidden))

    every = ("dp", "fsdp")
    devices = n * lax.axis_size("fsdp")
    shares = lax.all_to_all(
        taps.reshape(devices, 1, -1), every, split_axis=0, concat_axis=0, tiled=True
    )
    share = jnp.sum(shares, axis=0, keepdims=True) / rows
    grad_out = pl.pallas_call(
        out_kernel,
        out_shape=sds((wide, width), bf16),
        in_specs=[VMEM] * 2,
        out_specs=VMEM,
        scratch_shapes=[pltpu.VMEM((wide, 4 * rows), bf16)],
        compiler_params=params(),
        cost_estimate=cost(4),
    )(*near(hidden, masked))
    share, grad_out = lax.optimization_barrier((share, grad_out))
    whole = lax.all_to_all(
        jnp.broadcast_to(share, shares.shape), every, split_axis=0, concat_axis=0, tiled=True
    )
    kernel_grad = whole.reshape(2 * steps, width)[: depth_kernel.shape[0]]

    grad_in = pl.pallas_call(
        functools.partial(join_kernel, wide),
        out_shape=sds((deep, hidden_width), bf16),
        in_specs=[ANY] * 4,
        out_specs=ANY,
        scratch_shapes=[pltpu.VMEM((4, deep, wide), bf16), dma((2, 4))],
        compiler_params=params(),
        cost_estimate=cost(2),
    )(*far(g0, g1, g2, g3))
    return (grad_in[None], grad_out[None], kernel_grad)


def solution(mesh):
    placed = (
        P("dp", "fsdp", None, None, None),
        P("fsdp", "dp"),
        P("dp", "fsdp", None),
        P("fsdp", None),
        P("dp", "fsdp", None, None, None),
        P("fsdp", None),
        P(),
        P(),
        P("fsdp", None),
        P("fsdp", None),
    )
    return jax.shard_map(
        on_device,
        mesh=mesh,
        in_specs=placed,
        out_specs=(P("dp", "fsdp", None), P("dp", "fsdp", None), P()),
        check_vma=False,
    )
```

```python
import functools

import jax
import jax.numpy as jnp
from jax import lax
from jax.experimental import pallas as pl
from jax.experimental.pallas import tpu as pltpu
from jax.sharding import PartitionSpec as P

LANES = 128
HALF = 8
TILE = 16
EPSILON = 1e-05

VMEM = pl.BlockSpec(memory_space=pltpu.VMEM)
SMEM = pl.BlockSpec(memory_space=pltpu.SMEM)
ANY = pl.BlockSpec(memory_space=pl.ANY)


def params(mebibytes=16):
    return pltpu.CompilerParams(vmem_limit_bytes=mebibytes * 1024 * 1024)


def cost(microseconds):
    return pl.CostEstimate(
        flops=0, transcendentals=0, bytes_accessed=int(microseconds * 3.6e6)
    )


def near(*arrays):
    return [pltpu.with_memory_space_constraint(array, pltpu.VMEM) for array in arrays]


def far(*arrays):
    return [pltpu.with_memory_space_constraint(array, pltpu.HBM) for array in arrays]


def sds(shape, dtype):
    return jax.ShapeDtypeStruct(shape, dtype)


def sigmoid(values):
    return 0.5 * jnp.tanh(0.5 * values) + 0.5


def dot(left, right, left_dim, right_dim):
    return lax.dot_general(
        left, right, (((left_dim,), (right_dim,)), ((), ())), preferred_element_type=jnp.float32
    )


def across(value, k):
    n = lax.axis_size("fsdp")
    return lax.ppermute(value, "fsdp", [(i, i ^ k) for i in range(n)])


def across_dp(value, k):
    n = lax.axis_size("dp")
    return lax.ppermute(value, "dp", [(i, i ^ k) for i in range(n)])


def columns_of(index, width):
    return pl.ds(pl.multiple_of(index * width, LANES), width)


def prepare_kernel(
    blocks, steps, width, cot_ref, w_ref, cot_out, pair_out, cot, pair, scratch, sems
):
    rows = blocks * steps
    half = w_ref.shape[0] // 2
    cols = columns_of(lax.axis_index("fsdp") ^ 1, width)
    copies = [
        pltpu.make_async_copy(
            w_ref.at[i * half : (i + 1) * half, cols],
            pair.at[rows:, i * width : (i + 1) * width],
            sems.at[i],
        )
        for i in range(2)
    ]
    for copy in copies:
        copy.start()
    for c in range(cot_ref.shape[-1] // LANES):
        cols = slice(c * LANES, (c + 1) * LANES)
        scratch[c * rows : (c + 1) * rows, :] = (
            cot_ref[:, :, cols].reshape(rows, LANES).astype(jnp.float32)
        )
        for t in range(steps):
            at = slice(t * blocks, (t + 1) * blocks)
            turned = scratch[pl.ds(c * rows + t, blocks, stride=steps), :].astype(jnp.bfloat16)
            cot[at, cols] = turned
            pair[at, cols] = turned
    for copy in copies:
        copy.wait()
    leaving = [
        pltpu.make_async_copy(cot, cot_out, sems.at[3]),
        pltpu.make_async_copy(pair, pair_out, sems.at[4]),
    ]
    for copy in leaving:
        copy.start()
    for copy in leaving:
        copy.wait()


def pack_kernel(n, split, order_ref, info_ref, frames_ref, out_ref, held, sems):
    me = lax.axis_index("dp")
    classes = held.shape[0]
    coming = []
    for c in range(classes):
        source = frames_ref.at[:, c] if split else frames_ref.at[pl.ds(c, 1)]
        coming.append(pltpu.make_async_copy(source, held.at[c], sems.at[c]))
        coming[c].start()
    start = jnp.int32(0)
    for i in range(n - 1):
        start = start + jnp.where(i < me, info_ref[i, 0], 0)
    leaving = []
    for c in range(classes):
        target = order_ref[0, lax.rem(start + c, n)]
        leaving.append(
            pltpu.make_async_copy(held.at[c], out_ref.at[target], sems.at[classes + c])
        )
        coming[c].wait()
        leaving[c].start()
    for copy in leaving:
        copy.wait()


def unpack_kernel(
    n, cap, blocks, steps, order_ref, info_ref, got_ref, out_ref, landed, scratch, sems
):
    me = lax.axis_index("dp")
    residue = jnp.int32(0)
    for r in range(n):
        residue = residue + jnp.where(order_ref[0, r] == me, r, 0)
    starts, so_far = [], jnp.int32(0)
    for i in range(n):
        starts.append(so_far)
        so_far = so_far + info_ref[i, 0]
    length = got_ref.shape[1]
    copies, rows = [], []
    for m in range(blocks):
        g = residue + m * n
        source, start = jnp.int32(0), jnp.int32(0)
        for i in range(1, n):
            later = starts[i] <= g
            source = jnp.where(later, i, source)
            start = jnp.where(later, starts[i], start)
        h = g - start
        copy = pltpu.make_async_copy(
            got_ref.at[source * cap + lax.div(h, n)], landed.at[m], sems.at[m]
        )
        copy.start()
        copies.append(copy)
        rows.append(info_ref[source, 1 + h])
    height = lax.broadcasted_iota(jnp.int32, (blocks, out_ref.shape[1]), 0)
    counts = jnp.zeros((blocks, out_ref.shape[1]), jnp.int32)
    for m in range(blocks):
        counts = jnp.where(height == m, rows[m], counts)
    out_ref[steps * blocks :, :] = counts.astype(jnp.float32).astype(jnp.bfloat16)
    for m in range(blocks):
        copies[m].wait()
        scratch[m * length : (m + 1) * length, :] = landed[m].astype(jnp.float32)
    group = length // steps
    for t in range(steps):
        for j in range(group):
            out_ref[t * blocks : (t + 1) * blocks, j * LANES : (j + 1) * LANES] = scratch[
                pl.ds(group * t + j, blocks, stride=length), :
            ].astype(jnp.bfloat16)


def cut_kernel(width, w_ref, p2, p3, held, sems):
    me = lax.axis_index("fsdp")
    half = p2.shape[0]
    part = pl.ds(pl.multiple_of(lax.rem(lax.axis_index("dp"), 2) * half, TILE), half)
    coming = [
        pltpu.make_async_copy(w_ref.at[part, columns_of(me ^ k, width)], held.at[i], sems.at[0, i])
        for i, k in enumerate((2, 3))
    ]
    leaving = [
        pltpu.make_async_copy(held.at[i], target, sems.at[1, i])
        for i, target in enumerate((p2, p3))
    ]
    for copy in coming:
        copy.start()
    for first, second in zip(coming, leaving):
        first.wait()
        second.start()
    for copy in leaving:
        copy.wait()


def tree(terms, low, high):
    if high - low == 1:
        left, right = terms[low]
        return left * right
    middle = (low + high) // 2
    return tree(terms, low, middle) + tree(terms, middle, high)


def order_kernel(sub0, sub1, sub2, sub3, depth, gain, weight, scales, sems):
    me = lax.axis_index("fsdp")
    deep = sub0.shape[0]
    copies = [
        pltpu.make_async_copy(
            piece, weight.at[pl.ds(pl.multiple_of((me ^ k) * deep, TILE), deep), :], sems.at[k]
        )
        for k, piece in enumerate((sub0, sub1, sub2, sub3))
    ]
    for copy in copies:
        copy.start()
    scales[: depth.shape[0], :] = depth[...]
    scales[depth.shape[0] :, :] = gain[...]
    for copy in copies:
        copy.wait()


def forward_kernel(
    steps, blocks, patches, weight, scales, feat_ref, normed_ref, slope_ref, rstd_ref, work, mask
):
    rows = steps * blocks
    width, taps = scales.shape[1], scales.shape[0] - 1
    span = (taps - 1) // 2
    work[...] = dot(patches[:rows, :], weight[...], 1, 0)
    counts = patches[rows:, :LANES].astype(jnp.float32)
    spots = [slice(t * blocks, (t + 1) * blocks) for t in range(steps)]
    for t in range(steps):
        mask[spots[t], :] = jnp.where(counts > t, 1.0, 0.0)

    def column(c, _):
        cols = pl.ds(pl.multiple_of(c * LANES, LANES), LANES)
        weights = [
            jnp.broadcast_to(scales[k : k + 1, cols], (blocks, LANES)).astype(jnp.bfloat16)
            for k in range(taps)
        ]
        values = []
        for t in range(steps):
            values.append((work[spots[t], cols] * mask[spots[t], :]).astype(jnp.bfloat16))
            feat_ref[spots[t], cols] = values[t]
        for t in range(steps):
            terms = [
                (values[s], weights[s - t + span])
                for s in range(steps)
                if 0 <= s - t + span < taps
            ]
            conv = tree(terms, 0, len(terms)).astype(jnp.float32)
            keep = mask[spots[t], :]
            sigma = sigmoid(conv)
            swish = conv * sigma
            slope_ref[spots[t], cols] = (keep * (sigma + swish * (1.0 - sigma))).astype(
                jnp.bfloat16
            )
            work[spots[t], cols] = values[t].astype(jnp.float32) + keep * swish
        return 0

    lax.fori_loop(0, width // LANES, column, 0)

    def norm(i, _):
        at = pl.ds(pl.multiple_of(i * 32, 32), 32)
        values = work[at, :]
        centred = values - jnp.mean(values, axis=-1, keepdims=True)
        rstd = lax.rsqrt(jnp.mean(centred * centred, axis=-1, keepdims=True) + EPSILON)
        normed_ref[at, :] = (centred * rstd * scales[taps:, :]).astype(jnp.bfloat16)
        rstd_ref[at, :] = jnp.broadcast_to(rstd, (32, LANES))
        return 0

    lax.fori_loop(0, rows // 32, norm, 0)


def middle_kernel(steps, blocks, *refs):
    patches, normed, rstds, gain = refs[0:4], refs[4:8], refs[8:12], refs[12]
    cot0, pair, cot2, cot3, w_own, w2, w3, w2b, w3b, w_out_in = refs[13:23]
    grads, scaled, hidden, masked, w_in, means = refs[23:27], *refs[27:32]
    pre_grad, w_out, held, sems = refs[32:36]
    me = lax.axis_index("fsdp")
    parity = lax.rem(lax.axis_index("dp"), 2)
    rows = steps * blocks
    half, wide = w2.shape
    high = 2 * half
    used = iter(range(sems.shape[0]))

    def move(source, place):
        copy = pltpu.make_async_copy(source, place, sems.at[next(used)])
        copy.start()
        return copy

    def rows_of(index, part=0, size=high):
        return pl.ds(pl.multiple_of(index * high + part * half, TILE), size)

    coming = [
        move(w_own.at[:, columns_of(me, wide)], w_in.at[rows_of(me), :]),
        move(pair.at[rows:, :wide], w_in.at[rows_of(me ^ 1, 0, half), :]),
        move(pair.at[rows:, wide:], w_in.at[rows_of(me ^ 1, 1, half), :]),
        move(w2, w_in.at[rows_of(me ^ 2, parity, half), :]),
        move(w3, w_in.at[rows_of(me ^ 3, parity, half), :]),
        move(w2b, w_in.at[rows_of(me ^ 2, 1 - parity, half), :]),
        move(w3b, w_in.at[rows_of(me ^ 3, 1 - parity, half), :]),
    ]
    for copy in coming:
        copy.wait()
    later = [
        move(w_out_in, w_out),
        move(cot0, masked.at[:rows, :]),
        move(pair.at[:rows, :], masked.at[rows : 2 * rows, :]),
        move(cot2, masked.at[2 * rows : 3 * rows, :]),
        move(cot3, masked.at[3 * rows :, :]),
    ]
    fine = jnp.broadcast_to(gain[...], (TILE, gain.shape[1]))
    coarse = fine.astype(jnp.bfloat16)
    small = (fine - coarse.astype(jnp.float32)).astype(jnp.bfloat16)
    pulled = (dot(coarse, w_in[...], 1, 0) + dot(small, w_in[...], 1, 0))[:1, :]
    share = 1.0 / gain.shape[1]
    for k in range(4):
        at = slice(k * rows, (k + 1) * rows)
        counts = patches[k][rows:, :LANES].astype(jnp.float32)[:, :1]
        keep = jnp.concatenate([counts > t for t in range(steps)], axis=0)
        pre = dot(normed[k][...], w_in[...], 1, 0)
        for copy in later[:2] if k == 0 else later[k + 1 : k + 2]:
            copy.wait()
        kept = jnp.where(keep, masked[at, :], jnp.zeros((), jnp.bfloat16))
        masked[at, :] = kept
        back = dot(kept, w_out[...], 1, 1)
        sigma = sigmoid(pre)
        swish = pre * sigma
        hidden[at, :] = swish.astype(jnp.bfloat16)
        grown = 0.5 * back * (sigma + swish * (1.0 - sigma))
        pre_grad[at, :] = grown.astype(jnp.bfloat16)
        grown = grown * rstds[k][:, :1]
        scaled[at, :] = grown.astype(jnp.bfloat16)
        for i, other in enumerate((pulled, pre)):
            mean = jnp.sum(grown * other, axis=-1, keepdims=True) * share
            means[i, at, :] = jnp.broadcast_to(mean, (rows, LANES)).astype(jnp.bfloat16)
    leaving = []
    for k in (2, 3, 1, 0):
        cols = columns_of(me ^ k, high)
        left = jnp.concatenate([normed[j][:, cols] for j in range(4)], axis=0)
        held[k] = dot(left, pre_grad[...], 0, 0).astype(jnp.bfloat16)
        leaving.append(move(held.at[k], grads[k]))
    for copy in leaving:
        copy.wait()


def backward_kernel(steps, blocks, *refs):
    gain, scaled, w_in, masked, means = refs[0:5]
    normed, slope, feat = refs[5:9], refs[9:13], refs[13:17]
    taps_out, grad, totals = refs[17:20]
    rows = steps * blocks
    for k in range(4):
        at = slice(k * rows, (k + 1) * rows)
        pulled = dot(scaled[at, :], w_in[...], 1, 1) * gain[...]
        if k == 0:
            pulled = pulled + masked[at, :].astype(jnp.float32)
        grad[at, :] = pulled.astype(jnp.bfloat16)
    taps = 2 * steps - 1

    def column(k, c):
        cols = pl.ds(pl.multiple_of(c * LANES, LANES), LANES)
        inverse = jnp.broadcast_to(1.0 / gain[:, cols], (blocks, LANES)).astype(jnp.bfloat16)
        here = [slice(t * blocks, (t + 1) * blocks) for t in range(steps)]
        spots = [slice(k * rows + t * blocks, k * rows + (t + 1) * blocks) for t in range(steps)]
        left = [
            slope[k][at, cols]
            * (
                grad[spot, cols]
                - means[0, spot, :]
                - normed[k][at, cols] * inverse * means[1, spot, :]
            )
            for spot, at in zip(spots, here)
        ]
        right = [feat[k][at, cols] for at in here]
        for tap in range(taps):
            shift = tap - (steps - 1)
            terms = [(left[t], right[t + shift]) for t in range(steps) if 0 <= t + shift < steps]
            part = tree(terms, 0, len(terms))
            if k > 0:
                part = part + totals[tap, :, cols]
            if k < 3:
                totals[tap, :, cols] = part
            else:
                taps_out[tap, :, cols] = jnp.sum(part.astype(jnp.float32), axis=0, keepdims=True)
        if k == 3:
            taps_out[taps, :, cols] = jnp.zeros((1, LANES), jnp.float32)

    def step(c, _, k):
        column(k, c)
        return 0

    for k in range(4):
        lax.fori_loop(0, gain.shape[1] // LANES, functools.partial(step, k=k), 0)


def out_kernel(hidden, masked, out_ref, turned):
    turned[...] = hidden[...].T
    width = out_ref.shape[1]
    for c in range(0, width, 256):
        out_ref[:, c : c + 256] = (0.5 * dot(turned[...], masked[:, c : c + 256], 1, 0)).astype(
            jnp.bfloat16
        )


def join_kernel(width, *refs):
    pieces, out_ref, held, sems = refs[0:4], refs[4], refs[5], refs[6]
    me = lax.axis_index("fsdp")
    coming = [
        pltpu.make_async_copy(piece, held.at[k], sems.at[0, k]) for k, piece in enumerate(pieces)
    ]
    leaving = [
        pltpu.make_async_copy(held.at[k], out_ref.at[:, columns_of(me ^ k, width)], sems.at[1, k])
        for k in range(4)
    ]
    for copy in coming:
        copy.start()
    for first, second in zip(coming, leaving):
        first.wait()
        second.start()
    for copy in leaving:
        copy.wait()


def on_device(
    frames,
    occupied_slot_counts,
    block_frame_rows,
    order,
    cotangent,
    sub_weight,
    depth_kernel,
    norm_gain,
    w_in,
    w_out,
):
    n = lax.axis_size("dp")
    home = frames.shape[2]
    cap = (home + n - 1) // n
    split = home % n == 0
    blocks, steps, width = cotangent.shape[2:]
    rows = blocks * steps
    deep, hidden_width = w_in.shape
    wide = hidden_width // 4
    bf16, f32 = jnp.bfloat16, jnp.float32
    dma = pltpu.SemaphoreType.DMA

    info = jnp.concatenate([occupied_slot_counts[0], block_frame_rows[0, 0]])
    infos = lax.all_to_all(
        jnp.broadcast_to(info[None], (n, home + 1)), "dp", split_axis=0, concat_axis=0, tiled=True
    )

    w_far, w_out, sub_weight, depth_kernel = far(w_in, w_out, sub_weight, depth_kernel)
    sub1, sub2 = across(sub_weight, 1), across(sub_weight, 2)
    w2, w3 = pl.pallas_call(
        functools.partial(cut_kernel, wide),
        out_shape=(pltpu.HBM((deep // 2, wide), bf16),) * 2,
        in_specs=[ANY],
        out_specs=(ANY,) * 2,
        scratch_shapes=[pltpu.VMEM((2, deep // 2, wide), bf16), dma((2, 2))],
        compiler_params=params(),
        cost_estimate=cost(1),
    )(w_far)
    w2 = across(w2, 2)

    block_shape = frames.shape[3:]
    held = frames[0, 0].reshape((cap, n) + block_shape) if split else frames[0, 0]
    packed = pl.pallas_call(
        functools.partial(pack_kernel, n, split),
        out_shape=sds((n, cap) + block_shape, bf16),
        in_specs=[SMEM, SMEM, ANY],
        out_specs=ANY,
        scratch_shapes=[
            pltpu.VMEM((n if split else home, cap) + block_shape, bf16),
            dma((2 * (n if split else home),)),
        ],
        compiler_params=params(),
        cost_estimate=cost(2),
    )(order, infos, held)
    gain = norm_gain.reshape(1, width)
    packed, sub1, sub2, gain, cot, w2 = lax.optimization_barrier(
        (packed, sub1, sub2, gain, cotangent[0, 0], w2)
    )
    w3 = across(w3, 3)
    got = lax.all_to_all(packed, "dp", split_axis=0, concat_axis=0, tiled=True)
    sub_rows = sub_weight.shape[0]
    cot0, pair = pl.pallas_call(
        functools.partial(prepare_kernel, blocks, steps, wide),
        out_shape=(
            pltpu.HBM((rows, width), bf16),
            pltpu.HBM((rows + deep // 2, width), bf16),
        ),
        in_specs=[VMEM, ANY],
        out_specs=(ANY,) * 2,
        scratch_shapes=[
            pltpu.VMEM((rows, width), bf16),
            pltpu.VMEM((rows + deep // 2, width), bf16),
            pltpu.VMEM((rows * width // LANES, LANES), f32),
            dma((5,)),
        ],
        compiler_params=params(),
        cost_estimate=cost(2),
    )(cot, w_far)
    sub3 = across(sub2, 1)
    cot2, pair = across(cot0, 2), across(pair, 1)
    weight, scales = pl.pallas_call(
        order_kernel,
        out_shape=(
            pltpu.VMEM((4 * sub_rows, width), bf16),
            pltpu.VMEM((2 * steps, width), f32),
        ),
        in_specs=[ANY] * 4 + [VMEM] * 2,
        out_specs=(VMEM,) * 2,
        scratch_shapes=[dma((4,))],
        compiler_params=params(),
        cost_estimate=cost(1),
    )(sub_weight, *far(sub1, sub2, sub3), depth_kernel, gain)
    w2b = across_dp(w2, 1)
    got, weight, w3, w2b = lax.optimization_barrier((got, weight, w3, w2b))
    w3b = across_dp(w3, 1)
    patches0 = pl.pallas_call(
        functools.partial(unpack_kernel, n, cap, blocks, steps),
        out_shape=sds((rows + blocks, block_shape[0] // steps * LANES), bf16),
        in_specs=[SMEM, SMEM, ANY],
        out_specs=VMEM,
        scratch_shapes=[
            pltpu.VMEM((blocks,) + block_shape, bf16),
            pltpu.VMEM((blocks * block_shape[0], LANES), f32),
            dma((blocks,)),
        ],
        compiler_params=params(),
        cost_estimate=cost(2),
    )(order, infos, got.reshape((n * cap,) + block_shape))
    patches = [patches0, across(patches0, 1), across(patches0, 2)]

    kept = (
        pltpu.VMEM((rows, width), bf16),
        pltpu.VMEM((rows, width), bf16),
        pltpu.VMEM((rows, width), bf16),
        pltpu.VMEM((rows, LANES), f32),
    )
    forward = pl.pallas_call(
        functools.partial(forward_kernel, steps, blocks),
        out_shape=kept,
        in_specs=[VMEM] * 3,
        out_specs=(VMEM,) * 4,
        scratch_shapes=[pltpu.VMEM((rows, width), f32), pltpu.VMEM((rows, LANES), f32)],
        compiler_params=params(),
        cost_estimate=cost(4),
    )
    groups = [list(forward(*near(patches[0], weight, scales)))]
    groups[0][0], patches[1] = lax.optimization_barrier((groups[0][0], patches[1]))
    groups.append(list(forward(*near(patches[1], weight, scales))))
    groups[1][0], cot_relay, patches[2] = lax.optimization_barrier(
        (groups[1][0], cot2, patches[2])
    )
    cot3 = across(cot_relay, 1)
    patches.append(across(patches[2], 1))
    for k in (2, 3):
        groups.append(forward(*near(patches[k], weight, scales)))
    feats, normeds, slopes, rstds = [near(*arrays) for arrays in zip(*groups)]
    g0, g1, g2, g3, scaled, hidden, masked, w_slice, means = pl.pallas_call(
        functools.partial(middle_kernel, steps, blocks),
        out_shape=(
            *[pltpu.HBM((deep, wide), bf16)] * 4,
            pltpu.VMEM((4 * rows, wide), bf16),
            pltpu.VMEM((4 * rows, wide), bf16),
            pltpu.VMEM((4 * rows, width), bf16),
            pltpu.VMEM((width, wide), bf16),
            pltpu.VMEM((2, 4 * rows, LANES), bf16),
        ),
        in_specs=[VMEM] * 13 + [ANY] * 10,
        out_specs=(ANY,) * 4 + (VMEM,) * 5,
        scratch_shapes=[
            pltpu.VMEM((4 * rows, wide), bf16),
            pltpu.VMEM((wide, width), bf16),
            pltpu.VMEM((4, deep, wide), bf16),
            dma((16,)),
        ],
        compiler_params=params(24),
        cost_estimate=cost(12),
    )(
        *patches, *normeds, *rstds, gain,
        *far(cot0, pair, cot2, cot3), w_far, *far(w2, w3, w2b, w3b), w_out,
    )
    g3, g2, g1 = across(g3, 3), across(g2, 2), across(g1, 1)

    taps = pl.pallas_call(
        functools.partial(backward_kernel, steps, blocks),
        out_shape=sds((2 * steps, 1, width), f32),
        in_specs=[VMEM] * 17,
        out_specs=VMEM,
        scratch_shapes=[
            pltpu.VMEM((4 * rows, width), bf16),
            pltpu.VMEM((2 * steps - 1, blocks, width), bf16),
        ],
        compiler_params=params(),
        cost_estimate=cost(13),
    )(gain, *near(scaled, w_slice, masked, means), *normeds, *slopes, *feats)
    taps, g2, hidden = lax.optimization_barrier((taps, g2, hidden))

    every = ("dp", "fsdp")
    devices = n * lax.axis_size("fsdp")
    shares = lax.all_to_all(
        taps.reshape(devices, 1, -1), every, split_axis=0, concat_axis=0, tiled=True
    )
    share = jnp.sum(shares, axis=0, keepdims=True) / rows
    grad_out = pl.pallas_call(
        out_kernel,
        out_shape=sds((wide, width), bf16),
        in_specs=[VMEM] * 2,
        out_specs=VMEM,
        scratch_shapes=[pltpu.VMEM((wide, 4 * rows), bf16)],
        compiler_params=params(),
        cost_estimate=cost(4),
    )(*near(hidden, masked))
    share, grad_out = lax.optimization_barrier((share, grad_out))
    whole = lax.all_to_all(
        jnp.broadcast_to(share, shares.shape), every, split_axis=0, concat_axis=0, tiled=True
    )
    kernel_grad = whole.reshape(2 * steps, width)[: depth_kernel.shape[0]]

    grad_in = pl.pallas_call(
        functools.partial(join_kernel, wide),
        out_shape=sds((deep, hidden_width), bf16),
        in_specs=[ANY] * 4,
        out_specs=ANY,
        scratch_shapes=[pltpu.VMEM((4, deep, wide), bf16), dma((2, 4))],
        compiler_params=params(),
        cost_estimate=cost(2),
    )(g0, g1, g2, g3)
    return (grad_in[None], grad_out[None], kernel_grad)


def solution(mesh):
    placed = (
        P("dp", "fsdp", None, None, None),
        P("fsdp", "dp"),
        P("dp", "fsdp", None),
        P("fsdp", None),
        P("dp", "fsdp", None, None, None),
        P("fsdp", None),
        P(),
        P(),
        P("fsdp", None),
        P("fsdp", None),
    )
    return jax.shard_map(
        on_device,
        mesh=mesh,
        in_specs=placed,
        out_specs=(P("dp", "fsdp", None), P("dp", "fsdp", None), P()),
        check_vma=False,
    )
```

```python
import functools

import jax
import jax.numpy as jnp
from jax import lax
from jax.experimental import pallas as pl
from jax.experimental.pallas import tpu as pltpu
from jax.sharding import PartitionSpec as P

LANES = 128
HALF = 8
TILE = 16
EPSILON = 1e-05

VMEM = pl.BlockSpec(memory_space=pltpu.VMEM)
SMEM = pl.BlockSpec(memory_space=pltpu.SMEM)
ANY = pl.BlockSpec(memory_space=pl.ANY)


def params(mebibytes=16):
    return pltpu.CompilerParams(vmem_limit_bytes=mebibytes * 1024 * 1024)


def cost(microseconds):
    return pl.CostEstimate(
        flops=0, transcendentals=0, bytes_accessed=int(microseconds * 3.6e6)
    )


def near(*arrays):
    return [pltpu.with_memory_space_constraint(array, pltpu.VMEM) for array in arrays]


def far(*arrays):
    return [pltpu.with_memory_space_constraint(array, pltpu.HBM) for array in arrays]


def sds(shape, dtype):
    return jax.ShapeDtypeStruct(shape, dtype)


def sigmoid(values):
    return 0.5 * jnp.tanh(0.5 * values) + 0.5


def dot(left, right, left_dim, right_dim):
    return lax.dot_general(
        left, right, (((left_dim,), (right_dim,)), ((), ())), preferred_element_type=jnp.float32
    )


def across(value, k):
    n = lax.axis_size("fsdp")
    return lax.ppermute(value, "fsdp", [(i, i ^ k) for i in range(n)])


def across_dp(value, k):
    n = lax.axis_size("dp")
    return lax.ppermute(value, "dp", [(i, i ^ k) for i in range(n)])


def columns_of(index, width):
    return pl.ds(pl.multiple_of(index * width, LANES), width)


def prepare_kernel(
    blocks, steps, width, cot_ref, w_ref, cot_out, pair_out, cot, pair, scratch, sems
):
    rows = blocks * steps
    half = w_ref.shape[0] // 2
    cols = columns_of(lax.axis_index("fsdp") ^ 1, width)
    copies = [
        pltpu.make_async_copy(
            w_ref.at[i * half : (i + 1) * half, cols],
            pair.at[rows:, i * width : (i + 1) * width],
            sems.at[i],
        )
        for i in range(2)
    ]
    for copy in copies:
        copy.start()
    for c in range(cot_ref.shape[-1] // LANES):
        cols = slice(c * LANES, (c + 1) * LANES)
        scratch[c * rows : (c + 1) * rows, :] = (
            cot_ref[:, :, cols].reshape(rows, LANES).astype(jnp.float32)
        )
        for t in range(steps):
            at = slice(t * blocks, (t + 1) * blocks)
            turned = scratch[pl.ds(c * rows + t, blocks, stride=steps), :].astype(jnp.bfloat16)
            cot[at, cols] = turned
            pair[at, cols] = turned
    for copy in copies:
        copy.wait()
    leaving = [
        pltpu.make_async_copy(cot, cot_out, sems.at[3]),
        pltpu.make_async_copy(pair, pair_out, sems.at[4]),
    ]
    for copy in leaving:
        copy.start()
    for copy in leaving:
        copy.wait()


def pack_kernel(n, split, order_ref, info_ref, frames_ref, out_ref, held, sems):
    me = lax.axis_index("dp")
    classes = held.shape[0]
    coming = []
    for c in range(classes):
        source = frames_ref.at[:, c] if split else frames_ref.at[pl.ds(c, 1)]
        coming.append(pltpu.make_async_copy(source, held.at[c], sems.at[c]))
        coming[c].start()
    start = jnp.int32(0)
    for i in range(n - 1):
        start = start + jnp.where(i < me, info_ref[i, 0], 0)
    leaving = []
    for c in range(classes):
        target = order_ref[0, lax.rem(start + c, n)]
        leaving.append(
            pltpu.make_async_copy(held.at[c], out_ref.at[target], sems.at[classes + c])
        )
        coming[c].wait()
        leaving[c].start()
    for copy in leaving:
        copy.wait()


def unpack_kernel(
    n, cap, blocks, steps, order_ref, info_ref, got_ref, out_ref, landed, scratch, sems
):
    me = lax.axis_index("dp")
    residue = jnp.int32(0)
    for r in range(n):
        residue = residue + jnp.where(order_ref[0, r] == me, r, 0)
    starts, so_far = [], jnp.int32(0)
    for i in range(n):
        starts.append(so_far)
        so_far = so_far + info_ref[i, 0]
    length = got_ref.shape[1]
    copies, rows = [], []
    for m in range(blocks):
        g = residue + m * n
        source, start = jnp.int32(0), jnp.int32(0)
        for i in range(1, n):
            later = starts[i] <= g
            source = jnp.where(later, i, source)
            start = jnp.where(later, starts[i], start)
        h = g - start
        copy = pltpu.make_async_copy(
            got_ref.at[source * cap + lax.div(h, n)], landed.at[m], sems.at[m]
        )
        copy.start()
        copies.append(copy)
        rows.append(info_ref[source, 1 + h])
    height = lax.broadcasted_iota(jnp.int32, (blocks, out_ref.shape[1]), 0)
    counts = jnp.zeros((blocks, out_ref.shape[1]), jnp.int32)
    for m in range(blocks):
        counts = jnp.where(height == m, rows[m], counts)
    out_ref[steps * blocks :, :] = counts.astype(jnp.float32).astype(jnp.bfloat16)
    for m in range(blocks):
        copies[m].wait()
        scratch[m * length : (m + 1) * length, :] = landed[m].astype(jnp.float32)
    group = length // steps
    for t in range(steps):
        for j in range(group):
            out_ref[t * blocks : (t + 1) * blocks, j * LANES : (j + 1) * LANES] = scratch[
                pl.ds(group * t + j, blocks, stride=length), :
            ].astype(jnp.bfloat16)


def cut_kernel(width, w_ref, p2, p3, half2, full3, sems):
    me = lax.axis_index("fsdp")
    half = p2.shape[0]
    part = pl.ds(pl.multiple_of(lax.rem(lax.axis_index("dp"), 2) * half, TILE), half)
    coming = [
        pltpu.make_async_copy(w_ref.at[part, columns_of(me ^ 2, width)], half2, sems.at[0]),
        pltpu.make_async_copy(w_ref.at[:, columns_of(me ^ 3, width)], full3, sems.at[1]),
    ]
    leaving = [
        pltpu.make_async_copy(half2, p2, sems.at[2]),
        pltpu.make_async_copy(full3, p3, sems.at[3]),
    ]
    for copy in coming:
        copy.start()
    for first, second in zip(coming, leaving):
        first.wait()
        second.start()
    for copy in leaving:
        copy.wait()


def tree(terms, low, high):
    if high - low == 1:
        left, right = terms[low]
        return left * right
    middle = (low + high) // 2
    return tree(terms, low, middle) + tree(terms, middle, high)


def order_kernel(sub0, sub1, sub2, sub3, depth, gain, weight, scales, sems):
    me = lax.axis_index("fsdp")
    deep = sub0.shape[0]
    copies = [
        pltpu.make_async_copy(
            piece, weight.at[pl.ds(pl.multiple_of((me ^ k) * deep, TILE), deep), :], sems.at[k]
        )
        for k, piece in enumerate((sub0, sub1, sub2, sub3))
    ]
    for copy in copies:
        copy.start()
    scales[: depth.shape[0], :] = depth[...]
    scales[depth.shape[0] :, :] = gain[...]
    for copy in copies:
        copy.wait()


def forward_kernel(
    steps, blocks, patches, weight, scales, feat_ref, normed_ref, slope_ref, rstd_ref, work, mask
):
    rows = steps * blocks
    width, taps = scales.shape[1], scales.shape[0] - 1
    span = (taps - 1) // 2
    work[...] = dot(patches[:rows, :], weight[...], 1, 0)
    counts = patches[rows:, :LANES].astype(jnp.float32)
    spots = [slice(t * blocks, (t + 1) * blocks) for t in range(steps)]
    for t in range(steps):
        mask[spots[t], :] = jnp.where(counts > t, 1.0, 0.0)

    def column(c, _):
        cols = pl.ds(pl.multiple_of(c * LANES, LANES), LANES)
        weights = [
            jnp.broadcast_to(scales[k : k + 1, cols], (blocks, LANES)).astype(jnp.bfloat16)
            for k in range(taps)
        ]
        values = []
        for t in range(steps):
            values.append((work[spots[t], cols] * mask[spots[t], :]).astype(jnp.bfloat16))
            feat_ref[spots[t], cols] = values[t]
        for t in range(steps):
            terms = [
                (values[s], weights[s - t + span])
                for s in range(steps)
                if 0 <= s - t + span < taps
            ]
            conv = tree(terms, 0, len(terms)).astype(jnp.float32)
            keep = mask[spots[t], :]
            sigma = sigmoid(conv)
            swish = conv * sigma
            slope_ref[spots[t], cols] = (keep * (sigma + swish * (1.0 - sigma))).astype(
                jnp.bfloat16
            )
            work[spots[t], cols] = values[t].astype(jnp.float32) + keep * swish
        return 0

    lax.fori_loop(0, width // LANES, column, 0)

    def norm(i, _):
        at = pl.ds(pl.multiple_of(i * 32, 32), 32)
        values = work[at, :]
        centred = values - jnp.mean(values, axis=-1, keepdims=True)
        rstd = lax.rsqrt(jnp.mean(centred * centred, axis=-1, keepdims=True) + EPSILON)
        normed_ref[at, :] = (centred * rstd * scales[taps:, :]).astype(jnp.bfloat16)
        rstd_ref[at, :] = jnp.broadcast_to(rstd, (32, LANES))
        return 0

    lax.fori_loop(0, rows // 32, norm, 0)


def middle_kernel(steps, blocks, *refs):
    patches, normed, rstds, gain = refs[0:4], refs[4:8], refs[8:12], refs[12]
    cot0, pair, cot2, cot3, w_own, w2, w3, w2b, w_out_in = refs[13:22]
    grads, scaled, hidden, masked, w_in, means = refs[22:26], *refs[26:31]
    pre_grad, w_out, held, sems = refs[31:35]
    me = lax.axis_index("fsdp")
    parity = lax.rem(lax.axis_index("dp"), 2)
    rows = steps * blocks
    half, wide = w2.shape
    high = 2 * half
    used = iter(range(sems.shape[0]))

    def move(source, place):
        copy = pltpu.make_async_copy(source, place, sems.at[next(used)])
        copy.start()
        return copy

    def rows_of(index, part=0, size=high):
        return pl.ds(pl.multiple_of(index * high + part * half, TILE), size)

    coming = [
        move(w_own.at[:, columns_of(me, wide)], w_in.at[rows_of(me), :]),
        move(pair.at[rows:, :wide], w_in.at[rows_of(me ^ 1, 0, half), :]),
        move(pair.at[rows:, wide:], w_in.at[rows_of(me ^ 1, 1, half), :]),
        move(w2, w_in.at[rows_of(me ^ 2, parity, half), :]),
        move(w3, w_in.at[rows_of(me ^ 3), :]),
        move(w2b, w_in.at[rows_of(me ^ 2, 1 - parity, half), :]),
    ]
    for copy in coming:
        copy.wait()
    later = [
        move(w_out_in, w_out),
        move(cot0, masked.at[:rows, :]),
        move(pair.at[:rows, :], masked.at[rows : 2 * rows, :]),
        move(cot2, masked.at[2 * rows : 3 * rows, :]),
        move(cot3, masked.at[3 * rows :, :]),
    ]
    fine = jnp.broadcast_to(gain[...], (TILE, gain.shape[1]))
    coarse = fine.astype(jnp.bfloat16)
    small = (fine - coarse.astype(jnp.float32)).astype(jnp.bfloat16)
    pulled = (dot(coarse, w_in[...], 1, 0) + dot(small, w_in[...], 1, 0))[:1, :]
    share = 1.0 / gain.shape[1]
    for k in range(4):
        at = slice(k * rows, (k + 1) * rows)
        counts = patches[k][rows:, :LANES].astype(jnp.float32)[:, :1]
        keep = jnp.concatenate([counts > t for t in range(steps)], axis=0)
        pre = dot(normed[k][...], w_in[...], 1, 0)
        for copy in later[:2] if k == 0 else later[k + 1 : k + 2]:
            copy.wait()
        kept = jnp.where(keep, masked[at, :], jnp.zeros((), jnp.bfloat16))
        masked[at, :] = kept
        back = dot(kept, w_out[...], 1, 1)
        sigma = sigmoid(pre)
        swish = pre * sigma
        hidden[at, :] = swish.astype(jnp.bfloat16)
        grown = 0.5 * back * (sigma + swish * (1.0 - sigma))
        pre_grad[at, :] = grown.astype(jnp.bfloat16)
        grown = grown * rstds[k][:, :1]
        scaled[at, :] = grown.astype(jnp.bfloat16)
        for i, other in enumerate((pulled, pre)):
            mean = jnp.sum(grown * other, axis=-1, keepdims=True) * share
            means[i, at, :] = jnp.broadcast_to(mean, (rows, LANES)).astype(jnp.bfloat16)
    leaving = []
    for k in (2, 3, 1, 0):
        cols = columns_of(me ^ k, high)
        left = jnp.concatenate([normed[j][:, cols] for j in range(4)], axis=0)
        held[k] = dot(left, pre_grad[...], 0, 0).astype(jnp.bfloat16)
        leaving.append(move(held.at[k], grads[k]))
    for copy in leaving:
        copy.wait()


def backward_kernel(steps, blocks, *refs):
    gain, scaled, w_in, masked, means = refs[0:5]
    normed, slope, feat = refs[5:9], refs[9:13], refs[13:17]
    taps_out, grad, totals = refs[17:20]
    rows = steps * blocks
    for k in range(4):
        at = slice(k * rows, (k + 1) * rows)
        pulled = dot(scaled[at, :], w_in[...], 1, 1) * gain[...]
        if k == 0:
            pulled = pulled + masked[at, :].astype(jnp.float32)
        grad[at, :] = pulled.astype(jnp.bfloat16)
    taps = 2 * steps - 1

    def column(k, c):
        cols = pl.ds(pl.multiple_of(c * LANES, LANES), LANES)
        inverse = jnp.broadcast_to(1.0 / gain[:, cols], (blocks, LANES)).astype(jnp.bfloat16)
        here = [slice(t * blocks, (t + 1) * blocks) for t in range(steps)]
        spots = [slice(k * rows + t * blocks, k * rows + (t + 1) * blocks) for t in range(steps)]
        left = [
            slope[k][at, cols]
            * (
                grad[spot, cols]
                - means[0, spot, :]
                - normed[k][at, cols] * inverse * means[1, spot, :]
            )
            for spot, at in zip(spots, here)
        ]
        right = [feat[k][at, cols] for at in here]
        for tap in range(taps):
            shift = tap - (steps - 1)
            terms = [(left[t], right[t + shift]) for t in range(steps) if 0 <= t + shift < steps]
            part = tree(terms, 0, len(terms))
            if k > 0:
                part = part + totals[tap, :, cols]
            if k < 3:
                totals[tap, :, cols] = part
            else:
                taps_out[tap, :, cols] = jnp.sum(part.astype(jnp.float32), axis=0, keepdims=True)
        if k == 3:
            taps_out[taps, :, cols] = jnp.zeros((1, LANES), jnp.float32)

    def step(c, _, k):
        column(k, c)
        return 0

    for k in range(4):
        lax.fori_loop(0, gain.shape[1] // LANES, functools.partial(step, k=k), 0)


def out_kernel(hidden, masked, out_ref, turned):
    turned[...] = hidden[...].T
    width = out_ref.shape[1]
    for c in range(0, width, 256):
        out_ref[:, c : c + 256] = (0.5 * dot(turned[...], masked[:, c : c + 256], 1, 0)).astype(
            jnp.bfloat16
        )


def join_kernel(width, *refs):
    pieces, out_ref, held, sems = refs[0:4], refs[4], refs[5], refs[6]
    me = lax.axis_index("fsdp")
    coming = [
        pltpu.make_async_copy(piece, held.at[k], sems.at[0, k]) for k, piece in enumerate(pieces)
    ]
    leaving = [
        pltpu.make_async_copy(held.at[k], out_ref.at[:, columns_of(me ^ k, width)], sems.at[1, k])
        for k in range(4)
    ]
    for copy in coming:
        copy.start()
    for first, second in zip(coming, leaving):
        first.wait()
        second.start()
    for copy in leaving:
        copy.wait()


def on_device(
    frames,
    occupied_slot_counts,
    block_frame_rows,
    order,
    cotangent,
    sub_weight,
    depth_kernel,
    norm_gain,
    w_in,
    w_out,
):
    n = lax.axis_size("dp")
    home = frames.shape[2]
    cap = (home + n - 1) // n
    split = home % n == 0
    blocks, steps, width = cotangent.shape[2:]
    rows = blocks * steps
    deep, hidden_width = w_in.shape
    wide = hidden_width // 4
    bf16, f32 = jnp.bfloat16, jnp.float32
    dma = pltpu.SemaphoreType.DMA

    info = jnp.concatenate([occupied_slot_counts[0], block_frame_rows[0, 0]])
    infos = lax.all_to_all(
        jnp.broadcast_to(info[None], (n, home + 1)), "dp", split_axis=0, concat_axis=0, tiled=True
    )

    w_far, w_out, sub_weight, depth_kernel = far(w_in, w_out, sub_weight, depth_kernel)
    sub1, sub2 = across(sub_weight, 1), across(sub_weight, 2)
    w2, w3 = pl.pallas_call(
        functools.partial(cut_kernel, wide),
        out_shape=(pltpu.HBM((deep // 2, wide), bf16), pltpu.HBM((deep, wide), bf16)),
        in_specs=[ANY],
        out_specs=(ANY,) * 2,
        scratch_shapes=[
            pltpu.VMEM((deep // 2, wide), bf16),
            pltpu.VMEM((deep, wide), bf16),
            dma((4,)),
        ],
        compiler_params=params(),
        cost_estimate=cost(1),
    )(w_far)
    w2 = across(w2, 2)

    block_shape = frames.shape[3:]
    held = frames[0, 0].reshape((cap, n) + block_shape) if split else frames[0, 0]
    packed = pl.pallas_call(
        functools.partial(pack_kernel, n, split),
        out_shape=sds((n, cap) + block_shape, bf16),
        in_specs=[SMEM, SMEM, ANY],
        out_specs=ANY,
        scratch_shapes=[
            pltpu.VMEM((n if split else home, cap) + block_shape, bf16),
            dma((2 * (n if split else home),)),
        ],
        compiler_params=params(),
        cost_estimate=cost(2),
    )(order, infos, held)
    gain = norm_gain.reshape(1, width)
    packed, sub1, sub2, gain, cot, w2 = lax.optimization_barrier(
        (packed, sub1, sub2, gain, cotangent[0, 0], w2)
    )
    w3 = across(w3, 3)
    got = lax.all_to_all(packed, "dp", split_axis=0, concat_axis=0, tiled=True)
    sub_rows = sub_weight.shape[0]
    cot0, pair = pl.pallas_call(
        functools.partial(prepare_kernel, blocks, steps, wide),
        out_shape=(
            pltpu.HBM((rows, width), bf16),
            pltpu.HBM((rows + deep // 2, width), bf16),
        ),
        in_specs=[VMEM, ANY],
        out_specs=(ANY,) * 2,
        scratch_shapes=[
            pltpu.VMEM((rows, width), bf16),
            pltpu.VMEM((rows + deep // 2, width), bf16),
            pltpu.VMEM((rows * width // LANES, LANES), f32),
            dma((5,)),
        ],
        compiler_params=params(),
        cost_estimate=cost(2),
    )(cot, w_far)
    sub3 = across(sub2, 1)
    cot2, pair = across(cot0, 2), across(pair, 1)
    weight, scales = pl.pallas_call(
        order_kernel,
        out_shape=(
            pltpu.VMEM((4 * sub_rows, width), bf16),
            pltpu.VMEM((2 * steps, width), f32),
        ),
        in_specs=[ANY] * 4 + [VMEM] * 2,
        out_specs=(VMEM,) * 2,
        scratch_shapes=[dma((4,))],
        compiler_params=params(),
        cost_estimate=cost(1),
    )(sub_weight, *far(sub1, sub2, sub3), depth_kernel, gain)
    w2b = across_dp(w2, 1)
    got, weight, w2b = lax.optimization_barrier((got, weight, w2b))
    patches0 = pl.pallas_call(
        functools.partial(unpack_kernel, n, cap, blocks, steps),
        out_shape=sds((rows + blocks, block_shape[0] // steps * LANES), bf16),
        in_specs=[SMEM, SMEM, ANY],
        out_specs=VMEM,
        scratch_shapes=[
            pltpu.VMEM((blocks,) + block_shape, bf16),
            pltpu.VMEM((blocks * block_shape[0], LANES), f32),
            dma((blocks,)),
        ],
        compiler_params=params(),
        cost_estimate=cost(2),
    )(order, infos, got.reshape((n * cap,) + block_shape))
    patches = [patches0, across(patches0, 1), across(patches0, 2)]

    kept = (
        pltpu.VMEM((rows, width), bf16),
        pltpu.VMEM((rows, width), bf16),
        pltpu.VMEM((rows, width), bf16),
        pltpu.VMEM((rows, LANES), f32),
    )
    forward = pl.pallas_call(
        functools.partial(forward_kernel, steps, blocks),
        out_shape=kept,
        in_specs=[VMEM] * 3,
        out_specs=(VMEM,) * 4,
        scratch_shapes=[pltpu.VMEM((rows, width), f32), pltpu.VMEM((rows, LANES), f32)],
        compiler_params=params(),
        cost_estimate=cost(4),
    )
    groups = [list(forward(*near(patches[0], weight, scales)))]
    groups[0][0], patches[1], w3 = lax.optimization_barrier((groups[0][0], patches[1], w3))
    groups.append(list(forward(*near(patches[1], weight, scales))))
    groups[1][0], cot_relay, patches[2] = lax.optimization_barrier(
        (groups[1][0], cot2, patches[2])
    )
    cot3 = across(cot_relay, 1)
    patches.append(across(patches[2], 1))
    for k in (2, 3):
        groups.append(forward(*near(patches[k], weight, scales)))
    feats, normeds, slopes, rstds = [near(*arrays) for arrays in zip(*groups)]
    g0, g1, g2, g3, scaled, hidden, masked, w_slice, means = pl.pallas_call(
        functools.partial(middle_kernel, steps, blocks),
        out_shape=(
            *[pltpu.HBM((deep, wide), bf16)] * 4,
            pltpu.VMEM((4 * rows, wide), bf16),
            pltpu.VMEM((4 * rows, wide), bf16),
            pltpu.VMEM((4 * rows, width), bf16),
            pltpu.VMEM((width, wide), bf16),
            pltpu.VMEM((2, 4 * rows, LANES), bf16),
        ),
        in_specs=[VMEM] * 13 + [ANY] * 9,
        out_specs=(ANY,) * 4 + (VMEM,) * 5,
        scratch_shapes=[
            pltpu.VMEM((4 * rows, wide), bf16),
            pltpu.VMEM((wide, width), bf16),
            pltpu.VMEM((4, deep, wide), bf16),
            dma((16,)),
        ],
        compiler_params=params(24),
        cost_estimate=cost(12),
    )(
        *patches, *normeds, *rstds, gain,
        *far(cot0, pair, cot2, cot3), w_far, *far(w2, w3, w2b), w_out,
    )
    g3, g2, g1 = across(g3, 3), across(g2, 2), across(g1, 1)

    taps = pl.pallas_call(
        functools.partial(backward_kernel, steps, blocks),
        out_shape=sds((2 * steps, 1, width), f32),
        in_specs=[VMEM] * 17,
        out_specs=VMEM,
        scratch_shapes=[
            pltpu.VMEM((4 * rows, width), bf16),
            pltpu.VMEM((2 * steps - 1, blocks, width), bf16),
        ],
        compiler_params=params(),
        cost_estimate=cost(13),
    )(gain, *near(scaled, w_slice, masked, means), *normeds, *slopes, *feats)
    taps, g2, hidden = lax.optimization_barrier((taps, g2, hidden))

    every = ("dp", "fsdp")
    devices = n * lax.axis_size("fsdp")
    shares = lax.all_to_all(
        taps.reshape(devices, 1, -1), every, split_axis=0, concat_axis=0, tiled=True
    )
    share = jnp.sum(shares, axis=0, keepdims=True) / rows
    grad_out = pl.pallas_call(
        out_kernel,
        out_shape=sds((wide, width), bf16),
        in_specs=[VMEM] * 2,
        out_specs=VMEM,
        scratch_shapes=[pltpu.VMEM((wide, 4 * rows), bf16)],
        compiler_params=params(),
        cost_estimate=cost(4),
    )(*near(hidden, masked))
    share, grad_out = lax.optimization_barrier((share, grad_out))
    whole = lax.all_to_all(
        jnp.broadcast_to(share, shares.shape), every, split_axis=0, concat_axis=0, tiled=True
    )
    kernel_grad = whole.reshape(2 * steps, width)[: depth_kernel.shape[0]]

    grad_in = pl.pallas_call(
        functools.partial(join_kernel, wide),
        out_shape=sds((deep, hidden_width), bf16),
        in_specs=[ANY] * 4,
        out_specs=ANY,
        scratch_shapes=[pltpu.VMEM((4, deep, wide), bf16), dma((2, 4))],
        compiler_params=params(),
        cost_estimate=cost(2),
    )(*far(g0, g1, g2, g3))
    return (grad_in[None], grad_out[None], kernel_grad)


def solution(mesh):
    placed = (
        P("dp", "fsdp", None, None, None),
        P("fsdp", "dp"),
        P("dp", "fsdp", None),
        P("fsdp", None),
        P("dp", "fsdp", None, None, None),
        P("fsdp", None),
        P(),
        P(),
        P("fsdp", None),
        P("fsdp", None),
    )
    return jax.shard_map(
        on_device,
        mesh=mesh,
        in_specs=placed,
        out_specs=(P("dp", "fsdp", None), P("dp", "fsdp", None), P()),
        check_vma=False,
    )
```

```python
import functools

import jax
import jax.numpy as jnp
from jax import lax
from jax.experimental import pallas as pl
from jax.experimental.pallas import tpu as pltpu
from jax.sharding import PartitionSpec as P

LANES = 128
HALF = 8
TILE = 16
EPSILON = 1e-05

VMEM = pl.BlockSpec(memory_space=pltpu.VMEM)
SMEM = pl.BlockSpec(memory_space=pltpu.SMEM)
ANY = pl.BlockSpec(memory_space=pl.ANY)


def params(mebibytes=16):
    return pltpu.CompilerParams(vmem_limit_bytes=mebibytes * 1024 * 1024)


def cost(microseconds):
    return pl.CostEstimate(
        flops=0, transcendentals=0, bytes_accessed=int(microseconds * 3.6e6)
    )


def near(*arrays):
    return [pltpu.with_memory_space_constraint(array, pltpu.VMEM) for array in arrays]


def far(*arrays):
    return [pltpu.with_memory_space_constraint(array, pltpu.HBM) for array in arrays]


def sds(shape, dtype):
    return jax.ShapeDtypeStruct(shape, dtype)


def sigmoid(values):
    return 0.5 * jnp.tanh(0.5 * values) + 0.5


def dot(left, right, left_dim, right_dim):
    return lax.dot_general(
        left, right, (((left_dim,), (right_dim,)), ((), ())), preferred_element_type=jnp.float32
    )


def across(value, k):
    n = lax.axis_size("fsdp")
    return lax.ppermute(value, "fsdp", [(i, i ^ k) for i in range(n)])


def across_dp(value, k):
    n = lax.axis_size("dp")
    return lax.ppermute(value, "dp", [(i, i ^ k) for i in range(n)])


def columns_of(index, width):
    return pl.ds(pl.multiple_of(index * width, LANES), width)


def prepare_kernel(
    blocks, steps, width, cot_ref, w_ref, cot_out, pair_out, cot, pair, scratch, sems
):
    rows = blocks * steps
    half = w_ref.shape[0] // 2
    cols = columns_of(lax.axis_index("fsdp") ^ 1, width)
    copies = [
        pltpu.make_async_copy(
            w_ref.at[i * half : (i + 1) * half, cols],
            pair.at[rows:, i * width : (i + 1) * width],
            sems.at[i],
        )
        for i in range(2)
    ]
    for copy in copies:
        copy.start()
    for c in range(cot_ref.shape[-1] // LANES):
        cols = slice(c * LANES, (c + 1) * LANES)
        scratch[c * rows : (c + 1) * rows, :] = (
            cot_ref[:, :, cols].reshape(rows, LANES).astype(jnp.float32)
        )
        for t in range(steps):
            at = slice(t * blocks, (t + 1) * blocks)
            turned = scratch[pl.ds(c * rows + t, blocks, stride=steps), :].astype(jnp.bfloat16)
            cot[at, cols] = turned
            pair[at, cols] = turned
    for copy in copies:
        copy.wait()
    leaving = [
        pltpu.make_async_copy(cot, cot_out, sems.at[3]),
        pltpu.make_async_copy(pair, pair_out, sems.at[4]),
    ]
    for copy in leaving:
        copy.start()
    for copy in leaving:
        copy.wait()


def pack_kernel(n, split, order_ref, info_ref, frames_ref, out_ref, held, sems):
    me = lax.axis_index("dp")
    classes = held.shape[0]
    coming = []
    for c in range(classes):
        source = frames_ref.at[:, c] if split else frames_ref.at[pl.ds(c, 1)]
        coming.append(pltpu.make_async_copy(source, held.at[c], sems.at[c]))
        coming[c].start()
    start = jnp.int32(0)
    for i in range(n - 1):
        start = start + jnp.where(i < me, info_ref[i, 0], 0)
    leaving = []
    for c in range(classes):
        target = order_ref[0, lax.rem(start + c, n)]
        leaving.append(
            pltpu.make_async_copy(held.at[c], out_ref.at[target], sems.at[classes + c])
        )
        coming[c].wait()
        leaving[c].start()
    for copy in leaving:
        copy.wait()


def unpack_kernel(
    n, cap, blocks, steps, order_ref, info_ref, got_ref, out_ref, landed, scratch, sems
):
    me = lax.axis_index("dp")
    residue = jnp.int32(0)
    for r in range(n):
        residue = residue + jnp.where(order_ref[0, r] == me, r, 0)
    starts, so_far = [], jnp.int32(0)
    for i in range(n):
        starts.append(so_far)
        so_far = so_far + info_ref[i, 0]
    length = got_ref.shape[1]
    copies, rows = [], []
    for m in range(blocks):
        g = residue + m * n
        source, start = jnp.int32(0), jnp.int32(0)
        for i in range(1, n):
            later = starts[i] <= g
            source = jnp.where(later, i, source)
            start = jnp.where(later, starts[i], start)
        h = g - start
        copy = pltpu.make_async_copy(
            got_ref.at[source * cap + lax.div(h, n)], landed.at[m], sems.at[m]
        )
        copy.start()
        copies.append(copy)
        rows.append(info_ref[source, 1 + h])
    height = lax.broadcasted_iota(jnp.int32, (blocks, out_ref.shape[1]), 0)
    counts = jnp.zeros((blocks, out_ref.shape[1]), jnp.int32)
    for m in range(blocks):
        counts = jnp.where(height == m, rows[m], counts)
    out_ref[steps * blocks :, :] = counts.astype(jnp.float32).astype(jnp.bfloat16)
    for m in range(blocks):
        copies[m].wait()
        scratch[m * length : (m + 1) * length, :] = landed[m].astype(jnp.float32)
    group = length // steps
    for t in range(steps):
        for j in range(group):
            out_ref[t * blocks : (t + 1) * blocks, j * LANES : (j + 1) * LANES] = scratch[
                pl.ds(group * t + j, blocks, stride=length), :
            ].astype(jnp.bfloat16)


def cut_kernel(width, w_ref, p2, p3, half2, full3, sems):
    me = lax.axis_index("fsdp")
    half = p2.shape[0]
    part = pl.ds(pl.multiple_of(lax.rem(lax.axis_index("dp"), 2) * half, TILE), half)
    coming = [
        pltpu.make_async_copy(w_ref.at[part, columns_of(me ^ 2, width)], half2, sems.at[0]),
        pltpu.make_async_copy(w_ref.at[:, columns_of(me ^ 3, width)], full3, sems.at[1]),
    ]
    leaving = [
        pltpu.make_async_copy(half2, p2, sems.at[2]),
        pltpu.make_async_copy(full3, p3, sems.at[3]),
    ]
    for copy in coming:
        copy.start()
    for first, second in zip(coming, leaving):
        first.wait()
        second.start()
    for copy in leaving:
        copy.wait()


def tree(terms, low, high):
    if high - low == 1:
        left, right = terms[low]
        return left * right
    middle = (low + high) // 2
    return tree(terms, low, middle) + tree(terms, middle, high)


def order_kernel(sub0, sub1, sub2, sub3, depth, gain, weight, scales, sems):
    me = lax.axis_index("fsdp")
    deep = sub0.shape[0]
    copies = [
        pltpu.make_async_copy(
            piece, weight.at[pl.ds(pl.multiple_of((me ^ k) * deep, TILE), deep), :], sems.at[k]
        )
        for k, piece in enumerate((sub0, sub1, sub2, sub3))
    ]
    for copy in copies:
        copy.start()
    scales[: depth.shape[0], :] = depth[...]
    scales[depth.shape[0] :, :] = gain[...]
    for copy in copies:
        copy.wait()


def forward_kernel(
    steps, blocks, patches, weight, scales, feat_ref, normed_ref, slope_ref, rstd_ref, work, mask
):
    rows = steps * blocks
    width, taps = scales.shape[1], scales.shape[0] - 1
    span = (taps - 1) // 2
    work[...] = dot(patches[:rows, :], weight[...], 1, 0)
    counts = patches[rows:, :LANES].astype(jnp.float32)
    spots = [slice(t * blocks, (t + 1) * blocks) for t in range(steps)]
    for t in range(steps):
        mask[spots[t], :] = jnp.where(counts > t, 1.0, 0.0)

    def column(c, _):
        cols = pl.ds(pl.multiple_of(c * LANES, LANES), LANES)
        weights = [
            jnp.broadcast_to(scales[k : k + 1, cols], (blocks, LANES)).astype(jnp.bfloat16)
            for k in range(taps)
        ]
        values = []
        for t in range(steps):
            values.append((work[spots[t], cols] * mask[spots[t], :]).astype(jnp.bfloat16))
            feat_ref[spots[t], cols] = values[t]
        for t in range(steps):
            terms = [
                (values[s], weights[s - t + span])
                for s in range(steps)
                if 0 <= s - t + span < taps
            ]
            conv = tree(terms, 0, len(terms)).astype(jnp.float32)
            keep = mask[spots[t], :]
            sigma = sigmoid(conv)
            swish = conv * sigma
            slope_ref[spots[t], cols] = (keep * (sigma + swish * (1.0 - sigma))).astype(
                jnp.bfloat16
            )
            work[spots[t], cols] = values[t].astype(jnp.float32) + keep * swish
        return 0

    lax.fori_loop(0, width // LANES, column, 0)

    def norm(i, _):
        at = pl.ds(pl.multiple_of(i * 32, 32), 32)
        values = work[at, :]
        centred = values - jnp.mean(values, axis=-1, keepdims=True)
        rstd = lax.rsqrt(jnp.mean(centred * centred, axis=-1, keepdims=True) + EPSILON)
        normed_ref[at, :] = (centred * rstd * scales[taps:, :]).astype(jnp.bfloat16)
        rstd_ref[at, :] = jnp.broadcast_to(rstd, (32, LANES))
        return 0

    lax.fori_loop(0, rows // 32, norm, 0)


def middle_kernel(steps, blocks, *refs):
    patches, normed, rstds, gain = refs[0:4], refs[4:8], refs[8:12], refs[12]
    cot0, pair, cot2, cot3, w_own, w2, w3, w2b, w_out_in = refs[13:22]
    grads, scaled, hidden, masked, w_in, means = refs[22:26], *refs[26:31]
    pre_grad, w_out, held, sems = refs[31:35]
    me = lax.axis_index("fsdp")
    parity = lax.rem(lax.axis_index("dp"), 2)
    rows = steps * blocks
    half, wide = w2.shape
    high = 2 * half
    used = iter(range(sems.shape[0]))

    def move(source, place):
        copy = pltpu.make_async_copy(source, place, sems.at[next(used)])
        copy.start()
        return copy

    def rows_of(index, part=0, size=high):
        return pl.ds(pl.multiple_of(index * high + part * half, TILE), size)

    coming = [
        move(w_own.at[:, columns_of(me, wide)], w_in.at[rows_of(me), :]),
        move(pair.at[rows:, :wide], w_in.at[rows_of(me ^ 1, 0, half), :]),
        move(pair.at[rows:, wide:], w_in.at[rows_of(me ^ 1, 1, half), :]),
        move(w2, w_in.at[rows_of(me ^ 2, parity, half), :]),
        move(w3, w_in.at[rows_of(me ^ 3), :]),
        move(w2b, w_in.at[rows_of(me ^ 2, 1 - parity, half), :]),
    ]
    for copy in coming:
        copy.wait()
    later = [
        move(w_out_in, w_out),
        move(cot0, masked.at[:rows, :]),
        move(pair.at[:rows, :], masked.at[rows : 2 * rows, :]),
        move(cot2, masked.at[2 * rows : 3 * rows, :]),
        move(cot3, masked.at[3 * rows :, :]),
    ]
    fine = jnp.broadcast_to(gain[...], (TILE, gain.shape[1]))
    coarse = fine.astype(jnp.bfloat16)
    small = (fine - coarse.astype(jnp.float32)).astype(jnp.bfloat16)
    pulled = (dot(coarse, w_in[...], 1, 0) + dot(small, w_in[...], 1, 0))[:1, :]
    share = 1.0 / gain.shape[1]
    for k in range(4):
        at = slice(k * rows, (k + 1) * rows)
        counts = patches[k][rows:, :LANES].astype(jnp.float32)[:, :1]
        keep = jnp.concatenate([counts > t for t in range(steps)], axis=0)
        pre = dot(normed[k][...], w_in[...], 1, 0)
        for copy in later[:2] if k == 0 else later[k + 1 : k + 2]:
            copy.wait()
        kept = jnp.where(keep, masked[at, :], jnp.zeros((), jnp.bfloat16))
        masked[at, :] = kept
        back = dot(kept, w_out[...], 1, 1)
        sigma = sigmoid(pre)
        swish = pre * sigma
        hidden[at, :] = swish.astype(jnp.bfloat16)
        grown = 0.5 * back * (sigma + swish * (1.0 - sigma))
        pre_grad[at, :] = grown.astype(jnp.bfloat16)
        grown = grown * rstds[k][:, :1]
        scaled[at, :] = grown.astype(jnp.bfloat16)
        for i, other in enumerate((pulled, pre)):
            mean = jnp.sum(grown * other, axis=-1, keepdims=True) * share
            means[i, at, :] = jnp.broadcast_to(mean, (rows, LANES)).astype(jnp.bfloat16)
    leaving = []
    for k in (2, 3, 1, 0):
        cols = columns_of(me ^ k, high)
        left = jnp.concatenate([normed[j][:, cols] for j in range(4)], axis=0)
        held[k] = dot(left, pre_grad[...], 0, 0).astype(jnp.bfloat16)
        leaving.append(move(held.at[k], grads[k]))
    for copy in leaving:
        copy.wait()


def backward_kernel(steps, blocks, *refs):
    gain, scaled, w_in, masked, means = refs[0:5]
    normed, slope, feat = refs[5:9], refs[9:13], refs[13:17]
    taps_out, grad, totals = refs[17:20]
    rows = steps * blocks
    for k in range(4):
        at = slice(k * rows, (k + 1) * rows)
        pulled = dot(scaled[at, :], w_in[...], 1, 1) * gain[...]
        if k == 0:
            pulled = pulled + masked[at, :].astype(jnp.float32)
        grad[at, :] = pulled.astype(jnp.bfloat16)
    taps = 2 * steps - 1

    def column(k, c):
        cols = pl.ds(pl.multiple_of(c * LANES, LANES), LANES)
        inverse = jnp.broadcast_to(1.0 / gain[:, cols], (blocks, LANES)).astype(jnp.bfloat16)
        here = [slice(t * blocks, (t + 1) * blocks) for t in range(steps)]
        spots = [slice(k * rows + t * blocks, k * rows + (t + 1) * blocks) for t in range(steps)]
        left = [
            slope[k][at, cols]
            * (
                grad[spot, cols]
                - means[0, spot, :]
                - normed[k][at, cols] * inverse * means[1, spot, :]
            )
            for spot, at in zip(spots, here)
        ]
        right = [feat[k][at, cols] for at in here]
        for tap in range(taps):
            shift = tap - (steps - 1)
            terms = [(left[t], right[t + shift]) for t in range(steps) if 0 <= t + shift < steps]
            part = tree(terms, 0, len(terms))
            if k > 0:
                part = part + totals[tap, :, cols]
            if k < 3:
                totals[tap, :, cols] = part
            else:
                taps_out[tap, :, cols] = jnp.sum(part.astype(jnp.float32), axis=0, keepdims=True)
        if k == 3:
            taps_out[taps, :, cols] = jnp.zeros((1, LANES), jnp.float32)

    def step(c, _, k):
        column(k, c)
        return 0

    for k in range(4):
        lax.fori_loop(0, gain.shape[1] // LANES, functools.partial(step, k=k), 0)


def out_kernel(hidden, masked, out_ref, turned):
    turned[...] = hidden[...].T
    width = out_ref.shape[1]
    for c in range(0, width, 256):
        out_ref[:, c : c + 256] = (0.5 * dot(turned[...], masked[:, c : c + 256], 1, 0)).astype(
            jnp.bfloat16
        )


def join_kernel(width, *refs):
    pieces, out_ref, held, sems = refs[0:4], refs[4], refs[5], refs[6]
    me = lax.axis_index("fsdp")
    coming = [
        pltpu.make_async_copy(piece, held.at[k], sems.at[0, k]) for k, piece in enumerate(pieces)
    ]
    leaving = [
        pltpu.make_async_copy(held.at[k], out_ref.at[:, columns_of(me ^ k, width)], sems.at[1, k])
        for k in range(4)
    ]
    for copy in coming:
        copy.start()
    for first, second in zip(coming, leaving):
        first.wait()
        second.start()
    for copy in leaving:
        copy.wait()


def on_device(
    frames,
    occupied_slot_counts,
    block_frame_rows,
    order,
    cotangent,
    sub_weight,
    depth_kernel,
    norm_gain,
    w_in,
    w_out,
):
    n = lax.axis_size("dp")
    home = frames.shape[2]
    cap = (home + n - 1) // n
    split = home % n == 0
    blocks, steps, width = cotangent.shape[2:]
    rows = blocks * steps
    deep, hidden_width = w_in.shape
    wide = hidden_width // 4
    bf16, f32 = jnp.bfloat16, jnp.float32
    dma = pltpu.SemaphoreType.DMA

    info = jnp.concatenate([occupied_slot_counts[0], block_frame_rows[0, 0]])
    infos = lax.all_to_all(
        jnp.broadcast_to(info[None], (n, home + 1)), "dp", split_axis=0, concat_axis=0, tiled=True
    )

    w_far, w_out, sub_weight, depth_kernel = far(w_in, w_out, sub_weight, depth_kernel)
    sub1, sub2 = across(sub_weight, 1), across(sub_weight, 2)
    w2, w3 = pl.pallas_call(
        functools.partial(cut_kernel, wide),
        out_shape=(pltpu.HBM((deep // 2, wide), bf16), pltpu.HBM((deep, wide), bf16)),
        in_specs=[ANY],
        out_specs=(ANY,) * 2,
        scratch_shapes=[
            pltpu.VMEM((deep // 2, wide), bf16),
            pltpu.VMEM((deep, wide), bf16),
            dma((4,)),
        ],
        compiler_params=params(),
        cost_estimate=cost(1),
    )(w_far)
    w2 = across(w2, 2)

    block_shape = frames.shape[3:]
    held = frames[0, 0].reshape((cap, n) + block_shape) if split else frames[0, 0]
    packed = pl.pallas_call(
        functools.partial(pack_kernel, n, split),
        out_shape=sds((n, cap) + block_shape, bf16),
        in_specs=[SMEM, SMEM, ANY],
        out_specs=ANY,
        scratch_shapes=[
            pltpu.VMEM((n if split else home, cap) + block_shape, bf16),
            dma((2 * (n if split else home),)),
        ],
        compiler_params=params(),
        cost_estimate=cost(2),
    )(order, infos, held)
    gain = norm_gain.reshape(1, width)
    packed, sub1, sub2, gain, cot, w2 = lax.optimization_barrier(
        (packed, sub1, sub2, gain, cotangent[0, 0], w2)
    )
    w3 = across(w3, 3)
    got = lax.all_to_all(packed, "dp", split_axis=0, concat_axis=0, tiled=True)
    sub_rows = sub_weight.shape[0]
    cot0, pair = pl.pallas_call(
        functools.partial(prepare_kernel, blocks, steps, wide),
        out_shape=(
            pltpu.HBM((rows, width), bf16),
            pltpu.HBM((rows + deep // 2, width), bf16),
        ),
        in_specs=[VMEM, ANY],
        out_specs=(ANY,) * 2,
        scratch_shapes=[
            pltpu.VMEM((rows, width), bf16),
            pltpu.VMEM((rows + deep // 2, width), bf16),
            pltpu.VMEM((rows * width // LANES, LANES), f32),
            dma((5,)),
        ],
        compiler_params=params(),
        cost_estimate=cost(2),
    )(cot, w_far)
    sub3 = across(sub2, 1)
    cot2, pair = across(cot0, 2), across(pair, 1)
    weight, scales = pl.pallas_call(
        order_kernel,
        out_shape=(
            pltpu.VMEM((4 * sub_rows, width), bf16),
            pltpu.VMEM((2 * steps, width), f32),
        ),
        in_specs=[ANY] * 4 + [VMEM] * 2,
        out_specs=(VMEM,) * 2,
        scratch_shapes=[dma((4,))],
        compiler_params=params(),
        cost_estimate=cost(1),
    )(sub_weight, *far(sub1, sub2, sub3), depth_kernel, gain)
    w2b = across_dp(w2, 1)
    got, weight, w2b = lax.optimization_barrier((got, weight, w2b))
    patches0 = pl.pallas_call(
        functools.partial(unpack_kernel, n, cap, blocks, steps),
        out_shape=sds((rows + blocks, block_shape[0] // steps * LANES), bf16),
        in_specs=[SMEM, SMEM, ANY],
        out_specs=VMEM,
        scratch_shapes=[
            pltpu.VMEM((blocks,) + block_shape, bf16),
            pltpu.VMEM((blocks * block_shape[0], LANES), f32),
            dma((blocks,)),
        ],
        compiler_params=params(),
        cost_estimate=cost(2),
    )(order, infos, got.reshape((n * cap,) + block_shape))
    patches = [patches0, across(patches0, 1), across(patches0, 2)]

    kept = (
        pltpu.VMEM((rows, width), bf16),
        pltpu.VMEM((rows, width), bf16),
        pltpu.VMEM((rows, width), bf16),
        pltpu.VMEM((rows, LANES), f32),
    )
    forward = pl.pallas_call(
        functools.partial(forward_kernel, steps, blocks),
        out_shape=kept,
        in_specs=[VMEM] * 3,
        out_specs=(VMEM,) * 4,
        scratch_shapes=[pltpu.VMEM((rows, width), f32), pltpu.VMEM((rows, LANES), f32)],
        compiler_params=params(),
        cost_estimate=cost(4),
    )
    groups = [list(forward(*near(patches[0], weight, scales)))]
    groups[0][0], patches[1] = lax.optimization_barrier((groups[0][0], patches[1]))
    groups.append(list(forward(*near(patches[1], weight, scales))))
    groups[1][0], cot_relay, patches[2], w3 = lax.optimization_barrier(
        (groups[1][0], cot2, patches[2], w3)
    )
    cot3 = across(cot_relay, 1)
    patches.append(across(patches[2], 1))
    for k in (2, 3):
        groups.append(forward(*near(patches[k], weight, scales)))
    feats, normeds, slopes, rstds = [near(*arrays) for arrays in zip(*groups)]
    g0, g1, g2, g3, scaled, hidden, masked, w_slice, means = pl.pallas_call(
        functools.partial(middle_kernel, steps, blocks),
        out_shape=(
            *[pltpu.HBM((deep, wide), bf16)] * 4,
            pltpu.VMEM((4 * rows, wide), bf16),
            pltpu.VMEM((4 * rows, wide), bf16),
            pltpu.VMEM((4 * rows, width), bf16),
            pltpu.VMEM((width, wide), bf16),
            pltpu.VMEM((2, 4 * rows, LANES), bf16),
        ),
        in_specs=[VMEM] * 13 + [ANY] * 9,
        out_specs=(ANY,) * 4 + (VMEM,) * 5,
        scratch_shapes=[
            pltpu.VMEM((4 * rows, wide), bf16),
            pltpu.VMEM((wide, width), bf16),
            pltpu.VMEM((4, deep, wide), bf16),
            dma((16,)),
        ],
        compiler_params=params(24),
        cost_estimate=cost(12),
    )(
        *patches, *normeds, *rstds, gain,
        *far(cot0, pair, cot2, cot3), w_far, *far(w2, w3, w2b), w_out,
    )
    g3, g2, g1 = across(g3, 3), across(g2, 2), across(g1, 1)

    taps = pl.pallas_call(
        functools.partial(backward_kernel, steps, blocks),
        out_shape=sds((2 * steps, 1, width), f32),
        in_specs=[VMEM] * 17,
        out_specs=VMEM,
        scratch_shapes=[
            pltpu.VMEM((4 * rows, width), bf16),
            pltpu.VMEM((2 * steps - 1, blocks, width), bf16),
        ],
        compiler_params=params(),
        cost_estimate=cost(13),
    )(gain, *near(scaled, w_slice, masked, means), *normeds, *slopes, *feats)
    taps, g2, hidden = lax.optimization_barrier((taps, g2, hidden))

    every = ("dp", "fsdp")
    devices = n * lax.axis_size("fsdp")
    shares = lax.all_to_all(
        taps.reshape(devices, 1, -1), every, split_axis=0, concat_axis=0, tiled=True
    )
    share = jnp.sum(shares, axis=0, keepdims=True) / rows
    grad_out = pl.pallas_call(
        out_kernel,
        out_shape=sds((wide, width), bf16),
        in_specs=[VMEM] * 2,
        out_specs=VMEM,
        scratch_shapes=[pltpu.VMEM((wide, 4 * rows), bf16)],
        compiler_params=params(),
        cost_estimate=cost(4),
    )(*near(hidden, masked))
    share, grad_out = lax.optimization_barrier((share, grad_out))
    whole = lax.all_to_all(
        jnp.broadcast_to(share, shares.shape), every, split_axis=0, concat_axis=0, tiled=True
    )
    kernel_grad = whole.reshape(2 * steps, width)[: depth_kernel.shape[0]]

    grad_in = pl.pallas_call(
        functools.partial(join_kernel, wide),
        out_shape=sds((deep, hidden_width), bf16),
        in_specs=[ANY] * 4,
        out_specs=ANY,
        scratch_shapes=[pltpu.VMEM((4, deep, wide), bf16), dma((2, 4))],
        compiler_params=params(),
        cost_estimate=cost(2),
    )(*far(g0, g1, g2, g3))
    return (grad_in[None], grad_out[None], kernel_grad)


def solution(mesh):
    placed = (
        P("dp", "fsdp", None, None, None),
        P("fsdp", "dp"),
        P("dp", "fsdp", None),
        P("fsdp", None),
        P("dp", "fsdp", None, None, None),
        P("fsdp", None),
        P(),
        P(),
        P("fsdp", None),
        P("fsdp", None),
    )
    return jax.shard_map(
        on_device,
        mesh=mesh,
        in_specs=placed,
        out_specs=(P("dp", "fsdp", None), P("dp", "fsdp", None), P()),
        check_vma=False,
    )
```
